32 devices in a mesh: batch: 8 (over y, x, core), expert: 4 (over z).
Axes of the slice: x: 2, y: 2, z: 4, core: 2. Of those that a mesh axis runs over, the one named last changes fastest.
Arguments:
- dense_feats: float32 [32768, 13], P(('batch', 'expert')), may hold values from -6 to 6
- picks: int32 [32768, 26], P(('batch', 'expert')), may hold values from 0 to 16383, as said below
- labels: int32 [32768, 2], P(('batch', 'expert')), may hold values from 0 to 1
- label_mask: int32 [32768, 2], P(('batch', 'expert')), may hold values from 0 to 1
- requests: int32 [32, 8, 4, 512], P(('batch', 'expert')), may hold values from 0 to 4095
- table: float32 [131072, 16], P(('batch', 'expert')), may hold values from -6 to 6
- table_m: float32 [131072, 16], P(('batch', 'expert')), may hold values from -9.536743e-06 to 9.536743e-06
- table_v: float32 [131072, 16], P(('batch', 'expert')), may hold values from 3.7252902e-14 to 1.4901161e-13
- first_w: float32 [4, 512, 256], P('expert', 'batch'), may hold values from -1 to 1
- first_m: float32 [4, 512, 256], P('expert', 'batch'), may hold values from -0.00024414062 to 0.00024414062
- first_v: float32 [4, 512, 256], P('expert', 'batch'), may hold values from 2.746582e-11 to 1.0986328e-10
- second_w: float32 [4, 256, 128], P('expert', 'batch'), may hold values from -1.25 to 1.25
- second_m: float32 [4, 256, 128], P('expert', 'batch'), may hold values from -0.00024414062 to 0.00024414062
- second_v: float32 [4, 256, 128], P('expert', 'batch'), may hold values from 2.746582e-11 to 4.394531e-10
- small: float32 [23626], replicated
- small_m: float32 [23626], replicated, may hold values from -0.0024414062 to 0.0024414062
- small_v: float32 [23626], replicated, may hold values from 2.746582e-09 to 4.3945313e-08
Outputs:
- loss: float32 [], replicated
- new_table: float32 [131072, 16], P(('batch', 'expert'))
- new_table_m: float32 [131072, 16], P(('batch', 'expert'))
- new_table_v: float32 [131072, 16], P(('batch', 'expert'))
- new_first: float32 [4, 512, 256], P('expert', 'batch')
- new_first_m: float32 [4, 512, 256], P('expert', 'batch')
- new_first_v: float32 [4, 512, 256], P('expert', 'batch')
- new_second: float32 [4, 256, 128], P('expert', 'batch')
- new_second_m: float32 [4, 256, 128], P('expert', 'batch')
- new_second_v: float32 [4, 256, 128], P('expert', 'batch')
- new_small: float32 [23626], replicated
- new_small_m: float32 [23626], replicated
- new_small_v: float32 [23626], replicated
The draws below stay inside these ranges and needn't reach their ends.
Inputs may be any that keep to these rules, and one draw needn't show every extreme that they name: `picks`: slot of the impression's own device's request buffer; an impression t with b = (t % 1024) // 64 asks only slots s with (s % 512) // 32 == b. `requests`: row within the owner's 4096 rows.
All inputs are finite; a program needn't handle non-finite values.
Results may differ from the reference program's by a relative error of at most 0.018.
Values may be sent and summed in bfloat16 or wider, within the bound.
A program may use at most 128 MiB of HBM per device.

```python
import math
import jax
import jax.numpy as jnp
from jax import lax

FIELDS = 26
EMB = 16
DENSE = 13
DOUT = 96
HID = 256
OUT = 128
TOWER = 64
TASKS = 2
STEP = 5
TOK = 1024
ROWS_DEV = 4096
GROUP_TOK = 64
INPUT = 512
EXPERTS = 4
CAP = 512
SUB_SLOTS = 32
TOKENS = 32768
ROWS = 131072
SMALL = 23626
N_BATCH = 8
N_EXPERT = 4
DEVICES = 32


def draw_picks(key, part):
    owner_key, inner_key = jax.random.split(jax.random.fold_in(key, 11))
    owners = jax.random.randint(owner_key, (TOKENS, FIELDS), 0, DEVICES)
    inner = jax.random.randint(inner_key, (TOKENS, FIELDS), 0, SUB_SLOTS)
    group = (jnp.arange(TOKENS, dtype=jnp.int32) % TOK // GROUP_TOK)[:, None]
    result = owners * CAP + group * SUB_SLOTS + inner
    result = result.at[0, 0].set(0)
    result = result.at[TOKENS - 1, FIELDS - 1].set(DEVICES * CAP - 1)
    return result.astype(jnp.int32)


def draw_label_mask(key, part):
    device = (jnp.arange(TOKENS, dtype=jnp.int32) // TOK)[:, None]
    levels = jax.random.randint(key, (TOKENS, TASKS), 0, 4 * (DEVICES - 1))
    return (levels < DEVICES - 1 + 2 * device).astype(jnp.int32)


def draw_small(key, part):
    tower_scale = jnp.concatenate([jnp.full((TASKS, OUT, TOWER), 2.0 * OUT ** (-0.5), jnp.float32), jnp.full((TASKS, 1, TOWER), 0.1, jnp.float32)], 1).reshape(-1)
    head_scale = jnp.concatenate([jnp.full((TASKS, TOWER), 2.0 * TOWER ** (-0.5), jnp.float32), jnp.full((TASKS, 1), 0.1, jnp.float32)], 1).reshape(-1)
    scales = jnp.concatenate([jnp.full((EXPERTS * HID,), 0.1, jnp.float32), jnp.full((EXPERTS * OUT,), 0.1, jnp.float32), jnp.full((DENSE * DOUT,), DENSE ** (-0.5), jnp.float32), jnp.full((DOUT,), 0.1, jnp.float32), jnp.full((INPUT * TASKS * EXPERTS,), 0.7 * INPUT ** (-0.5), jnp.float32), jnp.full((TASKS * EXPERTS,), 0.1, jnp.float32), tower_scale, head_scale])
    return jax.random.normal(key, (SMALL,), jnp.float32) * scales


def log_band(key, shape, base, low_end, high_end):
    exponent = jax.random.uniform(key, shape, jnp.float32, math.log(low_end), math.log(high_end))
    return base * jnp.exp(exponent)


def draw_second_v(key, part):
    key = jax.random.fold_in(key, 23)
    shape = (EXPERTS, HID, OUT)
    base = 9e-07 / (DEVICES * TOK)
    result = log_band(key, shape, base, 1.0, 16.0)
    return jnp.clip(result, base, 16.0 * base).astype(jnp.float32)


def draw_small_v(key, part):
    key = jax.random.fold_in(key, 29)
    shape = (SMALL,)
    base = 9e-05 / (DEVICES * TOK)
    result = log_band(key, shape, base, 1.0, 16.0)
    return jnp.clip(result, base, 16.0 * base).astype(jnp.float32)


def touch_ends(drawn, key, least, top_value):
    dims = drawn.shape
    place = [jax.random.randint(jax.random.fold_in(key, axis), (), 0, dims[axis]) for axis in range(len(dims))]
    drawn = drawn.at[tuple(place)].set(least)
    longest = dims.index(max(dims))
    place[longest] = (place[longest] + 1) % dims[longest]
    return drawn.at[tuple(place)].set(top_value)


def block_levels(stream_key, dims, pieces, smallest, top_value):
    def one(dim, blocks):
        steps = jax.random.uniform(jax.random.fold_in(jax.random.fold_in(stream_key, 6), dim), (blocks,), jnp.float32, smallest / len(pieces), top_value / len(pieces))
        return jnp.repeat(jnp.exp(steps), dims[dim] // blocks).reshape((-1,) + (1,) * (len(dims) - dim - 1))

    loudness = one(*pieces[0])
    for cut in pieces[1:]:
        loudness = loudness * one(*cut)
    return loudness


def noise(key, dims, scale, bound, cuts=(), held_as=jnp.bfloat16):
    gain = block_levels(key, dims, cuts, -0.22, 0.18) if cuts else 1.0
    entries = jax.random.normal(key, dims, jnp.float32) * scale * gain
    return jnp.minimum(jnp.maximum(entries, -bound), bound).astype(held_as)


def setup_inputs(seed: int = 0) -> dict:
    splits = jax.random.split(jax.random.key(seed), 18)
    dense_feats = noise(splits[0], (TOKENS, DENSE), 1.0, 6.0, ((0, 32),), jnp.float32)
    picks = draw_picks(jax.random.fold_in(splits[17], 71), 0)
    labels = touch_ends(jax.random.randint(splits[2], (TOKENS, TASKS), 0, 2), jax.random.fold_in(splits[2], 1), 0, 1).astype(jnp.int32)
    label_mask = draw_label_mask(jax.random.fold_in(splits[17], 71), 0)
    requests = touch_ends(jax.random.randint(splits[4], (DEVICES, N_BATCH, N_EXPERT, CAP), 0, ROWS_DEV), jax.random.fold_in(splits[4], 1), 0, ROWS_DEV - 1).astype(jnp.int32)
    table = noise(splits[5], (ROWS, EMB), 1.0, 6.0, ((0, 32),), jnp.float32)
    table_m = noise(splits[6], (ROWS, EMB), (0.02 / (DEVICES * TOK)), 9.5367431640625e-06, ((0, 32),), jnp.float32)
    table_v = jnp.clip(jnp.exp(math.log(1.4901160817412662e-13) - 1.3862944 * jax.random.uniform(splits[7], (ROWS, EMB), jnp.float32) ** block_levels(splits[7], (ROWS, EMB), ((0, 32),), -0.2, 0.2)), 3.7252902043531655e-14, 1.4901160817412662e-13)
    first_w = noise(splits[8], (EXPERTS, INPUT, HID), ((2.0 / INPUT) ** 0.5), 1.0, ((0, 4), (1, 8)), jnp.float32)
    first_m = noise(splits[9], (EXPERTS, INPUT, HID), (0.003 / (DEVICES * TOK) ** 0.5), 0.00024414062, ((0, 4), (1, 8)), jnp.float32)
    first_v = jnp.clip(jnp.exp(math.log(1.0986327819706432e-10) - 1.3862944 * jax.random.uniform(splits[10], (EXPERTS, INPUT, HID), jnp.float32) ** block_levels(splits[10], (EXPERTS, INPUT, HID), ((0, 4), (1, 8)), -0.2, 0.2)), 2.746581954926608e-11, 1.0986327819706432e-10)
    second_w = noise(splits[11], (EXPERTS, HID, OUT), ((2.0 / HID) ** 0.5), 1.25, ((0, 4), (1, 8)), jnp.float32)
    second_m = noise(splits[12], (EXPERTS, HID, OUT), (0.003 / (DEVICES * TOK) ** 0.5), 0.00024414062, ((0, 4), (1, 8)), jnp.float32)
    second_v = draw_second_v(jax.random.fold_in(splits[17], 71), 0)
    small = draw_small(jax.random.fold_in(splits[17], 71), 0)
    small_m = noise(splits[15], (SMALL,), (0.03 / (DEVICES * TOK) ** 0.5), 0.0024414062, (), jnp.float32)
    small_v = draw_small_v(jax.random.fold_in(splits[17], 71), 0)
    return dict(dense_feats=dense_feats, picks=picks, labels=labels, label_mask=label_mask, requests=requests, table=table, table_m=table_m, table_v=table_v, first_w=first_w, first_m=first_m, first_v=first_v, second_w=second_w, second_m=second_m, second_v=second_v, small=small, small_m=small_m, small_v=small_v)


HI = lax.Precision.HIGHEST

@jax.custom_vjp
def low(v):
    return lax.optimization_barrier(v.astype(jnp.bfloat16)).astype(jnp.float32)

@jax.custom_vjp
def low_back(v):
    return v

def low_keep(v):
    return (low(v), None)

def low_pass(kept, grad):
    return (grad,)

def back_keep(v):
    return (v, None)

def back_low(kept, grad):
    return (low(grad),)
low.defvjp(low_keep, low_pass)
low_back.defvjp(back_keep, back_low)

def unpack(flat, experts):
    shapes = [(experts, HID), (experts, OUT), (DENSE + 1, DOUT), (INPUT + 1, TASKS * experts), (TASKS, OUT + 1, TOWER), (TASKS, TOWER + 1)]
    parts = []
    offset = 0
    for shape in shapes:
        length = 1
        for extent in shape:
            length = length * extent
        parts.append(flat[offset:offset + length].reshape(shape))
        offset = offset + length
    return parts

def adamw(weight, first, second, grad, rate):
    first = 0.9 * first + 0.1 * grad
    second = 0.999 * second + 0.001 * grad * grad
    fix_one = 1.0 - 0.9 ** STEP
    fix_two = 1.0 - 0.999 ** STEP
    weight = weight - rate * (first / fix_one / (jnp.sqrt(second / fix_two) + 1e-08) + 0.01 * weight)
    return (weight, first, second)

def block_loss(params, block, counts):
    table, first_w, second_w, small = params
    rows, dense, target, mask = block
    bias_one, bias_two, dense_w, gate_w, tower_w, head_w = unpack(small, EXPERTS)
    width = rows.shape[0]
    emb = low(table[rows]).reshape(width, FIELDS * EMB)
    dense_proj = low(jnp.dot(dense, dense_w[:DENSE], precision=HI) + dense_w[DENSE])
    inputs = jnp.concatenate([emb, dense_proj], 1)
    gate_logits = low_back(jnp.dot(inputs, low(gate_w[:INPUT]), precision=HI) + gate_w[INPUT])
    probs = jax.nn.softmax(gate_logits.reshape(width, TASKS, EXPERTS), axis=-1)
    gates = low(probs)
    pre_one = jnp.einsum('ti,eih->teh', inputs, low(first_w), precision=HI) + bias_one[None]
    hidden = low(low_back(jax.nn.silu(pre_one)))
    pre_two = jnp.einsum('teh,eho->teo', hidden, low(second_w), precision=HI) + bias_two[None]
    expert_out = low_back(jax.nn.silu(pre_two))
    mixed = jnp.einsum('tke,teo->tko', gates, expert_out, precision=HI)
    mixed_low = low(low_back(mixed))
    tower_pre = low_back(jnp.einsum('tko,koh->tkh', mixed_low, low(tower_w[:, :OUT]), precision=HI) + tower_w[:, OUT][None])
    tower_act = jax.nn.silu(tower_pre)
    logits = jnp.einsum('tkh,kh->tk', tower_act, head_w[:, :TOWER], precision=HI) + head_w[:, TOWER]
    return jnp.sum(mask * (jax.nn.softplus(logits) - target * logits) / counts)

def reference(dense_feats, picks, labels, label_mask, requests, table, table_m, table_v, first_w, first_m, first_v, second_w, second_m, second_v, small, small_m, small_v):
    block = min(4096, TOKENS)
    blocks = TOKENS // block
    device = (jnp.arange(TOKENS, dtype=jnp.int32) // TOK)[:, None]
    flat_req = requests.reshape(DEVICES, DEVICES * CAP)
    rows = (flat_req[device, picks] + picks // CAP * ROWS_DEV).astype(jnp.int32)
    mask = label_mask.astype(jnp.float32)
    target = labels.astype(jnp.float32)
    counts = jnp.maximum(lax.optimization_barrier(jnp.sum(mask, 0)), 1.0)
    data = (rows.reshape(blocks, block, FIELDS), dense_feats.reshape(blocks, block, DENSE), target.reshape(blocks, block, TASKS), mask.reshape(blocks, block, TASKS))

    def total(params):
        step_fn = jax.checkpoint(lambda prm, blk: block_loss(prm, blk, counts))

        def scan_body(carry, blk):
            return (carry + step_fn(params, blk), None)
        result, unused = lax.scan(scan_body, jnp.zeros((), jnp.float32), data)
        return result
    params = (table, first_w, second_w, small)
    loss, pull = jax.vjp(total, params)
    grads = pull(jnp.ones((), loss.dtype))[0]
    new_table, new_table_m, new_table_v = adamw(table, table_m, table_v, grads[0], 0.3)
    new_first, new_first_m, new_first_v = adamw(first_w, first_m, first_v, grads[1], 0.15)
    new_second, new_second_m, new_second_v = adamw(second_w, second_m, second_v, grads[2], 0.15)
    new_small, new_small_m, new_small_v = adamw(small, small_m, small_v, grads[3], 0.15)
    return (loss, new_table, new_table_m, new_table_v, new_first, new_first_m, new_first_v, new_second, new_second_m, new_second_v, new_small, new_small_m, new_small_v)
```

```python
import collections
import functools

import jax
import jax.numpy as jnp
from jax import lax
from jax.experimental import pallas as pl
from jax.experimental.pallas import tpu as pltpu
from jax.sharding import PartitionSpec as P

FIELDS = 26
EMB = 16
DENSE = 13
DOUT = 96
HID = 256
OUT = 128
TOWER = 64
TASKS = 2
STEP = 5
GROUP_TOK = 64
INPUT = 512


HI = lax.Precision.HIGHEST


def unpack(flat, experts):
    shapes = [
        (experts, HID),
        (experts, OUT),
        (DENSE + 1, DOUT),
        (INPUT + 1, TASKS * experts),
        (TASKS, OUT + 1, TOWER),
        (TASKS, TOWER + 1),
    ]
    parts = []
    offset = 0
    for shape in shapes:
        length = 1
        for extent in shape:
            length = length * extent
        parts.append(flat[offset : offset + length].reshape(shape))
        offset = offset + length
    return parts


def adamw(weight, first, second, grad, rate):
    first = 0.9 * first + 0.1 * grad
    second = 0.999 * second + 0.001 * grad * grad
    fix_one = 1.0 - 0.9**STEP
    fix_two = 1.0 - 0.999**STEP
    weight = weight - rate * (
        first / fix_one / (jnp.sqrt(second / fix_two) + 1e-08) + 0.01 * weight
    )
    return (weight, first, second)


def silu_slope(value):
    sig = jax.nn.sigmoid(value)
    return sig * (1.0 + value * (1.0 - sig))


def split_three(values):
    upper = values.astype(jnp.bfloat16)
    rest = values - upper.astype(jnp.float32)
    middle = rest.astype(jnp.bfloat16)
    lower_part = (rest - middle.astype(jnp.float32)).astype(jnp.bfloat16)
    return jnp.concatenate([upper, middle, lower_part], -1)


def join_three(values):
    return values[:, :EMB] + values[:, EMB : 2 * EMB] + values[:, 2 * EMB :]


def one_hot(index, extent):
    return (index[:, None] == jnp.arange(extent, dtype=jnp.int32)[None, :]).astype(jnp.bfloat16)


def pick_rows(index, source):
    return jnp.dot(
        one_hot(index, source.shape[0]), source, preferred_element_type=jnp.float32
    ).astype(jnp.bfloat16)


def add_rows(index, values, extent):
    spread = lax.dot_general(
        one_hot(index, extent),
        split_three(values),
        (((0,), (0,)), ((), ())),
        preferred_element_type=jnp.float32,
    )
    return join_three(spread)


def expert_forward(inputs, first_w, second_w, first_b, second_b):
    pre_one = (
        jnp.einsum("ti,eih->teh", inputs, first_w, preferred_element_type=jnp.float32)
        + first_b[None]
    )
    hidden = jax.nn.silu(pre_one).astype(jnp.bfloat16)
    pre_two = (
        jnp.einsum("teh,eho->teo", hidden, second_w, preferred_element_type=jnp.float32)
        + second_b[None]
    )
    return (pre_one, hidden, pre_two, jax.nn.silu(pre_two))


def expert_backward(inputs, first_w, second_w, pre_one, hidden, pre_two, d_out):
    d_two = (silu_slope(pre_two) * d_out).astype(jnp.bfloat16)
    d_second_w = jnp.einsum("teh,teo->eho", hidden, d_two, preferred_element_type=jnp.float32)
    d_second_b = jnp.sum(d_two, 0, dtype=jnp.float32)
    d_hidden = jnp.einsum("teo,eho->teh", d_two, second_w, preferred_element_type=jnp.float32)
    d_one = (silu_slope(pre_one) * d_hidden).astype(jnp.bfloat16)
    d_first_w = jnp.einsum("ti,teh->eih", inputs, d_one, preferred_element_type=jnp.float32)
    d_first_b = jnp.sum(d_one, 0, dtype=jnp.float32)
    d_inputs = jnp.einsum("teh,eih->ti", d_one, first_w, preferred_element_type=jnp.float32)
    return (d_first_w, d_second_w, d_first_b, d_second_b, d_inputs)


def plain(
    dense_feats,
    picks,
    labels,
    label_mask,
    requests,
    table,
    table_m,
    table_v,
    first_w,
    first_m,
    first_v,
    second_w,
    second_m,
    second_v,
    small,
    small_m,
    small_v,
):
    groups = lax.axis_size("batch")
    experts = lax.axis_size("expert")
    devices = groups * experts
    expert_idx = lax.axis_index("expert")
    tokens = dense_feats.shape[0]
    slots = requests.shape[-1]
    rows_dev = table.shape[0]
    tok_groups = tokens // GROUP_TOK
    sub_slots = slots // tok_groups
    group_slots = devices * sub_slots
    total_asked = devices * slots
    ask_block = min(1024, total_asked)
    bias_one, bias_two, dense_w, gate_w, tower_w, head_w = unpack(small, experts)
    first_full, second_full = (
        lax.all_gather(first_w.astype(jnp.bfloat16), "batch", axis=1, tiled=True),
        lax.all_gather(second_w.astype(jnp.bfloat16), "batch", axis=1, tiled=True),
    )
    asked = lax.all_to_all(
        lax.all_to_all(requests[0], "batch", split_axis=0, concat_axis=0, tiled=True),
        "expert",
        split_axis=1,
        concat_axis=1,
        tiled=True,
    )
    asked_blocks = asked.reshape(total_asked // ask_block, ask_block)
    table_low = table.astype(jnp.bfloat16)
    sent_rows = lax.map(lambda index: pick_rows(index, table_low), asked_blocks)
    sent_rows = sent_rows.reshape(groups, experts, slots * EMB)
    got_rows = lax.all_to_all(
        lax.all_to_all(sent_rows, "batch", split_axis=0, concat_axis=0, tiled=True),
        "expert",
        split_axis=1,
        concat_axis=1,
        tiled=True,
    )
    by_group = (
        got_rows.reshape(devices, tok_groups, sub_slots, EMB)
        .transpose(1, 0, 2, 3)
        .reshape(tok_groups, group_slots, EMB)
    )
    local_pick = (picks // slots * sub_slots + picks % sub_slots).reshape(
        tok_groups, GROUP_TOK * FIELDS
    )
    emb = lax.map(lambda item: pick_rows(item[0], item[1]), (local_pick, by_group)).reshape(
        tokens, FIELDS * EMB
    )
    dense_proj = jnp.dot(dense_feats, dense_w[:DENSE], precision=HI) + dense_w[DENSE]
    inputs = jnp.concatenate([emb, dense_proj.astype(jnp.bfloat16)], 1)
    gate_low = gate_w[:INPUT].astype(jnp.bfloat16)
    gate_logits = jnp.dot(inputs, gate_low, preferred_element_type=jnp.float32) + gate_w[INPUT]
    probs = jax.nn.softmax(gate_logits.reshape(tokens, TASKS, experts), axis=-1)
    gates = probs.astype(jnp.bfloat16)
    all_inputs, all_gates = (
        lax.all_gather(inputs, "expert", axis=0, tiled=True),
        lax.all_gather(gates.reshape(tokens, TASKS * experts), "expert", axis=0, tiled=True),
    )
    own_gates = lax.dynamic_slice_in_dim(
        all_gates.reshape(-1, TASKS, experts), expert_idx, 1, 2
    ).astype(jnp.float32)
    first_use, second_use = (first_full, second_full)
    first_b = lax.dynamic_slice_in_dim(bias_one, expert_idx, 1, 0)
    second_b = lax.dynamic_slice_in_dim(bias_two, expert_idx, 1, 0)
    pre_one, hidden, pre_two, expert_out = expert_forward(
        all_inputs, first_use, second_use, first_b, second_b
    )
    terms = jnp.einsum("tke,teo->tko", own_gates, expert_out, precision=HI).reshape(-1, TASKS * OUT)
    mixed = lax.psum_scatter(terms.astype(jnp.bfloat16), "expert", scatter_dimension=0, tiled=True)
    mask = label_mask.astype(jnp.float32)
    target = labels.astype(jnp.float32)
    counts = jnp.maximum(lax.psum(jnp.sum(mask, 0), ("batch", "expert")), 1.0)
    mixed_low = mixed.reshape(tokens, TASKS, OUT)
    tower_low = tower_w[:, :OUT].astype(jnp.bfloat16)
    tower_pre = (
        jnp.einsum("tko,koh->tkh", mixed_low, tower_low, preferred_element_type=jnp.float32)
        + tower_w[:, OUT][None]
    )
    tower_act = jax.nn.silu(tower_pre)
    logits = jnp.einsum("tkh,kh->tk", tower_act, head_w[:, :TOWER], precision=HI) + head_w[:, TOWER]
    loss_local = jnp.sum(mask * (jax.nn.softplus(logits) - target * logits) / counts)
    d_logits = mask * (jax.nn.sigmoid(logits) - target) / counts
    d_head = jnp.concatenate(
        [
            jnp.einsum("tkh,tk->kh", tower_act, d_logits, precision=HI),
            jnp.sum(d_logits, 0)[:, None],
        ],
        1,
    )
    d_act = d_logits[:, :, None] * head_w[None, :, :TOWER]
    d_tower_pre = (silu_slope(tower_pre) * d_act).astype(jnp.bfloat16)
    d_tower = jnp.concatenate(
        [
            jnp.einsum("tko,tkh->koh", mixed_low, d_tower_pre, preferred_element_type=jnp.float32),
            jnp.sum(d_tower_pre, 0, dtype=jnp.float32)[:, None, :],
        ],
        1,
    )
    d_mixed = jnp.einsum(
        "tkh,koh->tko", d_tower_pre, tower_low, preferred_element_type=jnp.float32
    ).astype(jnp.bfloat16)
    all_d_mixed = (
        lax.all_gather(d_mixed.reshape(tokens, TASKS * OUT), "expert", axis=0, tiled=True)
        .reshape(-1, TASKS, OUT)
        .astype(jnp.float32)
    )
    d_out = jnp.einsum("tke,tko->teo", own_gates, all_d_mixed, precision=HI)
    d_gate_col = jnp.einsum("teo,tko->tke", expert_out, all_d_mixed, precision=HI)
    d_first_w, d_second_w, d_first_b, d_second_b, d_rows = expert_backward(
        all_inputs, first_use, second_use, pre_one, hidden, pre_two, d_out
    )
    onehot = (jnp.arange(experts) == expert_idx).astype(jnp.float32)
    d_gate_full = (d_gate_col * onehot[None, None, :]).reshape(-1, TASKS * experts)
    d_inputs, d_gates = (
        lax.psum_scatter(
            d_rows.astype(jnp.bfloat16), "expert", scatter_dimension=0, tiled=True
        ).astype(jnp.float32),
        lax.psum_scatter(
            d_gate_full.astype(jnp.bfloat16), "expert", scatter_dimension=0, tiled=True
        ).astype(jnp.float32),
    )
    d_gates = d_gates.reshape(tokens, TASKS, experts)
    d_first_b = onehot[:, None] * d_first_b
    d_second_b = onehot[:, None] * d_second_b
    d_gate_logits = (
        (probs * (d_gates - jnp.sum(probs * d_gates, -1, keepdims=True)))
        .astype(jnp.bfloat16)
        .reshape(tokens, TASKS * experts)
    )
    d_gate_w = jnp.concatenate(
        [
            jnp.dot(inputs.T, d_gate_logits, preferred_element_type=jnp.float32),
            jnp.sum(d_gate_logits, 0, dtype=jnp.float32)[None],
        ],
        0,
    )
    d_x = d_inputs + jnp.dot(d_gate_logits, gate_low.T, preferred_element_type=jnp.float32)
    d_dense = d_x[:, FIELDS * EMB :]
    d_dense_w = jnp.concatenate(
        [jnp.dot(dense_feats.T, d_dense, precision=HI), jnp.sum(d_dense, 0)[None]], 0
    )
    d_emb = d_x[:, : FIELDS * EMB].reshape(tok_groups, GROUP_TOK * FIELDS, EMB)
    slot_grads = lax.map(lambda item: add_rows(item[0], item[1], group_slots), (local_pick, d_emb))
    slot_grads = (
        slot_grads.reshape(tok_groups, devices, sub_slots, EMB)
        .transpose(1, 0, 2, 3)
        .reshape(groups, experts, slots * EMB)
    )
    owner_grads = lax.all_to_all(
        lax.all_to_all(
            slot_grads.astype(jnp.bfloat16), "batch", split_axis=0, concat_axis=0, tiled=True
        ),
        "expert",
        split_axis=1,
        concat_axis=1,
        tiled=True,
    ).astype(slot_grads.dtype)
    owner_blocks = owner_grads.reshape(total_asked // ask_block, ask_block, EMB)

    def add_block(total, item):
        return (total + add_rows(item[0], item[1], rows_dev), None)

    table_grad, unused = lax.scan(
        add_block, jnp.zeros((rows_dev, EMB), jnp.float32), (asked_blocks, owner_blocks)
    )
    grad_first, grad_second = (
        lax.psum_scatter(
            d_first_w.astype(jnp.bfloat16), "batch", scatter_dimension=1, tiled=True
        ).astype(jnp.float32),
        lax.psum_scatter(
            d_second_w.astype(jnp.bfloat16), "batch", scatter_dimension=1, tiled=True
        ).astype(jnp.float32),
    )
    flat_grads = jnp.concatenate(
        [
            d_first_b.reshape(-1),
            d_second_b.reshape(-1),
            d_dense_w.reshape(-1),
            d_gate_w.reshape(-1),
            d_tower.reshape(-1),
            d_head.reshape(-1),
        ]
    )
    grad_small, loss = lax.psum((flat_grads, loss_local), ("batch", "expert"))
    new_table, new_table_m, new_table_v = adamw(table, table_m, table_v, table_grad, 0.3)
    new_first, new_first_m, new_first_v = adamw(first_w, first_m, first_v, grad_first, 0.15)
    new_second, new_second_m, new_second_v = adamw(second_w, second_m, second_v, grad_second, 0.15)
    new_small, new_small_m, new_small_v = adamw(small, small_m, small_v, grad_small, 0.15)
    return (
        loss,
        new_table,
        new_table_m,
        new_table_v,
        new_first,
        new_first_m,
        new_first_v,
        new_second,
        new_second_m,
        new_second_v,
        new_small,
        new_small_m,
        new_small_v,
    )


MESH = pl.DeviceIdType.MESH
BF = jnp.bfloat16
F32 = jnp.float32
NN = (((1,), (0,)), ((), ()))
NT = (((1,), (1,)), ((), ()))
KEYS = 256
CHUNK = 256
LANES = 128
ONES = 16

Sizes = collections.namedtuple(
    "Sizes",
    (
        "groups",
        "experts",
        "devices",
        "slots",
        "rows",
        "tokens",
        "first",
        "second",
        "pack",
        "span",
    ),
)


def sizes_of(mesh, tokens, slots, rows):
    groups = mesh.shape["batch"]
    experts = mesh.shape["expert"]
    first = INPUT // groups
    second = HID // groups
    span = tokens * LANES // slots
    return Sizes(
        groups,
        experts,
        groups * experts,
        slots,
        rows,
        tokens,
        first,
        second,
        first + second // 2,
        span,
    )


def fits(size):
    return (
        size.slots % LANES == 0
        and size.slots & (size.slots - 1) == 0
        and size.span == CHUNK
        and size.second % 32 == 0
        and size.first % 16 == 0
        and size.groups % 2 == 0
        and size.devices % 2 == 0
        and size.rows % KEYS == 0
        and size.experts == 4
    )


def mm(left, right, dims=NN, precision=None):
    return lax.dot_general(left, right, dims, preferred_element_type=F32, precision=precision)


def here(size):
    group = lax.axis_index("batch")
    expert = lax.axis_index("expert")
    return group, expert, group * size.experts + expert


def place(size, device):
    return (lax.div(device, size.experts), lax.rem(device, size.experts))


def greet(size, me):
    barrier = pltpu.get_barrier_semaphore()

    def one(step, carry):
        peer = lax.rem(me + step, size.devices)
        pl.semaphore_signal(barrier, inc=1, device_id=place(size, peer), device_id_type=MESH)
        return carry

    lax.fori_loop(1, size.devices, one, 0)
    return barrier


def push(source, target, sent, landed, where):
    return pltpu.make_async_remote_copy(
        src_ref=source,
        dst_ref=target,
        send_sem=sent,
        recv_sem=landed,
        device_id=where,
        device_id_type=MESH,
    )


def spread(index, extent, width):
    return lax.broadcasted_iota(jnp.int32, (extent, width), 0) == index


def as_low(flag):
    return jnp.where(flag, 1.0, 0.0).astype(BF)


def look_up(cells, key, high, levels):
    found = mm(cells, as_low(spread(key, KEYS, key.shape[1])))
    result = found[:EMB]
    for level in range(1, levels):
        result = jnp.where(high == level, found[level * EMB : (level + 1) * EMB], result)
    return result


def levels_of(values, high, levels):
    return jnp.concatenate(
        [jnp.where(high == level, values, 0.0) for level in range(levels)], 0
    ).astype(BF)


def front(
    size,
    requests,
    mask,
    table,
    first,
    second,
    asked,
    got,
    gathered,
    totals,
    message,
    cells,
    rows,
    ask_sent,
    ask_landed,
    row_sent,
    row_landed,
    z_sent,
    z_landed,
    y_sent,
    y_landed,
    c_sent,
    c_landed,
):
    group, expert, me = here(size)
    slots, devices, experts = size.slots, size.devices, size.experts
    chips = size.groups // 2
    chip, core = lax.div(group, 2), lax.rem(group, 2)
    barrier = greet(size, me)
    valid = mask[...].astype(F32)
    lane = lax.broadcasted_iota(jnp.int32, (1, LANES), 1)
    count = jnp.where(
        lane == 0,
        jnp.sum(valid[0:1], 1, keepdims=True),
        jnp.where(lane == 1, jnp.sum(valid[1:2], 1, keepdims=True), 0.0),
    ).astype(jnp.int32)
    for part in range(size.groups):
        for one in range(experts):
            peer = part * experts + one
            message[peer, :, :slots] = requests[part, one : one + 1, :]
            message[peer, :, slots:] = count
    gathered[group, expert, : size.first, :] = first[...].astype(BF)
    half = size.second // 2
    gathered[group, expert, size.first :, :LANES] = second[:half].astype(BF)
    gathered[group, expert, size.first :, LANES:] = second[half:].astype(BF)
    blocks = size.rows // KEYS
    for block in range(blocks):
        cells[block * EMB : (block + 1) * EMB, :] = table[
            :, block * KEYS : (block + 1) * KEYS
        ].astype(BF)
    pl.semaphore_wait(barrier, devices - 1)

    def ask(step, receive):
        peer = lax.rem(me + (devices - step if receive else step), devices)
        return push(
            message.at[peer],
            asked.at[peer if receive else me],
            ask_sent.at[step],
            ask_landed.at[peer if receive else me],
            place(size, peer),
        )

    def answer(step, receive):
        peer = lax.rem(me + devices - step, devices)
        return push(
            rows.at[peer],
            got.at[me],
            row_sent.at[step],
            row_landed.at[me],
            place(size, peer),
        )

    def arrival(step):
        peer = lax.rem(me + step, devices)
        return push(
            rows.at[peer],
            got.at[peer],
            row_sent.at[step],
            row_landed.at[peer],
            place(size, peer),
        )

    def along_z(step, receive):
        other = lax.rem(expert + (experts - step if receive else step), experts)
        block = gathered.at[group, other if receive else expert]
        return push(
            block, block, z_sent.at[step], z_landed.at[step], (group, other)
        )

    def along_y(step, receive):
        other = lax.rem(chip + (chips - step if receive else step), chips)
        block = gathered.at[(other if receive else chip) * 2 + core]
        return push(
            block, block, y_sent.at[step], y_landed.at[step], (other * 2 + core, expert)
        )

    def across(step, receive):
        other = lax.rem(chip + chips - step, chips)
        block = gathered.at[other * 2 + (1 - core if receive else core)]
        return push(
            block, block, c_sent.at[step], c_landed.at[step], (chip * 2 + 1 - core, expert)
        )

    def start_ask(step, carry):
        ask(step, False).start()
        return carry

    lax.fori_loop(1, devices, start_ask, 0)
    for step in range(1, experts):
        along_z(step, False).start()

    def serve(peer):
        index = asked[peer, :, :slots]
        rows[peer] = look_up(cells[...], index & (KEYS - 1), index >> 8, blocks).astype(BF)

    asked[me] = message[me]
    serve(me)
    got[me] = rows[me]

    def serve_one(step, carry):
        peer = lax.rem(me + devices - step, devices)
        ask(step, True).wait_recv()
        serve(peer)
        answer(step, False).start()
        return carry

    third = devices // 4
    lax.fori_loop(1, third, serve_one, 0)
    for step in range(1, experts):
        along_z(step, True).wait_recv()
    for step in range(1, chips):
        along_y(step, False).start()
    across(0, False).start()
    lax.fori_loop(third, devices, serve_one, 0)
    for step in range(1, chips):
        along_y(step, True).wait_recv()
        across(step, False).start()
    total = jnp.zeros((1, LANES), jnp.int32)
    for peer in range(devices):
        total = total + asked[peer, :, slots:]
    totals[...] = jnp.maximum(total.astype(F32), 1.0)

    def finish(step, carry):
        arrival(step).wait_recv()
        ask(step, False).wait_send()
        answer(step, False).wait_send()
        return carry

    lax.fori_loop(1, devices, finish, 0)
    for step in range(1, experts):
        along_z(step, False).wait_send()
    for step in range(1, chips):
        along_y(step, False).wait_send()
    for step in range(chips):
        across(step, True).wait_recv()
        across(step, False).wait_send()


def sigmoid(value):
    return 0.5 + 0.5 * jnp.tanh(0.5 * value)


def middle(
    size,
    got,
    picks,
    dense,
    labels,
    mask,
    totals,
    gathered,
    vectors,
    gate_t,
    gate_n,
    tower_n,
    tower_t,
    dense_w,
    out_slots,
    out_grads,
    out_bias_one,
    out_bias_two,
    out_dense,
    out_gate,
    out_tower,
    out_head,
    out_loss,
    columns,
    first_t,
    second_n,
    second_t,
    wide,
    feats,
    slot_cells,
    chosen,
    inputs,
    slope_one,
    slope_two,
    hidden,
    outs,
    mixes,
    deltas,
    d_inputs,
    slot_sum,
    sum_first,
    sum_second,
    sum_gate,
    sum_dense,
    sum_tower,
    sum_head,
    loss_sum,
):
    experts, slots = size.experts, size.slots
    levels = size.devices // 2
    shift = slots.bit_length() - 1
    half = size.second // 2
    flipped = jnp.concatenate([vectors[...], jnp.zeros((LANES - 16, LANES), F32)], 0).T
    for column in range(16):
        columns[column] = jnp.broadcast_to(flipped[:, column : column + 1], (LANES, LANES))
    for expert in range(experts):
        for part in range(size.groups):
            wide[
                part * size.first : (part + 1) * size.first, expert * HID : (expert + 1) * HID
            ] = gathered[part, expert, : size.first, :]
            base = part * size.second
            second_n[expert, base : base + half, :] = gathered[part, expert, size.first :, :LANES]
            second_n[expert, base + half : base + 2 * half, :] = gathered[
                part, expert, size.first :, LANES:
            ]
        first_t[expert] = wide[:, expert * HID : (expert + 1) * HID].T
        second_t[expert] = second_n[expert].T
    wide[:, experts * HID :] = gate_n[...]
    feats[...] = jnp.ones_like(feats)
    feats[:DENSE, :] = dense[...]
    inputs[INPUT:, :] = jnp.ones((ONES, CHUNK), BF)
    for expert in range(experts):
        hidden[expert, HID:, :] = jnp.ones((ONES, CHUNK), BF)
    for task in range(TASKS):
        mixes[task, OUT:, :] = jnp.ones((ONES, CHUNK), BF)
    deltas[experts * HID :, :] = jnp.zeros((LANES, CHUNK), BF)
    for total in (sum_first, sum_second, sum_gate, sum_dense, sum_tower, sum_head, loss_sum):
        total[...] = jnp.zeros_like(total)

    def column(index, begin=0, end=LANES):
        block = columns[index, begin:end, :]
        return jnp.concatenate([block] * (CHUNK // LANES), 1)

    def chunk(step, carry):
        token = pl.multiple_of(step * CHUNK, CHUNK)
        slot = pl.multiple_of(step * LANES, LANES)
        here_tokens = pl.ds(token, CHUNK)
        for owner in range(size.devices):
            level, lower = owner // 2, owner % 2
            slot_cells[
                level * EMB : (level + 1) * EMB, lower * LANES : (lower + 1) * LANES
            ] = got[owner, :, pl.ds(slot, LANES)]

        def split(field):
            index = picks[pl.ds(field, 1), here_tokens]
            owner = index >> shift
            return (owner & 1) * LANES + (index & (LANES - 1)), owner >> 1

        def pick(field, carry):
            key, high = split(field)
            flags = as_low(spread(key, KEYS, CHUNK))
            chosen[field] = flags
            found = mm(slot_cells[...], flags)
            result = found[:EMB]
            for level in range(1, levels):
                result = jnp.where(high == level, found[level * EMB : (level + 1) * EMB], result)
            inputs[pl.ds(pl.multiple_of(field * EMB, EMB), EMB), :] = result.astype(BF)
            return carry

        lax.fori_loop(0, FIELDS, pick, 0)
        inputs[FIELDS * EMB : INPUT, :] = mm(
            dense_w[...], feats[:, here_tokens], precision=HI
        ).astype(BF)
        x = inputs[:INPUT, :]
        logits = mm(gate_t[...], x)[: TASKS * experts] + column(14, 0, TASKS * experts)
        probs, gates = [], []
        for task in range(TASKS):
            line = [logits[task * experts + e : task * experts + e + 1] for e in range(experts)]
            top = functools.reduce(jnp.maximum, line)
            powers = [jnp.exp(item - top) for item in line]
            whole = 1.0 / functools.reduce(jnp.add, powers)
            probs.append([item * whole for item in powers])
            gates.append([item.astype(BF).astype(F32) for item in probs[-1]])
        mixed = [None] * TASKS
        for expert in range(experts):
            pre = mm(first_t[expert], x) + jnp.concatenate(
                [column(2 * expert), column(2 * expert + 1)], 0
            )
            sig = sigmoid(pre)
            act = pre * sig
            slope_one[expert] = sig + act * (1.0 - sig)
            hidden[expert, :HID, :] = act.astype(BF)
            pre = mm(second_t[expert], hidden[expert, :HID, :]) + column(8 + expert)
            sig = sigmoid(pre)
            act = pre * sig
            slope_two[expert] = sig + act * (1.0 - sig)
            outs[expert] = act
            for task in range(TASKS):
                term = gates[task][expert] * act
                mixed[task] = term if mixed[task] is None else mixed[task] + term
        d_mixed = []
        for task in range(TASKS):
            mixes[task, :OUT, :] = mixed[task].astype(BF)
            low, high = task * TOWER, (task + 1) * TOWER
            pre = mm(tower_t[task], mixes[task, :OUT, :]) + column(12, low, high)
            sig = sigmoid(pre)
            act = pre * sig
            head = column(13, low, high)
            logit = jnp.sum(act * head, 0, keepdims=True) + column(15, task, task + 1)
            valid = mask[task : task + 1, here_tokens].astype(F32)
            target = labels[task : task + 1, here_tokens].astype(F32)
            scale = valid / totals[0:1, task : task + 1]
            soft = jnp.maximum(logit, 0.0) + jnp.log(1.0 + jnp.exp(-jnp.abs(logit)))
            loss_sum[...] += scale * (soft - target * logit)
            d_logit = scale * (sigmoid(logit) - target)
            d_pre = ((sig + act * (1.0 - sig)) * (d_logit * head)).astype(BF)
            sum_head[task] += mm(
                jnp.broadcast_to(d_logit, (8, CHUNK)),
                jnp.concatenate([act, jnp.ones((8, CHUNK), F32)], 0),
                NT,
                HI,
            )
            sum_tower[task] += mm(mixes[task], d_pre, NT)
            d_mixed.append(mm(tower_n[task], d_pre).astype(BF).astype(F32))
        d_gates = [[None] * experts for task in range(TASKS)]
        for expert in range(experts):
            d_out = gates[0][expert] * d_mixed[0] + gates[1][expert] * d_mixed[1]
            for task in range(TASKS):
                d_gates[task][expert] = jnp.sum(outs[expert] * d_mixed[task], 0, keepdims=True)
            d_two = (slope_two[expert] * d_out).astype(BF)
            sum_second[expert] += mm(hidden[expert], d_two, NT)
            d_one = (slope_one[expert] * mm(second_n[expert], d_two)).astype(BF)
            deltas[expert * HID : (expert + 1) * HID, :] = d_one
            sum_first[expert] += mm(inputs[...], d_one, NT)
        lines = []
        for task in range(TASKS):
            inner = functools.reduce(
                jnp.add, [probs[task][e] * d_gates[task][e] for e in range(experts)]
            )
            lines += [probs[task][e] * (d_gates[task][e] - inner) for e in range(experts)]
        lines.append(jnp.zeros((16 - TASKS * experts, CHUNK), F32))
        d_gate = jnp.concatenate(lines, 0).astype(BF)
        deltas[experts * HID : experts * HID + 16, :] = d_gate
        sum_gate[...] += mm(inputs[...], d_gate, NT)
        d_inputs[...] = mm(wide[...], deltas[...])
        sum_dense[...] += mm(feats[:, here_tokens], d_inputs[FIELDS * EMB :, :], NT, HI)
        slot_sum[...] = jnp.zeros_like(slot_sum)

        def give(field, carry):
            key, high = split(field)
            values = d_inputs[pl.ds(pl.multiple_of(field * EMB, EMB), EMB), :]
            slot_sum[...] += mm(levels_of(values, high, levels), chosen[field], NT)
            return carry

        lax.fori_loop(0, FIELDS, give, 0)
        for owner in range(size.devices):
            level, lower = owner // 2, owner % 2
            out_slots[owner, :, pl.ds(slot, LANES)] = slot_sum[
                level * EMB : (level + 1) * EMB, lower * LANES : (lower + 1) * LANES
            ].astype(BF)
        return carry

    lax.fori_loop(0, size.tokens // CHUNK, chunk, 0)
    for expert in range(experts):
        for part in range(size.groups):
            out_grads[part, expert, : size.first, :] = sum_first[
                expert, part * size.first : (part + 1) * size.first, :
            ].astype(BF)
            base = part * size.second
            out_grads[part, expert, size.first :, :LANES] = sum_second[
                expert, base : base + half, :
            ].astype(BF)
            out_grads[part, expert, size.first :, LANES:] = sum_second[
                expert, base + half : base + 2 * half, :
            ].astype(BF)
        out_bias_one[expert : expert + 1, :] = sum_first[expert, INPUT : INPUT + 1, :]
        out_bias_two[expert : expert + 1, :] = sum_second[expert, HID : HID + 1, :]
    out_dense[...] = sum_dense[...]
    out_gate[...] = sum_gate[...]
    out_tower[...] = sum_tower[...]
    out_head[...] = sum_head[...]
    out_loss[...] = loss_sum[...]


def back(
    size,
    slots_in,
    asked,
    grads,
    small,
    table_grad,
    first_grad,
    second_grad,
    small_sum,
    slots_got,
    small_got,
    core_got,
    core_sum,
    chip_got,
    chip_sum,
    z_got,
    slot_sent,
    slot_landed,
    small_sent,
    small_landed,
    whole_sent,
    whole_landed,
    c_sent,
    c_landed,
    y_sent,
    y_landed,
    z_sent,
    z_landed,
):
    group, expert, me = here(size)
    slots, devices, experts = size.slots, size.devices, size.experts
    chips = size.groups // 2
    chip, core = lax.div(group, 2), lax.rem(group, 2)
    blocks = size.rows // KEYS
    barrier = greet(size, me)
    table_grad[...] = jnp.zeros_like(table_grad)
    pl.semaphore_wait(barrier, devices - 1)

    def across(step, receive):
        other = lax.rem(chip + step, chips)
        return push(
            grads.at[other * 2 + 1 - core],
            core_got.at[other],
            c_sent.at[step],
            c_landed.at[step],
            (chip * 2 + 1 - core, expert),
        )

    def along_y(step, receive):
        other = lax.rem(chip + (chips - step if receive else step), chips)
        return push(
            core_sum.at[other],
            chip_got.at[step],
            y_sent.at[step],
            y_landed.at[step],
            (other * 2 + core, expert),
        )

    def along_z(step, receive):
        other = lax.rem(expert + (experts - step if receive else step), experts)
        return push(
            chip_sum.at[other], z_got.at[step], z_sent.at[step], z_landed.at[step], (group, other)
        )

    def to_all(source, target, sent, landed, step, receive, mine=False):
        peer = lax.rem(me + (devices - step if receive else step), devices)
        return push(
            source.at[me if mine else peer],
            target.at[peer if receive else me],
            sent.at[step],
            landed.at[peer if receive else me],
            place(size, peer),
        )

    def send_slots(step, receive):
        return to_all(slots_in, slots_got, slot_sent, slot_landed, step, receive)

    def send_small(step, receive):
        return to_all(small, small_got, small_sent, small_landed, step, receive)

    def send_whole(step, receive):
        return to_all(small_sum, small_sum, whole_sent, whole_landed, step, receive, True)

    for step in range(1, chips + 1):
        across(step % chips, False).start()

    def start_small(step, carry):
        send_small(step, False).start()
        return carry

    lax.fori_loop(1, devices, start_small, 0)

    def start_slots(step, carry):
        send_slots(step, False).start()
        return carry

    lax.fori_loop(1, devices, start_slots, 0)
    for step in range(1, chips + 1):
        other = lax.rem(chip + step, chips)
        across(step % chips, True).wait_recv()
        core_sum[other] = (
            grads[other * 2 + core].astype(F32) + core_got[other].astype(F32)
        ).astype(BF)
        if step < chips:
            along_y(step, False).start()
    small_got[me] = small[me]

    def add_small(step, total):
        send_small(step, True).wait_recv()
        return total + small_got[lax.rem(me + devices - step, devices)]

    small_sum[me] = lax.fori_loop(1, devices, add_small, small_got[me])

    def start_whole(step, carry):
        send_whole(step, False).start()
        return carry

    lax.fori_loop(1, devices, start_whole, 0)
    total = core_sum[chip].astype(F32)
    for step in range(1, chips):
        along_y(step, True).wait_recv()
        total = total + chip_got[step].astype(F32)
    chip_sum[...] = total.astype(BF)
    for step in range(1, experts):
        along_z(step, False).start()

    def gather(peer, values):
        index = asked[peer, :, :slots]
        levels = levels_of(values, index >> 8, blocks)
        spots = as_low(spread(index & (KEYS - 1), KEYS, slots))
        table_grad[...] += mm(levels, spots, NT)

    gather(me, slots_in[me].astype(F32))

    def gather_one(step, carry):
        peer = lax.rem(me + devices - step, devices)
        send_slots(step, True).wait_recv()
        gather(peer, slots_got[peer].astype(F32))
        return carry

    lax.fori_loop(1, devices, gather_one, 0)
    total = chip_sum[expert].astype(F32)
    for step in range(1, experts):
        along_z(step, True).wait_recv()
        total = total + z_got[step].astype(F32)
    half = size.second // 2
    first_grad[...] = total[: size.first]
    second_grad[:half, :] = total[size.first :, :LANES]
    second_grad[half:, :] = total[size.first :, LANES:]

    def finish(step, carry):
        send_whole(step, True).wait_recv()
        send_whole(step, False).wait_send()
        send_small(step, False).wait_send()
        send_slots(step, False).wait_send()
        return carry

    lax.fori_loop(1, devices, finish, 0)
    for step in range(chips):
        across(step, False).wait_send()
    for step in range(1, chips):
        along_y(step, False).wait_send()
    for step in range(1, experts):
        along_z(step, False).wait_send()


def update(size, *refs):
    grads, state, results = refs[:3], refs[3:12], refs[12:]
    table_grad = grads[0][...]
    wide = jnp.concatenate(
        [table_grad[b * EMB : (b + 1) * EMB] for b in range(size.rows // KEYS)], 1
    )
    for index, grad in enumerate((wide, grads[1][...], grads[2][...])):
        rate = 0.3 if index == 0 else 0.15
        values = [ref[...] for ref in state[3 * index : 3 * index + 3]]
        for ref, value in zip(results[3 * index : 3 * index + 3], adamw(*values, grad, rate)):
            ref[...] = value


def shape(dims, dtype=F32):
    return jax.ShapeDtypeStruct(dims, dtype)


def call(kernel, outs, scratch, remote=None):
    vmem = pl.BlockSpec(memory_space=pltpu.VMEM)
    params = dict(vmem_limit_bytes=56 * 2**20)
    if remote is not None:
        params.update(collective_id=remote, has_side_effects=True)
    return lambda *args: pl.pallas_call(
        kernel,
        out_shape=outs,
        in_specs=[vmem] * len(args),
        out_specs=[vmem] * len(outs),
        scratch_shapes=scratch,
        compiler_params=pltpu.CompilerParams(**params),
    )(*args)


def pads(array, dims):
    return jnp.pad(array, [(0, want - have) for want, have in zip(dims, array.shape)])


def local(
    size,
    dense_feats,
    picks,
    labels,
    label_mask,
    requests,
    table,
    table_m,
    table_v,
    first_w,
    first_m,
    first_v,
    second_w,
    second_m,
    second_v,
    small,
    small_m,
    small_v,
):
    devices, experts, groups = size.devices, size.experts, size.groups
    chips = groups // 2
    dma = pltpu.SemaphoreType.DMA
    vm = pltpu.VMEM
    message = size.slots + LANES
    asked, got, gathered, totals = call(
        functools.partial(front, size),
        [
            shape((devices, 1, message), jnp.int32),
            shape((devices, EMB, size.slots), BF),
            shape((groups, experts, size.pack, HID), BF),
            shape((1, LANES)),
        ],
        [
            vm((devices, 1, message), jnp.int32),
            vm((size.rows // KEYS * EMB, KEYS), BF),
            vm((devices, EMB, size.slots), BF),
        ]
        + [dma((devices,))] * 4
        + [dma((experts,))] * 2
        + [dma((chips,))] * 4,
        0,
    )(requests[0], label_mask.T, table.T, first_w[0], second_w[0])
    bias_one, bias_two, dense_w, gate_w, tower_w, head_w = unpack(small, experts)
    vectors = jnp.concatenate(
        [
            bias_one.reshape(8, LANES),
            bias_two,
            tower_w[:, OUT].reshape(1, LANES),
            head_w[:, :TOWER].reshape(1, LANES),
            pads(gate_w[INPUT][None], (1, LANES)),
            pads(head_w[:, TOWER][None], (1, LANES)),
        ],
        0,
    )
    gate_low = gate_w[:INPUT].astype(BF)
    tower_low = tower_w[:, :OUT].astype(BF)
    outs = call(
        functools.partial(middle, size),
        [
            shape((devices, EMB, size.slots), BF),
            shape((groups, experts, size.pack, HID), BF),
            shape((experts, HID)),
            shape((experts, OUT)),
            shape((16, DOUT)),
            shape((INPUT + ONES, 16)),
            shape((TASKS, OUT + ONES, TOWER)),
            shape((TASKS, 8, TOWER + 8)),
            shape((1, CHUNK)),
        ],
        [
            vm((16, LANES, LANES), F32),
            vm((experts, HID, INPUT), BF),
            vm((experts, HID, OUT), BF),
            vm((experts, OUT, HID), BF),
            vm((INPUT, experts * HID + LANES), BF),
            vm((16, size.tokens), F32),
            vm((devices // 2 * EMB, KEYS), BF),
            vm((FIELDS, KEYS, CHUNK), BF),
            vm((INPUT + ONES, CHUNK), BF),
            vm((experts, HID, CHUNK), F32),
            vm((experts, OUT, CHUNK), F32),
            vm((experts, HID + ONES, CHUNK), BF),
            vm((experts, OUT, CHUNK), F32),
            vm((TASKS, OUT + ONES, CHUNK), BF),
            vm((experts * HID + LANES, CHUNK), BF),
            vm((INPUT, CHUNK), F32),
            vm((devices // 2 * EMB, KEYS), F32),
            vm((experts, INPUT + ONES, HID), F32),
            vm((experts, HID + ONES, OUT), F32),
            vm((INPUT + ONES, 16), F32),
            vm((16, DOUT), F32),
            vm((TASKS, OUT + ONES, TOWER), F32),
            vm((TASKS, 8, TOWER + 8), F32),
            vm((1, CHUNK), F32),
        ],
    )(
        got,
        picks.T,
        dense_feats.T,
        labels.T,
        label_mask.T,
        totals,
        gathered,
        vectors,
        pads(gate_low.T, (16, INPUT)),
        pads(gate_low, (INPUT, LANES)),
        tower_low,
        tower_low.transpose(0, 2, 1),
        pads(dense_w.T, (DOUT, 16)),
    )
    slot_grads, grads, d_bias_one, d_bias_two, d_dense, d_gate, d_tower, d_head, loss = outs
    flat = jnp.concatenate(
        [
            d_bias_one.reshape(-1),
            d_bias_two.reshape(-1),
            d_dense[: DENSE + 1].reshape(-1),
            d_gate[: INPUT + 1, : TASKS * experts].reshape(-1),
            d_tower[:, : OUT + 1].reshape(-1),
            d_head[:, 0, : TOWER + 1].reshape(-1),
            jnp.sum(loss).reshape(1),
        ]
    )
    count = flat.shape[0] - 1
    lines = -(-(count + 1) // (devices * 8 * LANES)) * 8
    flat = jnp.pad(flat, (0, devices * lines * LANES - count - 1)).reshape(devices, lines, LANES)
    table_grad, first_grad, second_grad, flat = call(
        functools.partial(back, size),
        [
            shape((size.rows // KEYS * EMB, KEYS)),
            shape((size.first, HID)),
            shape((size.second, OUT)),
            shape((devices, lines, LANES)),
        ],
        [
            vm((devices, EMB, size.slots), BF),
            vm((devices, lines, LANES), F32),
            vm((chips, experts, size.pack, HID), BF),
            vm((chips, experts, size.pack, HID), BF),
            vm((chips, experts, size.pack, HID), BF),
            vm((experts, size.pack, HID), BF),
            vm((experts, size.pack, HID), BF),
        ]
        + [dma((devices,))] * 6
        + [dma((chips,))] * 4
        + [dma((experts,))] * 2,
        1,
    )(slot_grads, asked, grads, flat)
    tables = (table.T, table_m.T, table_v.T)
    firsts = (first_w[0], first_m[0], first_v[0])
    seconds = (second_w[0], second_m[0], second_v[0])
    new = call(
        functools.partial(update, size),
        [shape(a.shape) for a in tables + firsts + seconds],
        [],
    )(table_grad, first_grad, second_grad, *tables, *firsts, *seconds)
    flat = flat.reshape(-1)
    new_small = adamw(small, small_m, small_v, flat[:count], 0.15)
    return (
        (flat[count],)
        + tuple(a.T for a in new[:3])
        + tuple(a[None] for a in new[3:])
        + tuple(new_small)
    )


def solution(mesh):
    both = P(("batch", "expert"), None)
    shard = P("expert", "batch", None)
    ins = (both,) * 4 + (P(("batch", "expert"), None, None, None),) + (both,) * 3
    ins = ins + (shard,) * 6 + (P(),) * 3

    def step(*args):
        devices = mesh.shape["batch"] * mesh.shape["expert"]
        size = sizes_of(
            mesh, args[0].shape[0] // devices, args[4].shape[-1], args[5].shape[0] // devices
        )
        return jax.shard_map(
            functools.partial(local, size) if fits(size) else plain,
            mesh=mesh,
            in_specs=ins,
            out_specs=(P(),) + (both,) * 3 + (shard,) * 6 + (P(),) * 3,
            check_vma=False,
        )(*args)

    return step
```

```python
import collections
import functools

import jax
import jax.numpy as jnp
from jax import lax
from jax.experimental import pallas as pl
from jax.experimental.pallas import tpu as pltpu
from jax.sharding import PartitionSpec as P

FIELDS = 26
EMB = 16
DENSE = 13
DOUT = 96
HID = 256
OUT = 128
TOWER = 64
TASKS = 2
STEP = 5
GROUP_TOK = 64
INPUT = 512


HI = lax.Precision.HIGHEST


def unpack(flat, experts):
    shapes = [
        (experts, HID),
        (experts, OUT),
        (DENSE + 1, DOUT),
        (INPUT + 1, TASKS * experts),
        (TASKS, OUT + 1, TOWER),
        (TASKS, TOWER + 1),
    ]
    parts = []
    offset = 0
    for shape in shapes:
        length = 1
        for extent in shape:
            length = length * extent
        parts.append(flat[offset : offset + length].reshape(shape))
        offset = offset + length
    return parts


def adamw(weight, first, second, grad, rate):
    first = 0.9 * first + 0.1 * grad
    second = 0.999 * second + 0.001 * grad * grad
    fix_one = 1.0 - 0.9**STEP
    fix_two = 1.0 - 0.999**STEP
    weight = weight - rate * (
        first / fix_one / (jnp.sqrt(second / fix_two) + 1e-08) + 0.01 * weight
    )
    return (weight, first, second)


def silu_slope(value):
    sig = jax.nn.sigmoid(value)
    return sig * (1.0 + value * (1.0 - sig))


def split_three(values):
    upper = values.astype(jnp.bfloat16)
    rest = values - upper.astype(jnp.float32)
    middle = rest.astype(jnp.bfloat16)
    lower_part = (rest - middle.astype(jnp.float32)).astype(jnp.bfloat16)
    return jnp.concatenate([upper, middle, lower_part], -1)


def join_three(values):
    return values[:, :EMB] + values[:, EMB : 2 * EMB] + values[:, 2 * EMB :]


def one_hot(index, extent):
    return (index[:, None] == jnp.arange(extent, dtype=jnp.int32)[None, :]).astype(jnp.bfloat16)


def pick_rows(index, source):
    return jnp.dot(
        one_hot(index, source.shape[0]), source, preferred_element_type=jnp.float32
    ).astype(jnp.bfloat16)


def add_rows(index, values, extent):
    spread = lax.dot_general(
        one_hot(index, extent),
        split_three(values),
        (((0,), (0,)), ((), ())),
        preferred_element_type=jnp.float32,
    )
    return join_three(spread)


def expert_forward(inputs, first_w, second_w, first_b, second_b):
    pre_one = (
        jnp.einsum("ti,eih->teh", inputs, first_w, preferred_element_type=jnp.float32)
        + first_b[None]
    )
    hidden = jax.nn.silu(pre_one).astype(jnp.bfloat16)
    pre_two = (
        jnp.einsum("teh,eho->teo", hidden, second_w, preferred_element_type=jnp.float32)
        + second_b[None]
    )
    return (pre_one, hidden, pre_two, jax.nn.silu(pre_two))


def expert_backward(inputs, first_w, second_w, pre_one, hidden, pre_two, d_out):
    d_two = (silu_slope(pre_two) * d_out).astype(jnp.bfloat16)
    d_second_w = jnp.einsum("teh,teo->eho", hidden, d_two, preferred_element_type=jnp.float32)
    d_second_b = jnp.sum(d_two, 0, dtype=jnp.float32)
    d_hidden = jnp.einsum("teo,eho->teh", d_two, second_w, preferred_element_type=jnp.float32)
    d_one = (silu_slope(pre_one) * d_hidden).astype(jnp.bfloat16)
    d_first_w = jnp.einsum("ti,teh->eih", inputs, d_one, preferred_element_type=jnp.float32)
    d_first_b = jnp.sum(d_one, 0, dtype=jnp.float32)
    d_inputs = jnp.einsum("teh,eih->ti", d_one, first_w, preferred_element_type=jnp.float32)
    return (d_first_w, d_second_w, d_first_b, d_second_b, d_inputs)


def plain(
    dense_feats,
    picks,
    labels,
    label_mask,
    requests,
    table,
    table_m,
    table_v,
    first_w,
    first_m,
    first_v,
    second_w,
    second_m,
    second_v,
    small,
    small_m,
    small_v,
):
    groups = lax.axis_size("batch")
    experts = lax.axis_size("expert")
    devices = groups * experts
    expert_idx = lax.axis_index("expert")
    tokens = dense_feats.shape[0]
    slots = requests.shape[-1]
    rows_dev = table.shape[0]
    tok_groups = tokens // GROUP_TOK
    sub_slots = slots // tok_groups
    group_slots = devices * sub_slots
    total_asked = devices * slots
    ask_block = min(1024, total_asked)
    bias_one, bias_two, dense_w, gate_w, tower_w, head_w = unpack(small, experts)
    first_full, second_full = (
        lax.all_gather(first_w.astype(jnp.bfloat16), "batch", axis=1, tiled=True),
        lax.all_gather(second_w.astype(jnp.bfloat16), "batch", axis=1, tiled=True),
    )
    asked = lax.all_to_all(
        lax.all_to_all(requests[0], "batch", split_axis=0, concat_axis=0, tiled=True),
        "expert",
        split_axis=1,
        concat_axis=1,
        tiled=True,
    )
    asked_blocks = asked.reshape(total_asked // ask_block, ask_block)
    table_low = table.astype(jnp.bfloat16)
    sent_rows = lax.map(lambda index: pick_rows(index, table_low), asked_blocks)
    sent_rows = sent_rows.reshape(groups, experts, slots * EMB)
    got_rows = lax.all_to_all(
        lax.all_to_all(sent_rows, "batch", split_axis=0, concat_axis=0, tiled=True),
        "expert",
        split_axis=1,
        concat_axis=1,
        tiled=True,
    )
    by_group = (
        got_rows.reshape(devices, tok_groups, sub_slots, EMB)
        .transpose(1, 0, 2, 3)
        .reshape(tok_groups, group_slots, EMB)
    )
    local_pick = (picks // slots * sub_slots + picks % sub_slots).reshape(
        tok_groups, GROUP_TOK * FIELDS
    )
    emb = lax.map(lambda item: pick_rows(item[0], item[1]), (local_pick, by_group)).reshape(
        tokens, FIELDS * EMB
    )
    dense_proj = jnp.dot(dense_feats, dense_w[:DENSE], precision=HI) + dense_w[DENSE]
    inputs = jnp.concatenate([emb, dense_proj.astype(jnp.bfloat16)], 1)
    gate_low = gate_w[:INPUT].astype(jnp.bfloat16)
    gate_logits = jnp.dot(inputs, gate_low, preferred_element_type=jnp.float32) + gate_w[INPUT]
    probs = jax.nn.softmax(gate_logits.reshape(tokens, TASKS, experts), axis=-1)
    gates = probs.astype(jnp.bfloat16)
    all_inputs, all_gates = (
        lax.all_gather(inputs, "expert", axis=0, tiled=True),
        lax.all_gather(gates.reshape(tokens, TASKS * experts), "expert", axis=0, tiled=True),
    )
    own_gates = lax.dynamic_slice_in_dim(
        all_gates.reshape(-1, TASKS, experts), expert_idx, 1, 2
    ).astype(jnp.float32)
    first_use, second_use = (first_full, second_full)
    first_b = lax.dynamic_slice_in_dim(bias_one, expert_idx, 1, 0)
    second_b = lax.dynamic_slice_in_dim(bias_two, expert_idx, 1, 0)
    pre_one, hidden, pre_two, expert_out = expert_forward(
        all_inputs, first_use, second_use, first_b, second_b
    )
    terms = jnp.einsum("tke,teo->tko", own_gates, expert_out, precision=HI).reshape(-1, TASKS * OUT)
    mixed = lax.psum_scatter(terms.astype(jnp.bfloat16), "expert", scatter_dimension=0, tiled=True)
    mask = label_mask.astype(jnp.float32)
    target = labels.astype(jnp.float32)
    counts = jnp.maximum(lax.psum(jnp.sum(mask, 0), ("batch", "expert")), 1.0)
    mixed_low = mixed.reshape(tokens, TASKS, OUT)
    tower_low = tower_w[:, :OUT].astype(jnp.bfloat16)
    tower_pre = (
        jnp.einsum("tko,koh->tkh", mixed_low, tower_low, preferred_element_type=jnp.float32)
        + tower_w[:, OUT][None]
    )
    tower_act = jax.nn.silu(tower_pre)
    logits = jnp.einsum("tkh,kh->tk", tower_act, head_w[:, :TOWER], precision=HI) + head_w[:, TOWER]
    loss_local = jnp.sum(mask * (jax.nn.softplus(logits) - target * logits) / counts)
    d_logits = mask * (jax.nn.sigmoid(logits) - target) / counts
    d_head = jnp.concatenate(
        [
            jnp.einsum("tkh,tk->kh", tower_act, d_logits, precision=HI),
            jnp.sum(d_logits, 0)[:, None],
        ],
        1,
    )
    d_act = d_logits[:, :, None] * head_w[None, :, :TOWER]
    d_tower_pre = (silu_slope(tower_pre) * d_act).astype(jnp.bfloat16)
    d_tower = jnp.concatenate(
        [
            jnp.einsum("tko,tkh->koh", mixed_low, d_tower_pre, preferred_element_type=jnp.float32),
            jnp.sum(d_tower_pre, 0, dtype=jnp.float32)[:, None, :],
        ],
        1,
    )
    d_mixed = jnp.einsum(
        "tkh,koh->tko", d_tower_pre, tower_low, preferred_element_type=jnp.float32
    ).astype(jnp.bfloat16)
    all_d_mixed = (
        lax.all_gather(d_mixed.reshape(tokens, TASKS * OUT), "expert", axis=0, tiled=True)
        .reshape(-1, TASKS, OUT)
        .astype(jnp.float32)
    )
    d_out = jnp.einsum("tke,tko->teo", own_gates, all_d_mixed, precision=HI)
    d_gate_col = jnp.einsum("teo,tko->tke", expert_out, all_d_mixed, precision=HI)
    d_first_w, d_second_w, d_first_b, d_second_b, d_rows = expert_backward(
        all_inputs, first_use, second_use, pre_one, hidden, pre_two, d_out
    )
    onehot = (jnp.arange(experts) == expert_idx).astype(jnp.float32)
    d_gate_full = (d_gate_col * onehot[None, None, :]).reshape(-1, TASKS * experts)
    d_inputs, d_gates = (
        lax.psum_scatter(
            d_rows.astype(jnp.bfloat16), "expert", scatter_dimension=0, tiled=True
        ).astype(jnp.float32),
        lax.psum_scatter(
            d_gate_full.astype(jnp.bfloat16), "expert", scatter_dimension=0, tiled=True
        ).astype(jnp.float32),
    )
    d_gates = d_gates.reshape(tokens, TASKS, experts)
    d_first_b = onehot[:, None] * d_first_b
    d_second_b = onehot[:, None] * d_second_b
    d_gate_logits = (
        (probs * (d_gates - jnp.sum(probs * d_gates, -1, keepdims=True)))
        .astype(jnp.bfloat16)
        .reshape(tokens, TASKS * experts)
    )
    d_gate_w = jnp.concatenate(
        [
            jnp.dot(inputs.T, d_gate_logits, preferred_element_type=jnp.float32),
            jnp.sum(d_gate_logits, 0, dtype=jnp.float32)[None],
        ],
        0,
    )
    d_x = d_inputs + jnp.dot(d_gate_logits, gate_low.T, preferred_element_type=jnp.float32)
    d_dense = d_x[:, FIELDS * EMB :]
    d_dense_w = jnp.concatenate(
        [jnp.dot(dense_feats.T, d_dense, precision=HI), jnp.sum(d_dense, 0)[None]], 0
    )
    d_emb = d_x[:, : FIELDS * EMB].reshape(tok_groups, GROUP_TOK * FIELDS, EMB)
    slot_grads = lax.map(lambda item: add_rows(item[0], item[1], group_slots), (local_pick, d_emb))
    slot_grads = (
        slot_grads.reshape(tok_groups, devices, sub_slots, EMB)
        .transpose(1, 0, 2, 3)
        .reshape(groups, experts, slots * EMB)
    )
    owner_grads = lax.all_to_all(
        lax.all_to_all(
            slot_grads.astype(jnp.bfloat16), "batch", split_axis=0, concat_axis=0, tiled=True
        ),
        "expert",
        split_axis=1,
        concat_axis=1,
        tiled=True,
    ).astype(slot_grads.dtype)
    owner_blocks = owner_grads.reshape(total_asked // ask_block, ask_block, EMB)

    def add_block(total, item):
        return (total + add_rows(item[0], item[1], rows_dev), None)

    table_grad, unused = lax.scan(
        add_block, jnp.zeros((rows_dev, EMB), jnp.float32), (asked_blocks, owner_blocks)
    )
    grad_first, grad_second = (
        lax.psum_scatter(
            d_first_w.astype(jnp.bfloat16), "batch", scatter_dimension=1, tiled=True
        ).astype(jnp.float32),
        lax.psum_scatter(
            d_second_w.astype(jnp.bfloat16), "batch", scatter_dimension=1, tiled=True
        ).astype(jnp.float32),
    )
    flat_grads = jnp.concatenate(
        [
            d_first_b.reshape(-1),
            d_second_b.reshape(-1),
            d_dense_w.reshape(-1),
            d_gate_w.reshape(-1),
            d_tower.reshape(-1),
            d_head.reshape(-1),
        ]
    )
    grad_small, loss = lax.psum((flat_grads, loss_local), ("batch", "expert"))
    new_table, new_table_m, new_table_v = adamw(table, table_m, table_v, table_grad, 0.3)
    new_first, new_first_m, new_first_v = adamw(first_w, first_m, first_v, grad_first, 0.15)
    new_second, new_second_m, new_second_v = adamw(second_w, second_m, second_v, grad_second, 0.15)
    new_small, new_small_m, new_small_v = adamw(small, small_m, small_v, grad_small, 0.15)
    return (
        loss,
        new_table,
        new_table_m,
        new_table_v,
        new_first,
        new_first_m,
        new_first_v,
        new_second,
        new_second_m,
        new_second_v,
        new_small,
        new_small_m,
        new_small_v,
    )


MESH = pl.DeviceIdType.MESH
BF = jnp.bfloat16
F32 = jnp.float32
NN = (((1,), (0,)), ((), ()))
NT = (((1,), (1,)), ((), ()))
KEYS = 256
CHUNK = 256
LANES = 128
ONES = 16

Sizes = collections.namedtuple(
    "Sizes",
    (
        "groups",
        "experts",
        "devices",
        "slots",
        "rows",
        "tokens",
        "first",
        "second",
        "pack",
        "span",
    ),
)


def sizes_of(mesh, tokens, slots, rows):
    groups = mesh.shape["batch"]
    experts = mesh.shape["expert"]
    first = INPUT // groups
    second = HID // groups
    span = tokens * LANES // slots
    return Sizes(
        groups,
        experts,
        groups * experts,
        slots,
        rows,
        tokens,
        first,
        second,
        first + second // 2,
        span,
    )


def fits(size):
    return (
        size.slots % LANES == 0
        and size.slots & (size.slots - 1) == 0
        and size.span == CHUNK
        and size.second % 32 == 0
        and size.first % 16 == 0
        and size.groups % 2 == 0
        and size.devices % 2 == 0
        and size.rows % KEYS == 0
        and size.experts == 4
    )


def mm(left, right, dims=NN, precision=None):
    return lax.dot_general(left, right, dims, preferred_element_type=F32, precision=precision)


def here(size):
    group = lax.axis_index("batch")
    expert = lax.axis_index("expert")
    return group, expert, group * size.experts + expert


def place(size, device):
    return (lax.div(device, size.experts), lax.rem(device, size.experts))


def greet(size, me):
    barrier = pltpu.get_barrier_semaphore()

    def one(step, carry):
        peer = lax.rem(me + step, size.devices)
        pl.semaphore_signal(barrier, inc=1, device_id=place(size, peer), device_id_type=MESH)
        return carry

    lax.fori_loop(1, size.devices, one, 0)
    return barrier


def push(source, target, sent, landed, where):
    return pltpu.make_async_remote_copy(
        src_ref=source,
        dst_ref=target,
        send_sem=sent,
        recv_sem=landed,
        device_id=where,
        device_id_type=MESH,
    )


def spread(index, extent, width):
    return lax.broadcasted_iota(jnp.int32, (extent, width), 0) == index


def as_low(flag):
    return jnp.where(flag, 1.0, 0.0).astype(BF)


def look_up(cells, key, high, levels):
    found = mm(cells, as_low(spread(key, KEYS, key.shape[1])))
    result = found[:EMB]
    for level in range(1, levels):
        result = jnp.where(high == level, found[level * EMB : (level + 1) * EMB], result)
    return result


def levels_of(values, high, levels):
    return jnp.concatenate(
        [jnp.where(high == level, values, 0.0) for level in range(levels)], 0
    ).astype(BF)


def sigmoid(value):
    return 0.5 + 0.5 * jnp.tanh(0.5 * value)


def lanes_of(rows=1):
    return lax.broadcasted_iota(jnp.int32, (rows, LANES), 1)


def turn(values, shift):
    shift = shift % LANES
    return pltpu.roll(values, shift, 1) if shift else values


def take(flat, offset, count):
    row, shift = offset // LANES, offset % LANES
    if shift == 0:
        return flat[row : row + count, :]
    return jnp.where(
        lanes_of(count) < LANES - shift,
        turn(flat[row : row + count, :], -shift),
        turn(flat[row + 1 : row + 1 + count, :], -shift),
    )


def put(flat, offset, values):
    row, shift = offset // LANES, offset % LANES
    count = values.shape[0]
    moved = turn(values, shift)
    if shift == 0:
        flat[row : row + count, :] += moved
        return
    flat[row : row + count, :] += jnp.where(lanes_of(count) >= shift, moved, 0.0)
    flat[row + 1 : row + 1 + count, :] += jnp.where(lanes_of(count) < shift, moved, 0.0)


def offsets(experts):
    sizes = [
        experts * HID,
        experts * OUT,
        (DENSE + 1) * DOUT,
        (INPUT + 1) * TASKS * experts,
        TASKS * (OUT + 1) * TOWER,
        TASKS * (TOWER + 1),
    ]
    return [sum(sizes[:index]) for index in range(len(sizes) + 1)]


def step_kernel(
    size,
    requests,
    picks,
    dense,
    labels,
    mask,
    table,
    first,
    second,
    small,
    table_grad,
    first_grad,
    second_grad,
    small_sum,
    message,
    asked,
    cells,
    rows,
    got,
    slots_out,
    slots_got,
    gathered,
    grads,
    core_got,
    core_sum,
    chip_got,
    chip_sum,
    z_got,
    vectors,
    columns,
    gate_rows,
    gate_t,
    tower_rows,
    tower_n,
    tower_t,
    dense_rows,
    dense_w,
    small_part,
    small_got,
    first_t,
    second_n,
    second_t,
    wide,
    feats,
    slot_cells,
    chosen,
    inputs,
    slope_one,
    slope_two,
    hidden,
    outs,
    mixes,
    deltas,
    d_inputs,
    slot_sum,
    sum_first,
    sum_second,
    sum_gate,
    sum_dense,
    sum_tower,
    sum_head,
    loss_sum,
    ask_sent,
    ask_landed,
    row_sent,
    row_landed,
    slot_sent,
    slot_landed,
    small_sent,
    small_landed,
    whole_sent,
    whole_landed,
    gz_sent,
    gz_landed,
    gy_sent,
    gy_landed,
    gc_sent,
    gc_landed,
    sz_sent,
    sz_landed,
    sy_sent,
    sy_landed,
    sc_sent,
    sc_landed,
):
    group, expert_here, me = here(size)
    slots, devices, experts = size.slots, size.devices, size.experts
    chips = size.groups // 2
    chip, core = lax.div(group, 2), lax.rem(group, 2)
    blocks = size.rows // KEYS
    half = size.second // 2
    levels = devices // 2
    shift = slots.bit_length() - 1
    chunks = size.tokens // CHUNK
    gates_wide = TASKS * experts
    at_one, at_two, at_dense, at_gate, at_tower, at_head, at_loss = offsets(experts)
    lane = lanes_of()
    barrier = greet(size, me)

    def own_lines(device):
        count = small_got.shape[1]
        return pl.ds(pl.multiple_of(device * count, count), count)

    def to_all(source, target, sent, landed, step, receive):
        peer = lax.rem(me + (devices - step if receive else step), devices)
        return push(
            source(peer),
            target(peer if receive else me),
            sent.at[step],
            landed.at[peer if receive else me],
            place(size, peer),
        )

    def ask(step, receive):
        return to_all(
            lambda p: message.at[p], lambda p: asked.at[p], ask_sent, ask_landed, step, receive
        )

    def answer(part, step, receive):
        peer = lax.rem(me + (step if receive else devices - step), devices)
        return push(
            rows.at[part, peer],
            got.at[part, peer if receive else me],
            row_sent.at[part, step],
            row_landed.at[part, peer if receive else me],
            place(size, peer),
        )

    def give_slots(part, step, receive):
        return to_all(
            lambda p: slots_out.at[part, p],
            lambda p: slots_got.at[part, p],
            slot_sent.at[part],
            slot_landed.at[part],
            step,
            receive,
        )

    def give_small(step, receive):
        return to_all(
            lambda p: small_part.at[own_lines(p), :],
            lambda p: small_got.at[p],
            small_sent,
            small_landed,
            step,
            receive,
        )

    def give_whole(step, receive):
        return to_all(
            lambda p: small_sum.at[own_lines(me), :],
            lambda p: small_sum.at[own_lines(p), :],
            whole_sent,
            whole_landed,
            step,
            receive,
        )

    def turned(index, count, step, receive):
        return lax.rem(index + (count - step if receive else step), count)

    def weights_z(step, receive):
        other = turned(expert_here, experts, step, receive)
        block = gathered.at[group, other if receive else expert_here]
        return push(block, block, gz_sent.at[step], gz_landed.at[step], (group, other))

    def weights_y(step, receive):
        other = turned(chip, chips, step, receive)
        block = gathered.at[(other if receive else chip) * 2 + core]
        return push(
            block, block, gy_sent.at[step], gy_landed.at[step], (other * 2 + core, expert_here)
        )

    def weights_c(step, receive):
        other = turned(chip, chips, step, True)
        block = gathered.at[other * 2 + (1 - core if receive else core)]
        return push(
            block, block, gc_sent.at[step], gc_landed.at[step], (chip * 2 + 1 - core, expert_here)
        )

    def sums_c(step):
        other = turned(chip, chips, step, False)
        return push(
            grads.at[other * 2 + 1 - core],
            core_got.at[other],
            sc_sent.at[step],
            sc_landed.at[step],
            (chip * 2 + 1 - core, expert_here),
        )

    def sums_y(step, receive):
        other = turned(chip, chips, step, receive)
        return push(
            core_sum.at[other],
            chip_got.at[step],
            sy_sent.at[step],
            sy_landed.at[step],
            (other * 2 + core, expert_here),
        )

    def sums_z(step, receive):
        other = turned(expert_here, experts, step, receive)
        return push(
            chip_sum.at[other],
            z_got.at[step],
            sz_sent.at[step],
            sz_landed.at[step],
            (group, other),
        )

    def loop(begin, end, body, unroll=1):
        def one(step, carry):
            body(step)
            return carry

        lax.fori_loop(begin, end, one, 0, unroll=unroll)

    valid = mask[...].astype(F32)
    count = jnp.where(
        lane == 0,
        jnp.sum(valid[0:1], 1, keepdims=True),
        jnp.where(lane == 1, jnp.sum(valid[1:2], 1, keepdims=True), 0.0),
    ).astype(jnp.int32)
    for part in range(size.groups):
        for one in range(experts):
            peer = part * experts + one
            message[peer, :, :slots] = requests[part, one : one + 1, :]
            message[peer, :, slots:] = count
    gathered[group, expert_here, : size.first, :] = first[...].astype(BF)
    gathered[group, expert_here, size.first :, :LANES] = second[:half].astype(BF)
    gathered[group, expert_here, size.first :, LANES:] = second[half:].astype(BF)
    for block in range(blocks):
        cells[block * EMB : (block + 1) * EMB, :] = table[
            :, block * KEYS : (block + 1) * KEYS
        ].astype(BF)
    pl.semaphore_wait(barrier, devices - 1)
    loop(1, devices, lambda step: ask(step, False).start())
    for step in range(1, experts):
        weights_z(step, False).start()

    vectors[...] = jnp.zeros_like(vectors)
    vectors[: at_dense // LANES, :] = small[: at_dense // LANES, :]
    lines = take(small, at_tower, TASKS * (OUT + 1) * TOWER // LANES)
    count_rows = lines.shape[0]
    tower_rows[pl.ds(0, count_rows, stride=2), :] = lines
    tower_rows[pl.ds(1, count_rows, stride=2), :] = turn(lines, TOWER)
    for task in range(TASKS):
        base = task * (OUT + 1)
        block = tower_rows[base : base + OUT, :]
        tower_n[task] = block[:, :TOWER].astype(BF)
        tower_t[task] = block.T[:TOWER].astype(BF)
    last = [tower_rows[k * (OUT + 1) + OUT : (k + 1) * (OUT + 1), :] for k in range(TASKS)]
    vectors[12:13, :] = jnp.where(lane < TOWER, last[0], turn(last[1], TOWER))
    heads = [take(small, at_head, 1)]
    end = at_head + TOWER + 1
    heads.append(turn(small[end // LANES : end // LANES + 1, :], -(end % LANES)))
    vectors[13:14, :] = jnp.where(lane < TOWER, heads[0], turn(heads[1], TOWER))
    vectors[15:16, :] = jnp.where(lane == 0, turn(heads[0], -TOWER), turn(heads[1], 1 - TOWER))
    per_line = LANES // gates_wide
    lines = take(small, at_gate, INPUT // per_line + 1)
    for spot in range(per_line):
        gate_rows[pl.ds(spot, lines.shape[0], stride=per_line), :] = jnp.where(
            lanes_of(lines.shape[0]) < gates_wide, turn(lines, -spot * gates_wide), 0.0
        )
    for block in range(INPUT // LANES):
        piece = gate_rows[block * LANES : (block + 1) * LANES, :]
        gate_t[:, block * LANES : (block + 1) * LANES] = piece.T[:16].astype(BF)
        wide[block * LANES : (block + 1) * LANES, experts * HID :] = piece.astype(BF)
    vectors[14:15, :] = gate_rows[INPUT : INPUT + 1, :]
    dense_rows[...] = jnp.zeros_like(dense_rows)
    for line in range(DENSE + 1):
        dense_rows[line : line + 1, :] = take(small, at_dense + line * DOUT, 1)
    dense_w[...] = dense_rows[...].T[:DOUT, :16]
    flipped = vectors[...].T
    for column in range(16):
        columns[column] = jnp.broadcast_to(flipped[:, column : column + 1], (LANES, LANES))
    feats[...] = jnp.ones_like(feats)
    feats[:DENSE, :] = dense[...]
    inputs[INPUT:, :] = jnp.ones((ONES, CHUNK), BF)
    for expert in range(experts):
        hidden[expert, HID:, :] = jnp.ones((ONES, CHUNK), BF)
    for task in range(TASKS):
        mixes[task, OUT:, :] = jnp.ones((ONES, CHUNK), BF)
    deltas[experts * HID :, :] = jnp.zeros((LANES, CHUNK), BF)
    for total in (
        sum_first,
        sum_second,
        sum_gate,
        sum_dense,
        sum_tower,
        sum_head,
        loss_sum,
        small_part,
        table_grad,
    ):
        total[...] = jnp.zeros_like(total)

    asked[me] = message[me]
    batch = 4

    def serve(part, first_round):
        columns_here = pl.ds(part * LANES, LANES)

        def some(turn_no, own):
            steps = [turn_no * batch + i for i in range(batch)]
            peers = [lax.rem(me + devices - step, devices) for step in steps]
            if first_round:
                for i, step in enumerate(steps):
                    if not (own and i == 0):
                        ask(step, True).wait_recv()
            index = jnp.concatenate([asked[peer, :, columns_here] for peer in peers], 1)
            found = look_up(cells[...], index & (KEYS - 1), index >> 8, blocks).astype(BF)
            for i, peer in enumerate(peers):
                piece = found[:, i * LANES : (i + 1) * LANES]
                if own and i == 0:
                    got[part, peer] = piece
                else:
                    rows[part, peer] = piece
                    answer(part, steps[i], False).start()

        some(0, True)
        loop(1, devices // batch, lambda turn_no: some(turn_no, False))

    serve(0, True)
    for step in range(1, experts):
        weights_z(step, True).wait_recv()
    for step in range(1, chips):
        weights_y(step, False).start()
    weights_c(0, False).start()
    total = jnp.zeros((1, LANES), jnp.int32)
    for peer in range(devices):
        total = total + asked[peer, :, slots:]
    totals = jnp.maximum(total.astype(F32), 1.0)
    for part in range(1, chunks):
        serve(part, False)
        if part == chunks - 2:
            for step in range(1, chips):
                weights_y(step, True).wait_recv()
                weights_c(step, False).start()
    for step in range(chips):
        weights_c(step, True).wait_recv()
    for expert in range(experts):
        for part in range(size.groups):
            wide[
                part * size.first : (part + 1) * size.first, expert * HID : (expert + 1) * HID
            ] = gathered[part, expert, : size.first, :]
            base = part * size.second
            second_n[expert, base : base + half, :] = gathered[part, expert, size.first :, :LANES]
            second_n[expert, base + half : base + 2 * half, :] = gathered[
                part, expert, size.first :, LANES:
            ]
        first_t[expert] = wide[:, expert * HID : (expert + 1) * HID].T
        second_t[expert] = second_n[expert].T

    def column(index, begin=0, end=LANES):
        block = columns[index, begin:end, :]
        return jnp.concatenate([block] * (CHUNK // LANES), 1)

    def chunk(step):
        here_tokens = pl.ds(pl.multiple_of(step * CHUNK, CHUNK), CHUNK)
        loop(1, devices, lambda hop: answer(step, hop, True).wait_recv())
        for owner in range(devices):
            level, lower = owner // 2, owner % 2
            slot_cells[
                level * EMB : (level + 1) * EMB, lower * LANES : (lower + 1) * LANES
            ] = got[step, owner]

        def split(field):
            index = picks[pl.ds(field, 1), here_tokens]
            owner = index >> shift
            return (owner & 1) * LANES + (index & (LANES - 1)), owner >> 1

        def pick(field):
            key, high = split(field)
            flags = as_low(spread(key, KEYS, CHUNK))
            chosen[field] = flags
            found = mm(slot_cells[...], flags)
            result = found[:EMB]
            for level in range(1, levels):
                result = jnp.where(high == level, found[level * EMB : (level + 1) * EMB], result)
            inputs[pl.ds(pl.multiple_of(field * EMB, EMB), EMB), :] = result.astype(BF)

        loop(0, FIELDS, pick, 13)
        inputs[FIELDS * EMB : INPUT, :] = mm(
            dense_w[...], feats[:, here_tokens], precision=HI
        ).astype(BF)
        x = inputs[:INPUT, :]
        logits = mm(gate_t[...], x)[:gates_wide] + column(14, 0, gates_wide)
        probs, gates = [], []
        for task in range(TASKS):
            line = [logits[task * experts + e : task * experts + e + 1] for e in range(experts)]
            top = functools.reduce(jnp.maximum, line)
            powers = [jnp.exp(item - top) for item in line]
            whole = 1.0 / functools.reduce(jnp.add, powers)
            probs.append([item * whole for item in powers])
            gates.append([item.astype(BF).astype(F32) for item in probs[-1]])
        mixed = [None] * TASKS
        for expert in range(experts):
            pre = mm(first_t[expert], x) + jnp.concatenate(
                [column(2 * expert), column(2 * expert + 1)], 0
            )
            sig = sigmoid(pre)
            act = pre * sig
            slope_one[expert] = sig + act * (1.0 - sig)
            hidden[expert, :HID, :] = act.astype(BF)
            pre = mm(second_t[expert], hidden[expert, :HID, :]) + column(8 + expert)
            sig = sigmoid(pre)
            act = pre * sig
            slope_two[expert] = sig + act * (1.0 - sig)
            outs[expert] = act
            for task in range(TASKS):
                term = gates[task][expert] * act
                mixed[task] = term if mixed[task] is None else mixed[task] + term
        d_mixed = []
        for task in range(TASKS):
            mixes[task, :OUT, :] = mixed[task].astype(BF)
            low, high = task * TOWER, (task + 1) * TOWER
            pre = mm(tower_t[task], mixes[task, :OUT, :]) + column(12, low, high)
            sig = sigmoid(pre)
            act = pre * sig
            head = column(13, low, high)
            logit = jnp.sum(act * head, 0, keepdims=True) + column(15, task, task + 1)
            scale = mask[task : task + 1, here_tokens].astype(F32) / totals[:, task : task + 1]
            target = labels[task : task + 1, here_tokens].astype(F32)
            soft = jnp.maximum(logit, 0.0) + jnp.log(1.0 + jnp.exp(-jnp.abs(logit)))
            loss_sum[...] += scale * (soft - target * logit)
            d_logit = scale * (sigmoid(logit) - target)
            d_pre = ((sig + act * (1.0 - sig)) * (d_logit * head)).astype(BF)
            sum_head[task] += mm(
                jnp.broadcast_to(d_logit, (8, CHUNK)),
                jnp.concatenate(
                    [act, jnp.ones((8, CHUNK), F32), jnp.zeros((LANES - TOWER - 8, CHUNK), F32)], 0
                ),
                NT,
                HI,
            )
            sum_tower[task] += mm(mixes[task], d_pre, NT)
            d_mixed.append(mm(tower_n[task], d_pre).astype(BF).astype(F32))
        d_gates = [[None] * experts for task in range(TASKS)]
        for expert in range(experts):
            d_out = gates[0][expert] * d_mixed[0] + gates[1][expert] * d_mixed[1]
            for task in range(TASKS):
                d_gates[task][expert] = jnp.sum(outs[expert] * d_mixed[task], 0, keepdims=True)
            d_two = (slope_two[expert] * d_out).astype(BF)
            sum_second[expert] += mm(hidden[expert], d_two, NT)
            d_one = (slope_one[expert] * mm(second_n[expert], d_two)).astype(BF)
            deltas[expert * HID : (expert + 1) * HID, :] = d_one
            sum_first[expert] += mm(inputs[...], d_one, NT)
        lines = []
        for task in range(TASKS):
            inner = functools.reduce(
                jnp.add, [probs[task][e] * d_gates[task][e] for e in range(experts)]
            )
            lines += [probs[task][e] * (d_gates[task][e] - inner) for e in range(experts)]
        lines.append(jnp.zeros((16 - gates_wide, CHUNK), F32))
        deltas[experts * HID : experts * HID + 16, :] = jnp.concatenate(lines, 0).astype(BF)
        sum_gate[...] += mm(inputs[...], deltas[experts * HID :, :], NT)
        d_inputs[...] = mm(wide[...], deltas[...])
        sum_dense[...] += mm(feats[:, here_tokens], d_inputs[INPUT - LANES :, :], NT, HI)
        slot_sum[...] = jnp.zeros_like(slot_sum)

        def give(field):
            key, high = split(field)
            values = d_inputs[pl.ds(pl.multiple_of(field * EMB, EMB), EMB), :]
            slot_sum[...] += mm(levels_of(values, high, levels), chosen[field], NT)

        loop(0, FIELDS, give, 13)
        for owner in range(devices):
            level, lower = owner // 2, owner % 2
            slots_out[step, owner] = slot_sum[
                level * EMB : (level + 1) * EMB, lower * LANES : (lower + 1) * LANES
            ].astype(BF)
        loop(1, devices, lambda hop: give_slots(step, hop, False).start())
        slots_got[step, me] = slots_out[step, me]

    loop(0, chunks, chunk)

    for part in range(size.groups):
        base = part * size.second
        for expert in range(experts):
            grads[part, expert, : size.first, :] = sum_first[
                expert, part * size.first : (part + 1) * size.first, :
            ].astype(BF)
            grads[part, expert, size.first :, :LANES] = sum_second[
                expert, base : base + half, :
            ].astype(BF)
            grads[part, expert, size.first :, LANES:] = sum_second[
                expert, base + half : base + 2 * half, :
            ].astype(BF)
    for step in range(1, chips + 1):
        sums_c(step % chips).start()
    for expert in range(experts):
        per = HID // LANES
        for piece in range(per):
            line = expert * per + piece
            small_part[line : line + 1, :] = sum_first[
                expert, INPUT : INPUT + 1, piece * LANES : (piece + 1) * LANES
            ]
        line = experts * per + expert
        small_part[line : line + 1, :] = sum_second[expert, HID : HID + 1, :]
    for line in range(DENSE + 1):
        values = jnp.where(lane < DOUT, turn(sum_dense[line : line + 1, :], DOUT - LANES), 0.0)
        put(small_part, at_dense + line * DOUT, values)
    lines = INPUT // per_line + 1
    packed = jnp.zeros((lines, LANES), F32)
    for spot in range(per_line):
        packed = packed + turn(sum_gate[pl.ds(spot, lines, stride=per_line), :], spot * gates_wide)
    inside = lax.broadcasted_iota(jnp.int32, (lines, LANES), 0) < lines - 1
    put(
        small_part,
        at_gate,
        jnp.where(inside | (lanes_of(lines) < gates_wide), packed, 0.0),
    )
    tower_rows[...] = jnp.zeros_like(tower_rows)
    for task in range(TASKS):
        base = task * (OUT + 1)
        tower_rows[base : base + OUT + 1, :TOWER] = sum_tower[task, : OUT + 1, :]
    put(
        small_part,
        at_tower,
        tower_rows[pl.ds(0, count_rows, stride=2), :]
        + turn(tower_rows[pl.ds(1, count_rows, stride=2), :], TOWER),
    )
    for task in range(TASKS):
        put(
            small_part,
            at_head + task * (TOWER + 1),
            jnp.where(lane < TOWER + 1, sum_head[task, 0:1, :], 0.0),
        )
    whole_loss = jnp.sum(loss_sum[...], 1, keepdims=True)
    put(small_part, at_loss, jnp.where(lane == 0, whole_loss, 0.0))
    loop(1, devices, lambda step: give_small(step, False).start())

    def collect(part):
        columns_here = pl.ds(part * LANES, LANES)

        def some(turn_no, own):
            steps = [turn_no * batch + i for i in range(batch)]
            peers = [lax.rem(me + devices - step, devices) for step in steps]
            for i, step in enumerate(steps):
                if not (own and i == 0):
                    give_slots(part, step, True).wait_recv()
            index = jnp.concatenate([asked[peer, :, columns_here] for peer in peers], 1)
            values = jnp.concatenate([slots_got[part, peer] for peer in peers], 1).astype(F32)
            spots = as_low(spread(index & (KEYS - 1), KEYS, batch * LANES))
            table_grad[...] += mm(levels_of(values, index >> 8, blocks), spots, NT)

        some(0, True)
        loop(1, devices // batch, lambda turn_no: some(turn_no, False), devices // batch - 1)

    collect(0)
    for step in range(1, chips + 1):
        other = turned(chip, chips, step % chips, False)
        sums_c(step % chips).wait_recv()
        core_sum[other] = (
            grads[other * 2 + core].astype(F32) + core_got[other].astype(F32)
        ).astype(BF)
        if step < chips:
            sums_y(step, False).start()
    collect(1)
    small_got[me] = small_part[own_lines(me), :]

    def add_small(step, total):
        give_small(step, True).wait_recv()
        return total + small_got[lax.rem(me + devices - step, devices)]

    small_sum[own_lines(me), :] = lax.fori_loop(1, devices, add_small, small_got[me])
    loop(1, devices, lambda step: give_whole(step, False).start())
    collect(2)
    total = core_sum[chip].astype(F32)
    for step in range(1, chips):
        sums_y(step, True).wait_recv()
        total = total + chip_got[step].astype(F32)
    chip_sum[...] = total.astype(BF)
    for step in range(1, experts):
        sums_z(step, False).start()
    for part in range(3, chunks):
        collect(part)
    total = chip_sum[expert_here].astype(F32)
    for step in range(1, experts):
        sums_z(step, True).wait_recv()
        total = total + z_got[step].astype(F32)
    first_grad[...] = total[: size.first]
    second_grad[:half, :] = total[size.first :, :LANES]
    second_grad[half:, :] = total[size.first :, LANES:]

    def finish(step):
        give_whole(step, True).wait_recv()
        ask(step, False).wait_send()
        for part in range(chunks):
            answer(part, step, False).wait_send()
            give_slots(part, step, False).wait_send()
        give_small(step, False).wait_send()
        give_whole(step, False).wait_send()

    loop(1, devices, finish)
    for step in range(chips):
        weights_c(step, False).wait_send()
        sums_c(step).wait_send()
    for step in range(1, chips):
        weights_y(step, False).wait_send()
        sums_y(step, False).wait_send()
    for step in range(1, experts):
        weights_z(step, False).wait_send()
        sums_z(step, False).wait_send()


def update(size, *refs):
    grads, state, results = refs[:3], refs[3:12], refs[12:]
    table_grad = grads[0][...]
    wide = jnp.concatenate(
        [table_grad[b * EMB : (b + 1) * EMB] for b in range(size.rows // KEYS)], 1
    )
    for index, grad in enumerate((wide, grads[1][...], grads[2][...])):
        rate = 0.3 if index == 0 else 0.15
        values = [ref[...] for ref in state[3 * index : 3 * index + 3]]
        for ref, value in zip(results[3 * index : 3 * index + 3], adamw(*values, grad, rate)):
            ref[...] = value


def shape(dims, dtype=F32):
    return jax.ShapeDtypeStruct(dims, dtype)


def call(kernel, outs, scratch, remote=None):
    vmem = pl.BlockSpec(memory_space=pltpu.VMEM)
    params = dict(vmem_limit_bytes=56 * 2**20)
    if remote is not None:
        params.update(collective_id=remote, has_side_effects=True)
    return lambda *args: pl.pallas_call(
        kernel,
        out_shape=outs,
        in_specs=[vmem] * len(args),
        out_specs=[vmem] * len(outs),
        scratch_shapes=scratch,
        compiler_params=pltpu.CompilerParams(**params),
    )(*args)


def local(
    size,
    dense_feats,
    picks,
    labels,
    label_mask,
    requests,
    table,
    table_m,
    table_v,
    first_w,
    first_m,
    first_v,
    second_w,
    second_m,
    second_v,
    small,
    small_m,
    small_v,
):
    devices, experts, groups = size.devices, size.experts, size.groups
    chips = groups // 2
    chunks = size.tokens // CHUNK
    dma = pltpu.SemaphoreType.DMA
    vm = pltpu.VMEM
    message = size.slots + LANES
    count = small.shape[0]
    lines = -(-(count + 1) // (devices * 8 * LANES)) * 8
    flat_lines = -(-count // LANES)
    exchange = vm((chunks, devices, EMB, LANES), BF)
    weights = vm((groups, experts, size.pack, HID), BF)
    of_chips = vm((chips, experts, size.pack, HID), BF)
    of_chip = vm((experts, size.pack, HID), BF)
    table_grad, first_grad, second_grad, flat = call(
        functools.partial(step_kernel, size),
        [
            shape((size.rows // KEYS * EMB, KEYS)),
            shape((size.first, HID)),
            shape((size.second, OUT)),
            shape((devices * lines, LANES)),
        ],
        [
            vm((devices, 1, message), jnp.int32),
            vm((devices, 1, message), jnp.int32),
            vm((size.rows // KEYS * EMB, KEYS), BF),
        ]
        + [exchange] * 4
        + [weights, weights, of_chips, of_chips, of_chips, of_chip, of_chip]
        + [
            vm((LANES, LANES), F32),
            vm((16, LANES, LANES), F32),
            vm((INPUT + ONES, LANES), F32),
            vm((16, INPUT), BF),
            vm((TASKS * (OUT + 1) + 6, LANES), F32),
            vm((TASKS, OUT, TOWER), BF),
            vm((TASKS, TOWER, OUT), BF),
            vm((LANES, LANES), F32),
            vm((DOUT, 16), F32),
            vm((devices * lines, LANES), F32),
            vm((devices, lines, LANES), F32),
            vm((experts, HID, INPUT), BF),
            vm((experts, HID, OUT), BF),
            vm((experts, OUT, HID), BF),
            vm((INPUT, experts * HID + LANES), BF),
            vm((16, size.tokens), F32),
            vm((devices // 2 * EMB, KEYS), BF),
            vm((FIELDS, KEYS, CHUNK), BF),
            vm((INPUT + ONES, CHUNK), BF),
            vm((experts, HID, CHUNK), F32),
            vm((experts, OUT, CHUNK), F32),
            vm((experts, HID + ONES, CHUNK), BF),
            vm((experts, OUT, CHUNK), F32),
            vm((TASKS, OUT + ONES, CHUNK), BF),
            vm((experts * HID + LANES, CHUNK), BF),
            vm((INPUT, CHUNK), F32),
            vm((devices // 2 * EMB, KEYS), F32),
            vm((experts, INPUT + ONES, HID), F32),
            vm((experts, HID + ONES, OUT), F32),
            vm((INPUT + ONES, LANES), F32),
            vm((16, LANES), F32),
            vm((TASKS, OUT + ONES, TOWER), F32),
            vm((TASKS, 8, LANES), F32),
            vm((1, CHUNK), F32),
        ]
        + [dma((devices,))] * 2
        + [dma((chunks, devices))] * 4
        + [dma((devices,))] * 4
        + [dma((experts,))] * 2
        + [dma((chips,))] * 4
        + [dma((experts,))] * 2
        + [dma((chips,))] * 4,
        0,
    )(
        requests[0],
        picks.T,
        dense_feats.T,
        labels.T,
        label_mask.T,
        table.T,
        first_w[0],
        second_w[0],
        jnp.pad(small, (0, flat_lines * LANES - count)).reshape(flat_lines, LANES),
    )
    tables = (table.T, table_m.T, table_v.T)
    firsts = (first_w[0], first_m[0], first_v[0])
    seconds = (second_w[0], second_m[0], second_v[0])
    new = call(
        functools.partial(update, size),
        [shape(a.shape) for a in tables + firsts + seconds],
        [],
    )(table_grad, first_grad, second_grad, *tables, *firsts, *seconds)
    flat = flat.reshape(-1)
    new_small = adamw(small, small_m, small_v, flat[:count], 0.15)
    return (
        (flat[count],)
        + tuple(a.T for a in new[:3])
        + tuple(a[None] for a in new[3:])
        + tuple(new_small)
    )


def solution(mesh):
    both = P(("batch", "expert"), None)
    shard = P("expert", "batch", None)
    ins = (both,) * 4 + (P(("batch", "expert"), None, None, None),) + (both,) * 3
    ins = ins + (shard,) * 6 + (P(),) * 3

    def step(*args):
        devices = mesh.shape["batch"] * mesh.shape["expert"]
        size = sizes_of(
            mesh, args[0].shape[0] // devices, args[4].shape[-1], args[5].shape[0] // devices
        )
        return jax.shard_map(
            functools.partial(local, size) if fits(size) else plain,
            mesh=mesh,
            in_specs=ins,
            out_specs=(P(),) + (both,) * 3 + (shard,) * 6 + (P(),) * 3,
            check_vma=False,
        )(*args)

    return step
```

```python
import collections
import functools

import jax
import jax.numpy as jnp
from jax import lax
from jax.experimental import pallas as pl
from jax.experimental.pallas import tpu as pltpu
from jax.sharding import PartitionSpec as P

FIELDS = 26
EMB = 16
DENSE = 13
DOUT = 96
HID = 256
OUT = 128
TOWER = 64
TASKS = 2
STEP = 5
GROUP_TOK = 64
INPUT = 512


HI = lax.Precision.HIGHEST


def unpack(flat, experts):
    shapes = [
        (experts, HID),
        (experts, OUT),
        (DENSE + 1, DOUT),
        (INPUT + 1, TASKS * experts),
        (TASKS, OUT + 1, TOWER),
        (TASKS, TOWER + 1),
    ]
    parts = []
    offset = 0
    for shape in shapes:
        length = 1
        for extent in shape:
            length = length * extent
        parts.append(flat[offset : offset + length].reshape(shape))
        offset = offset + length
    return parts


def adamw(weight, first, second, grad, rate):
    first = 0.9 * first + 0.1 * grad
    second = 0.999 * second + 0.001 * grad * grad
    fix_one = 1.0 - 0.9**STEP
    fix_two = 1.0 - 0.999**STEP
    weight = weight - rate * (
        first / fix_one / (jnp.sqrt(second / fix_two) + 1e-08) + 0.01 * weight
    )
    return (weight, first, second)


def silu_slope(value):
    sig = jax.nn.sigmoid(value)
    return sig * (1.0 + value * (1.0 - sig))


def split_three(values):
    upper = values.astype(jnp.bfloat16)
    rest = values - upper.astype(jnp.float32)
    middle = rest.astype(jnp.bfloat16)
    lower_part = (rest - middle.astype(jnp.float32)).astype(jnp.bfloat16)
    return jnp.concatenate([upper, middle, lower_part], -1)


def join_three(values):
    return values[:, :EMB] + values[:, EMB : 2 * EMB] + values[:, 2 * EMB :]


def one_hot(index, extent):
    return (index[:, None] == jnp.arange(extent, dtype=jnp.int32)[None, :]).astype(jnp.bfloat16)


def pick_rows(index, source):
    return jnp.dot(
        one_hot(index, source.shape[0]), source, preferred_element_type=jnp.float32
    ).astype(jnp.bfloat16)


def add_rows(index, values, extent):
    spread = lax.dot_general(
        one_hot(index, extent),
        split_three(values),
        (((0,), (0,)), ((), ())),
        preferred_element_type=jnp.float32,
    )
    return join_three(spread)


def expert_forward(inputs, first_w, second_w, first_b, second_b):
    pre_one = (
        jnp.einsum("ti,eih->teh", inputs, first_w, preferred_element_type=jnp.float32)
        + first_b[None]
    )
    hidden = jax.nn.silu(pre_one).astype(jnp.bfloat16)
    pre_two = (
        jnp.einsum("teh,eho->teo", hidden, second_w, preferred_element_type=jnp.float32)
        + second_b[None]
    )
    return (pre_one, hidden, pre_two, jax.nn.silu(pre_two))


def expert_backward(inputs, first_w, second_w, pre_one, hidden, pre_two, d_out):
    d_two = (silu_slope(pre_two) * d_out).astype(jnp.bfloat16)
    d_second_w = jnp.einsum("teh,teo->eho", hidden, d_two, preferred_element_type=jnp.float32)
    d_second_b = jnp.sum(d_two, 0, dtype=jnp.float32)
    d_hidden = jnp.einsum("teo,eho->teh", d_two, second_w, preferred_element_type=jnp.float32)
    d_one = (silu_slope(pre_one) * d_hidden).astype(jnp.bfloat16)
    d_first_w = jnp.einsum("ti,teh->eih", inputs, d_one, preferred_element_type=jnp.float32)
    d_first_b = jnp.sum(d_one, 0, dtype=jnp.float32)
    d_inputs = jnp.einsum("teh,eih->ti", d_one, first_w, preferred_element_type=jnp.float32)
    return (d_first_w, d_second_w, d_first_b, d_second_b, d_inputs)


def plain(
    dense_feats,
    picks,
    labels,
    label_mask,
    requests,
    table,
    table_m,
    table_v,
    first_w,
    first_m,
    first_v,
    second_w,
    second_m,
    second_v,
    small,
    small_m,
    small_v,
):
    groups = lax.axis_size("batch")
    experts = lax.axis_size("expert")
    devices = groups * experts
    expert_idx = lax.axis_index("expert")
    tokens = dense_feats.shape[0]
    slots = requests.shape[-1]
    rows_dev = table.shape[0]
    tok_groups = tokens // GROUP_TOK
    sub_slots = slots // tok_groups
    group_slots = devices * sub_slots
    total_asked = devices * slots
    ask_block = min(1024, total_asked)
    bias_one, bias_two, dense_w, gate_w, tower_w, head_w = unpack(small, experts)
    first_full, second_full = (
        lax.all_gather(first_w.astype(jnp.bfloat16), "batch", axis=1, tiled=True),
        lax.all_gather(second_w.astype(jnp.bfloat16), "batch", axis=1, tiled=True),
    )
    asked = lax.all_to_all(
        lax.all_to_all(requests[0], "batch", split_axis=0, concat_axis=0, tiled=True),
        "expert",
        split_axis=1,
        concat_axis=1,
        tiled=True,
    )
    asked_blocks = asked.reshape(total_asked // ask_block, ask_block)
    table_low = table.astype(jnp.bfloat16)
    sent_rows = lax.map(lambda index: pick_rows(index, table_low), asked_blocks)
    sent_rows = sent_rows.reshape(groups, experts, slots * EMB)
    got_rows = lax.all_to_all(
        lax.all_to_all(sent_rows, "batch", split_axis=0, concat_axis=0, tiled=True),
        "expert",
        split_axis=1,
        concat_axis=1,
        tiled=True,
    )
    by_group = (
        got_rows.reshape(devices, tok_groups, sub_slots, EMB)
        .transpose(1, 0, 2, 3)
        .reshape(tok_groups, group_slots, EMB)
    )
    local_pick = (picks // slots * sub_slots + picks % sub_slots).reshape(
        tok_groups, GROUP_TOK * FIELDS
    )
    emb = lax.map(lambda item: pick_rows(item[0], item[1]), (local_pick, by_group)).reshape(
        tokens, FIELDS * EMB
    )
    dense_proj = jnp.dot(dense_feats, dense_w[:DENSE], precision=HI) + dense_w[DENSE]
    inputs = jnp.concatenate([emb, dense_proj.astype(jnp.bfloat16)], 1)
    gate_low = gate_w[:INPUT].astype(jnp.bfloat16)
    gate_logits = jnp.dot(inputs, gate_low, preferred_element_type=jnp.float32) + gate_w[INPUT]
    probs = jax.nn.softmax(gate_logits.reshape(tokens, TASKS, experts), axis=-1)
    gates = probs.astype(jnp.bfloat16)
    all_inputs, all_gates = (
        lax.all_gather(inputs, "expert", axis=0, tiled=True),
        lax.all_gather(gates.reshape(tokens, TASKS * experts), "expert", axis=0, tiled=True),
    )
    own_gates = lax.dynamic_slice_in_dim(
        all_gates.reshape(-1, TASKS, experts), expert_idx, 1, 2
    ).astype(jnp.float32)
    first_use, second_use = (first_full, second_full)
    first_b = lax.dynamic_slice_in_dim(bias_one, expert_idx, 1, 0)
    second_b = lax.dynamic_slice_in_dim(bias_two, expert_idx, 1, 0)
    pre_one, hidden, pre_two, expert_out = expert_forward(
        all_inputs, first_use, second_use, first_b, second_b
    )
    terms = jnp.einsum("tke,teo->tko", own_gates, expert_out, precision=HI).reshape(-1, TASKS * OUT)
    mixed = lax.psum_scatter(terms.astype(jnp.bfloat16), "expert", scatter_dimension=0, tiled=True)
    mask = label_mask.astype(jnp.float32)
    target = labels.astype(jnp.float32)
    counts = jnp.maximum(lax.psum(jnp.sum(mask, 0), ("batch", "expert")), 1.0)
    mixed_low = mixed.reshape(tokens, TASKS, OUT)
    tower_low = tower_w[:, :OUT].astype(jnp.bfloat16)
    tower_pre = (
        jnp.einsum("tko,koh->tkh", mixed_low, tower_low, preferred_element_type=jnp.float32)
        + tower_w[:, OUT][None]
    )
    tower_act = jax.nn.silu(tower_pre)
    logits = jnp.einsum("tkh,kh->tk", tower_act, head_w[:, :TOWER], precision=HI) + head_w[:, TOWER]
    loss_local = jnp.sum(mask * (jax.nn.softplus(logits) - target * logits) / counts)
    d_logits = mask * (jax.nn.sigmoid(logits) - target) / counts
    d_head = jnp.concatenate(
        [
            jnp.einsum("tkh,tk->kh", tower_act, d_logits, precision=HI),
            jnp.sum(d_logits, 0)[:, None],
        ],
        1,
    )
    d_act = d_logits[:, :, None] * head_w[None, :, :TOWER]
    d_tower_pre = (silu_slope(tower_pre) * d_act).astype(jnp.bfloat16)
    d_tower = jnp.concatenate(
        [
            jnp.einsum("tko,tkh->koh", mixed_low, d_tower_pre, preferred_element_type=jnp.float32),
            jnp.sum(d_tower_pre, 0, dtype=jnp.float32)[:, None, :],
        ],
        1,
    )
    d_mixed = jnp.einsum(
        "tkh,koh->tko", d_tower_pre, tower_low, preferred_element_type=jnp.float32
    ).astype(jnp.bfloat16)
    all_d_mixed = (
        lax.all_gather(d_mixed.reshape(tokens, TASKS * OUT), "expert", axis=0, tiled=True)
        .reshape(-1, TASKS, OUT)
        .astype(jnp.float32)
    )
    d_out = jnp.einsum("tke,tko->teo", own_gates, all_d_mixed, precision=HI)
    d_gate_col = jnp.einsum("teo,tko->tke", expert_out, all_d_mixed, precision=HI)
    d_first_w, d_second_w, d_first_b, d_second_b, d_rows = expert_backward(
        all_inputs, first_use, second_use, pre_one, hidden, pre_two, d_out
    )
    onehot = (jnp.arange(experts) == expert_idx).astype(jnp.float32)
    d_gate_full = (d_gate_col * onehot[None, None, :]).reshape(-1, TASKS * experts)
    d_inputs, d_gates = (
        lax.psum_scatter(
            d_rows.astype(jnp.bfloat16), "expert", scatter_dimension=0, tiled=True
        ).astype(jnp.float32),
        lax.psum_scatter(
            d_gate_full.astype(jnp.bfloat16), "expert", scatter_dimension=0, tiled=True
        ).astype(jnp.float32),
    )
    d_gates = d_gates.reshape(tokens, TASKS, experts)
    d_first_b = onehot[:, None] * d_first_b
    d_second_b = onehot[:, None] * d_second_b
    d_gate_logits = (
        (probs * (d_gates - jnp.sum(probs * d_gates, -1, keepdims=True)))
        .astype(jnp.bfloat16)
        .reshape(tokens, TASKS * experts)
    )
    d_gate_w = jnp.concatenate(
        [
            jnp.dot(inputs.T, d_gate_logits, preferred_element_type=jnp.float32),
            jnp.sum(d_gate_logits, 0, dtype=jnp.float32)[None],
        ],
        0,
    )
    d_x = d_inputs + jnp.dot(d_gate_logits, gate_low.T, preferred_element_type=jnp.float32)
    d_dense = d_x[:, FIELDS * EMB :]
    d_dense_w = jnp.concatenate(
        [jnp.dot(dense_feats.T, d_dense, precision=HI), jnp.sum(d_dense, 0)[None]], 0
    )
    d_emb = d_x[:, : FIELDS * EMB].reshape(tok_groups, GROUP_TOK * FIELDS, EMB)
    slot_grads = lax.map(lambda item: add_rows(item[0], item[1], group_slots), (local_pick, d_emb))
    slot_grads = (
        slot_grads.reshape(tok_groups, devices, sub_slots, EMB)
        .transpose(1, 0, 2, 3)
        .reshape(groups, experts, slots * EMB)
    )
    owner_grads = lax.all_to_all(
        lax.all_to_all(
            slot_grads.astype(jnp.bfloat16), "batch", split_axis=0, concat_axis=0, tiled=True
        ),
        "expert",
        split_axis=1,
        concat_axis=1,
        tiled=True,
    ).astype(slot_grads.dtype)
    owner_blocks = owner_grads.reshape(total_asked // ask_block, ask_block, EMB)

    def add_block(total, item):
        return (total + add_rows(item[0], item[1], rows_dev), None)

    table_grad, unused = lax.scan(
        add_block, jnp.zeros((rows_dev, EMB), jnp.float32), (asked_blocks, owner_blocks)
    )
    grad_first, grad_second = (
        lax.psum_scatter(
            d_first_w.astype(jnp.bfloat16), "batch", scatter_dimension=1, tiled=True
        ).astype(jnp.float32),
        lax.psum_scatter(
            d_second_w.astype(jnp.bfloat16), "batch", scatter_dimension=1, tiled=True
        ).astype(jnp.float32),
    )
    flat_grads = jnp.concatenate(
        [
            d_first_b.reshape(-1),
            d_second_b.reshape(-1),
            d_dense_w.reshape(-1),
            d_gate_w.reshape(-1),
            d_tower.reshape(-1),
            d_head.reshape(-1),
        ]
    )
    grad_small, loss = lax.psum((flat_grads, loss_local), ("batch", "expert"))
    new_table, new_table_m, new_table_v = adamw(table, table_m, table_v, table_grad, 0.3)
    new_first, new_first_m, new_first_v = adamw(first_w, first_m, first_v, grad_first, 0.15)
    new_second, new_second_m, new_second_v = adamw(second_w, second_m, second_v, grad_second, 0.15)
    new_small, new_small_m, new_small_v = adamw(small, small_m, small_v, grad_small, 0.15)
    return (
        loss,
        new_table,
        new_table_m,
        new_table_v,
        new_first,
        new_first_m,
        new_first_v,
        new_second,
        new_second_m,
        new_second_v,
        new_small,
        new_small_m,
        new_small_v,
    )


MESH = pl.DeviceIdType.MESH
BF = jnp.bfloat16
F32 = jnp.float32
NN = (((1,), (0,)), ((), ()))
NT = (((1,), (1,)), ((), ()))
KEYS = 256
CHUNK = 256
LANES = 128
ONES = 16

Sizes = collections.namedtuple(
    "Sizes",
    (
        "groups",
        "experts",
        "devices",
        "slots",
        "rows",
        "tokens",
        "first",
        "second",
        "pack",
        "span",
    ),
)


def sizes_of(mesh, tokens, slots, rows):
    groups = mesh.shape["batch"]
    experts = mesh.shape["expert"]
    first = INPUT // groups
    second = HID // groups
    span = tokens * LANES // slots
    return Sizes(
        groups,
        experts,
        groups * experts,
        slots,
        rows,
        tokens,
        first,
        second,
        first + second // 2,
        span,
    )


def fits(size):
    return (
        size.slots % LANES == 0
        and size.slots & (size.slots - 1) == 0
        and size.span == CHUNK
        and size.second % 32 == 0
        and size.first % 16 == 0
        and size.groups % 2 == 0
        and size.devices % 2 == 0
        and size.rows % KEYS == 0
        and size.experts == 4
    )


def mm(left, right, dims=NN, precision=None):
    return lax.dot_general(left, right, dims, preferred_element_type=F32, precision=precision)


def here(size):
    group = lax.axis_index("batch")
    expert = lax.axis_index("expert")
    return group, expert, group * size.experts + expert


def place(size, device):
    return (lax.div(device, size.experts), lax.rem(device, size.experts))


def greet(size, me):
    barrier = pltpu.get_barrier_semaphore()

    def one(step, carry):
        peer = lax.rem(me + step, size.devices)
        pl.semaphore_signal(barrier, inc=1, device_id=place(size, peer), device_id_type=MESH)
        return carry

    lax.fori_loop(1, size.devices, one, 0)
    return barrier


def push(source, target, sent, landed, where):
    return pltpu.make_async_remote_copy(
        src_ref=source,
        dst_ref=target,
        send_sem=sent,
        recv_sem=landed,
        device_id=where,
        device_id_type=MESH,
    )


def spread(index, extent, width):
    return lax.broadcasted_iota(jnp.int32, (extent, width), 0) == index


def as_low(flag):
    return jnp.where(flag, 1.0, 0.0).astype(BF)


def look_up(cells, key, high, levels):
    found = mm(cells, as_low(spread(key, KEYS, key.shape[1])))
    result = found[:EMB]
    for level in range(1, levels):
        result = jnp.where(high == level, found[level * EMB : (level + 1) * EMB], result)
    return result


def levels_of(values, high, levels):
    return jnp.concatenate(
        [jnp.where(high == level, values, 0.0) for level in range(levels)], 0
    ).astype(BF)


def sigmoid(value):
    return 0.5 + 0.5 * jnp.tanh(0.5 * value)


def lanes_of(rows=1):
    return lax.broadcasted_iota(jnp.int32, (rows, LANES), 1)


def turn(values, shift):
    shift = shift % LANES
    return pltpu.roll(values, shift, 1) if shift else values


def take(flat, offset, count):
    row, shift = offset // LANES, offset % LANES
    if shift == 0:
        return flat[row : row + count, :]
    return jnp.where(
        lanes_of(count) < LANES - shift,
        turn(flat[row : row + count, :], -shift),
        turn(flat[row + 1 : row + 1 + count, :], -shift),
    )


def put(flat, offset, values):
    row, shift = offset // LANES, offset % LANES
    count = values.shape[0]
    moved = turn(values, shift)
    if shift == 0:
        flat[row : row + count, :] += moved
        return
    flat[row : row + count, :] += jnp.where(lanes_of(count) >= shift, moved, 0.0)
    flat[row + 1 : row + 1 + count, :] += jnp.where(lanes_of(count) < shift, moved, 0.0)


def offsets(experts):
    sizes = [
        experts * HID,
        experts * OUT,
        (DENSE + 1) * DOUT,
        (INPUT + 1) * TASKS * experts,
        TASKS * (OUT + 1) * TOWER,
        TASKS * (TOWER + 1),
    ]
    return [sum(sizes[:index]) for index in range(len(sizes) + 1)]


def step_kernel(
    size,
    requests,
    picks,
    dense,
    labels,
    mask,
    table,
    first,
    second,
    small,
    table_grad,
    first_grad,
    second_grad,
    small_sum,
    message,
    asked,
    cells,
    rows,
    got,
    slots_out,
    slots_got,
    gathered,
    grads,
    core_got,
    core_sum,
    chip_got,
    chip_sum,
    z_got,
    vectors,
    columns,
    gate_rows,
    gate_t,
    tower_rows,
    tower_n,
    tower_t,
    dense_rows,
    dense_w,
    small_part,
    small_got,
    first_t,
    second_n,
    second_t,
    wide,
    feats,
    slot_cells,
    chosen,
    inputs,
    slope_one,
    slope_two,
    hidden,
    outs,
    mixes,
    deltas,
    d_inputs,
    slot_sum,
    sum_first,
    sum_second,
    sum_gate,
    sum_dense,
    sum_tower,
    sum_head,
    loss_sum,
    ask_sent,
    ask_landed,
    row_sent,
    row_landed,
    slot_sent,
    slot_landed,
    small_sent,
    small_landed,
    whole_sent,
    whole_landed,
    gz_sent,
    gz_landed,
    gy_sent,
    gy_landed,
    gc_sent,
    gc_landed,
    sz_sent,
    sz_landed,
    sy_sent,
    sy_landed,
    sc_sent,
    sc_landed,
):
    group, expert_here, me = here(size)
    slots, devices, experts = size.slots, size.devices, size.experts
    chips = size.groups // 2
    chip, core = lax.div(group, 2), lax.rem(group, 2)
    blocks = size.rows // KEYS
    half = size.second // 2
    levels = devices // 2
    shift = slots.bit_length() - 1
    chunks = size.tokens // CHUNK
    gates_wide = TASKS * experts
    at_one, at_two, at_dense, at_gate, at_tower, at_head, at_loss = offsets(experts)
    lane = lanes_of()
    barrier = greet(size, me)

    def own_lines(device):
        count = small_got.shape[1]
        return pl.ds(pl.multiple_of(device * count, count), count)

    def to_all(source, target, sent, landed, step, receive):
        peer = lax.rem(me + (devices - step if receive else step), devices)
        return push(
            source(peer),
            target(peer if receive else me),
            sent,
            landed,
            place(size, peer),
        )

    def ask(step, receive):
        return to_all(
            lambda p: message.at[p], lambda p: asked.at[p], ask_sent, ask_landed, step, receive
        )

    def answer(part, step, receive):
        peer = lax.rem(me + (step if receive else devices - step), devices)
        return push(
            rows.at[part, peer],
            got.at[part, peer if receive else me],
            row_sent,
            row_landed.at[part],
            place(size, peer),
        )

    def give_slots(part, step, receive):
        return to_all(
            lambda p: slots_out.at[part, p],
            lambda p: slots_got.at[part, p],
            slot_sent,
            slot_landed.at[part],
            step,
            receive,
        )

    def give_small(step, receive):
        return to_all(
            lambda p: small_part.at[own_lines(p), :],
            lambda p: small_got.at[p],
            small_sent,
            small_landed,
            step,
            receive,
        )

    def give_whole(step, receive):
        return to_all(
            lambda p: small_sum.at[own_lines(me), :],
            lambda p: small_sum.at[own_lines(p), :],
            whole_sent,
            whole_landed,
            step,
            receive,
        )

    def turned(index, count, step, receive):
        return lax.rem(index + (count - step if receive else step), count)

    def weights_z(step, receive):
        other = turned(expert_here, experts, step, receive)
        block = gathered.at[group, other if receive else expert_here]
        return push(block, block, gz_sent, gz_landed, (group, other))

    def weights_y(step, receive):
        other = turned(chip, chips, step, receive)
        block = gathered.at[(other if receive else chip) * 2 + core]
        return push(
            block, block, gy_sent, gy_landed, (other * 2 + core, expert_here)
        )

    def weights_c(step, receive):
        other = turned(chip, chips, step, True)
        block = gathered.at[other * 2 + (1 - core if receive else core)]
        return push(
            block, block, gc_sent, gc_landed, (chip * 2 + 1 - core, expert_here)
        )

    def sums_c(step):
        other = turned(chip, chips, step, False)
        return push(
            grads.at[other * 2 + 1 - core],
            core_got.at[other],
            sc_sent,
            sc_landed,
            (chip * 2 + 1 - core, expert_here),
        )

    def sums_y(step, receive):
        other = turned(chip, chips, step, receive)
        return push(
            core_sum.at[other],
            chip_got.at[step],
            sy_sent,
            sy_landed,
            (other * 2 + core, expert_here),
        )

    def sums_z(step, receive):
        other = turned(expert_here, experts, step, receive)
        return push(
            chip_sum.at[other],
            z_got.at[step],
            sz_sent,
            sz_landed,
            (group, other),
        )

    def wait(semaphore, block):
        pltpu.make_async_copy(block, block, semaphore).wait()

    others = pl.ds(0, devices - 1)
    other_chips = pl.ds(0, chips - 1)
    other_experts = pl.ds(0, experts - 1)

    def loop(begin, end, body, unroll=1):
        def one(step, carry):
            body(step)
            return carry

        lax.fori_loop(begin, end, one, 0, unroll=unroll)

    valid = mask[...].astype(F32)
    count = jnp.where(
        lane == 0,
        jnp.sum(valid[0:1], 1, keepdims=True),
        jnp.where(lane == 1, jnp.sum(valid[1:2], 1, keepdims=True), 0.0),
    ).astype(jnp.int32)
    for part in range(size.groups):
        for one in range(experts):
            peer = part * experts + one
            message[peer, :, :slots] = requests[part, one : one + 1, :]
            message[peer, :, slots:] = count
    gathered[group, expert_here, : size.first, :] = first[...].astype(BF)
    gathered[group, expert_here, size.first :, :LANES] = second[:half].astype(BF)
    gathered[group, expert_here, size.first :, LANES:] = second[half:].astype(BF)
    for block in range(blocks):
        cells[block * EMB : (block + 1) * EMB, :] = table[
            :, block * KEYS : (block + 1) * KEYS
        ].astype(BF)
    pl.semaphore_wait(barrier, devices - 1)
    loop(1, devices, lambda step: ask(step, False).start())
    for step in range(1, experts):
        weights_z(step, False).start()

    vectors[...] = jnp.zeros_like(vectors)
    vectors[: at_dense // LANES, :] = small[: at_dense // LANES, :]
    lines = take(small, at_tower, TASKS * (OUT + 1) * TOWER // LANES)
    count_rows = lines.shape[0]
    tower_rows[pl.ds(0, count_rows, stride=2), :] = lines
    tower_rows[pl.ds(1, count_rows, stride=2), :] = turn(lines, TOWER)
    for task in range(TASKS):
        base = task * (OUT + 1)
        block = tower_rows[base : base + OUT, :]
        tower_n[task] = block[:, :TOWER].astype(BF)
        tower_t[task] = block.T[:TOWER].astype(BF)
    last = [tower_rows[k * (OUT + 1) + OUT : (k + 1) * (OUT + 1), :] for k in range(TASKS)]
    vectors[12:13, :] = jnp.where(lane < TOWER, last[0], turn(last[1], TOWER))
    heads = [take(small, at_head, 1)]
    end = at_head + TOWER + 1
    heads.append(turn(small[end // LANES : end // LANES + 1, :], -(end % LANES)))
    vectors[13:14, :] = jnp.where(lane < TOWER, heads[0], turn(heads[1], TOWER))
    vectors[15:16, :] = jnp.where(lane == 0, turn(heads[0], -TOWER), turn(heads[1], 1 - TOWER))
    per_line = LANES // gates_wide
    lines = take(small, at_gate, INPUT // per_line + 1)
    for spot in range(per_line):
        gate_rows[pl.ds(spot, lines.shape[0], stride=per_line), :] = jnp.where(
            lanes_of(lines.shape[0]) < gates_wide, turn(lines, -spot * gates_wide), 0.0
        )
    for block in range(INPUT // LANES):
        piece = gate_rows[block * LANES : (block + 1) * LANES, :]
        gate_t[:, block * LANES : (block + 1) * LANES] = piece.T[:16].astype(BF)
        wide[block * LANES : (block + 1) * LANES, experts * HID :] = piece.astype(BF)
    vectors[14:15, :] = gate_rows[INPUT : INPUT + 1, :]
    dense_rows[...] = jnp.zeros_like(dense_rows)
    for line in range(DENSE + 1):
        dense_rows[line : line + 1, :] = take(small, at_dense + line * DOUT, 1)
    dense_w[...] = dense_rows[...].T[:DOUT, :16]
    flipped = vectors[...].T
    for column in range(16):
        columns[column] = jnp.broadcast_to(flipped[:, column : column + 1], (LANES, LANES))
    feats[...] = jnp.ones_like(feats)
    feats[:DENSE, :] = dense[...]
    inputs[INPUT:, :] = jnp.ones((ONES, CHUNK), BF)
    for expert in range(experts):
        hidden[expert, HID:, :] = jnp.ones((ONES, CHUNK), BF)
    for task in range(TASKS):
        mixes[task, OUT:, :] = jnp.ones((ONES, CHUNK), BF)
    deltas[experts * HID :, :] = jnp.zeros((LANES, CHUNK), BF)
    for total in (
        sum_first,
        sum_second,
        sum_gate,
        sum_dense,
        sum_tower,
        sum_head,
        loss_sum,
        small_part,
        table_grad,
    ):
        total[...] = jnp.zeros_like(total)

    asked[me] = message[me]
    batch = 4

    def serve(part):
        columns_here = pl.ds(part * LANES, LANES)

        def some(turn_no, own):
            steps = [turn_no * batch + i for i in range(batch)]
            peers = [lax.rem(me + devices - step, devices) for step in steps]
            index = jnp.concatenate([asked[peer, :, columns_here] for peer in peers], 1)
            found = look_up(cells[...], index & (KEYS - 1), index >> 8, blocks).astype(BF)
            for i, peer in enumerate(peers):
                piece = found[:, i * LANES : (i + 1) * LANES]
                if own and i == 0:
                    got[part, peer] = piece
                else:
                    rows[part, peer] = piece
                    answer(part, steps[i], False).start()

        some(0, True)
        loop(1, devices // batch, lambda turn_no: some(turn_no, False), devices // batch - 1)

    wait(ask_landed, asked.at[others])
    serve(0)
    wait(gz_landed, gathered.at[0, other_experts])
    for step in range(1, chips):
        weights_y(step, False).start()
    weights_c(0, False).start()
    total = jnp.zeros((1, LANES), jnp.int32)
    for peer in range(devices):
        total = total + asked[peer, :, slots:]
    totals = jnp.maximum(total.astype(F32), 1.0)
    for part in range(1, chunks):
        serve(part)
        if part == chunks - 2:
            wait(gy_landed, gathered.at[other_chips])
            for step in range(1, chips):
                weights_c(step, False).start()

    def column(index, begin=0, end=LANES):
        block = columns[index, begin:end, :]
        return jnp.concatenate([block] * (CHUNK // LANES), 1)

    def chunk(step):
        here_tokens = pl.ds(pl.multiple_of(step * CHUNK, CHUNK), CHUNK)
        wait(row_landed.at[step], got.at[step, others])
        for owner in range(devices):
            level, lower = owner // 2, owner % 2
            slot_cells[
                level * EMB : (level + 1) * EMB, lower * LANES : (lower + 1) * LANES
            ] = got[step, owner]

        def split(field):
            index = picks[pl.ds(field, 1), here_tokens]
            owner = index >> shift
            return (owner & 1) * LANES + (index & (LANES - 1)), owner >> 1

        def pick(field):
            key, high = split(field)
            flags = as_low(spread(key, KEYS, CHUNK))
            chosen[field] = flags
            found = mm(slot_cells[...], flags)
            result = found[:EMB]
            for level in range(1, levels):
                result = jnp.where(high == level, found[level * EMB : (level + 1) * EMB], result)
            inputs[pl.ds(pl.multiple_of(field * EMB, EMB), EMB), :] = result.astype(BF)

        loop(0, FIELDS, pick, 13)

        @pl.when(step == 0)
        def weights_ready():
            wait(gc_landed, gathered.at[pl.ds(0, chips)])
            for expert in range(experts):
                for part in range(size.groups):
                    wide[
                        part * size.first : (part + 1) * size.first, expert * HID : (expert + 1) * HID
                    ] = gathered[part, expert, : size.first, :]
                    base = part * size.second
                    second_n[expert, base : base + half, :] = gathered[part, expert, size.first :, :LANES]
                    second_n[expert, base + half : base + 2 * half, :] = gathered[
                        part, expert, size.first :, LANES:
                    ]
                first_t[expert] = wide[:, expert * HID : (expert + 1) * HID].T
                second_t[expert] = second_n[expert].T

        inputs[FIELDS * EMB : INPUT, :] = mm(
            dense_w[...], feats[:, here_tokens], precision=HI
        ).astype(BF)
        x = inputs[:INPUT, :]
        logits = mm(gate_t[...], x)[:gates_wide] + column(14, 0, gates_wide)
        probs, gates = [], []
        for task in range(TASKS):
            line = [logits[task * experts + e : task * experts + e + 1] for e in range(experts)]
            top = functools.reduce(jnp.maximum, line)
            powers = [jnp.exp(item - top) for item in line]
            whole = 1.0 / functools.reduce(jnp.add, powers)
            probs.append([item * whole for item in powers])
            gates.append([item.astype(BF).astype(F32) for item in probs[-1]])
        mixed = [None] * TASKS
        for expert in range(experts):
            pre = mm(first_t[expert], x) + jnp.concatenate(
                [column(2 * expert), column(2 * expert + 1)], 0
            )
            sig = sigmoid(pre)
            act = pre * sig
            slope_one[expert] = sig + act * (1.0 - sig)
            hidden[expert, :HID, :] = act.astype(BF)
            pre = mm(second_t[expert], hidden[expert, :HID, :]) + column(8 + expert)
            sig = sigmoid(pre)
            act = pre * sig
            slope_two[expert] = sig + act * (1.0 - sig)
            outs[expert] = act
            for task in range(TASKS):
                term = gates[task][expert] * act
                mixed[task] = term if mixed[task] is None else mixed[task] + term
        d_mixed = []
        for task in range(TASKS):
            mixes[task, :OUT, :] = mixed[task].astype(BF)
            low, high = task * TOWER, (task + 1) * TOWER
            pre = mm(tower_t[task], mixes[task, :OUT, :]) + column(12, low, high)
            sig = sigmoid(pre)
            act = pre * sig
            head = column(13, low, high)
            logit = jnp.sum(act * head, 0, keepdims=True) + column(15, task, task + 1)
            scale = mask[task : task + 1, here_tokens].astype(F32) / totals[:, task : task + 1]
            target = labels[task : task + 1, here_tokens].astype(F32)
            soft = jnp.maximum(logit, 0.0) + jnp.log(1.0 + jnp.exp(-jnp.abs(logit)))
            loss_sum[...] += scale * (soft - target * logit)
            d_logit = scale * (sigmoid(logit) - target)
            d_pre = ((sig + act * (1.0 - sig)) * (d_logit * head)).astype(BF)
            sum_head[task] += mm(
                jnp.broadcast_to(d_logit, (8, CHUNK)),
                jnp.concatenate(
                    [act, jnp.ones((8, CHUNK), F32), jnp.zeros((LANES - TOWER - 8, CHUNK), F32)], 0
                ),
                NT,
                HI,
            )
            sum_tower[task] += mm(mixes[task], d_pre, NT)
            d_mixed.append(mm(tower_n[task], d_pre).astype(BF).astype(F32))
        d_gates = [[None] * experts for task in range(TASKS)]
        for expert in range(experts):
            d_out = gates[0][expert] * d_mixed[0] + gates[1][expert] * d_mixed[1]
            for task in range(TASKS):
                d_gates[task][expert] = jnp.sum(outs[expert] * d_mixed[task], 0, keepdims=True)
            d_two = (slope_two[expert] * d_out).astype(BF)
            sum_second[expert] += mm(hidden[expert], d_two, NT)
            d_one = (slope_one[expert] * mm(second_n[expert], d_two)).astype(BF)
            deltas[expert * HID : (expert + 1) * HID, :] = d_one
            sum_first[expert] += mm(inputs[...], d_one, NT)
        lines = []
        for task in range(TASKS):
            inner = functools.reduce(
                jnp.add, [probs[task][e] * d_gates[task][e] for e in range(experts)]
            )
            lines += [probs[task][e] * (d_gates[task][e] - inner) for e in range(experts)]
        lines.append(jnp.zeros((16 - gates_wide, CHUNK), F32))
        deltas[experts * HID : experts * HID + 16, :] = jnp.concatenate(lines, 0).astype(BF)
        sum_gate[...] += mm(inputs[...], deltas[experts * HID :, :], NT)
        d_inputs[...] = mm(wide[...], deltas[...])
        sum_dense[...] += mm(feats[:, here_tokens], d_inputs[INPUT - LANES :, :], NT, HI)

        @pl.when(step == chunks - 1)
        def sums_ready():
            for part in range(size.groups):
                base = part * size.second
                for expert in range(experts):
                    grads[part, expert, : size.first, :] = sum_first[
                        expert, part * size.first : (part + 1) * size.first, :
                    ].astype(BF)
                    grads[part, expert, size.first :, :LANES] = sum_second[
                        expert, base : base + half, :
                    ].astype(BF)
                    grads[part, expert, size.first :, LANES:] = sum_second[
                        expert, base + half : base + 2 * half, :
                    ].astype(BF)
            for step in range(1, chips + 1):
                sums_c(step % chips).start()
            for expert in range(experts):
                per = HID // LANES
                for piece in range(per):
                    line = expert * per + piece
                    small_part[line : line + 1, :] = sum_first[
                        expert, INPUT : INPUT + 1, piece * LANES : (piece + 1) * LANES
                    ]
                line = experts * per + expert
                small_part[line : line + 1, :] = sum_second[expert, HID : HID + 1, :]
            for line in range(DENSE + 1):
                values = jnp.where(lane < DOUT, turn(sum_dense[line : line + 1, :], DOUT - LANES), 0.0)
                put(small_part, at_dense + line * DOUT, values)
            lines = INPUT // per_line + 1
            packed = jnp.zeros((lines, LANES), F32)
            for spot in range(per_line):
                packed = packed + turn(sum_gate[pl.ds(spot, lines, stride=per_line), :], spot * gates_wide)
            inside = lax.broadcasted_iota(jnp.int32, (lines, LANES), 0) < lines - 1
            put(
                small_part,
                at_gate,
                jnp.where(inside | (lanes_of(lines) < gates_wide), packed, 0.0),
            )
            tower_rows[...] = jnp.zeros_like(tower_rows)
            for task in range(TASKS):
                base = task * (OUT + 1)
                tower_rows[base : base + OUT + 1, :TOWER] = sum_tower[task, : OUT + 1, :]
            put(
                small_part,
                at_tower,
                tower_rows[pl.ds(0, count_rows, stride=2), :]
                + turn(tower_rows[pl.ds(1, count_rows, stride=2), :], TOWER),
            )
            for task in range(TASKS):
                put(
                    small_part,
                    at_head + task * (TOWER + 1),
                    jnp.where(lane < TOWER + 1, sum_head[task, 0:1, :], 0.0),
                )
            whole_loss = jnp.sum(loss_sum[...], 1, keepdims=True)
            put(small_part, at_loss, jnp.where(lane == 0, whole_loss, 0.0))
            loop(1, devices, lambda step: give_small(step, False).start())

        slot_sum[...] = jnp.zeros_like(slot_sum)

        def give(field):
            key, high = split(field)
            values = d_inputs[pl.ds(pl.multiple_of(field * EMB, EMB), EMB), :]
            slot_sum[...] += mm(levels_of(values, high, levels), chosen[field], NT)

        loop(0, FIELDS, give, 13)
        for owner in range(devices):
            level, lower = owner // 2, owner % 2
            slots_out[step, owner] = slot_sum[
                level * EMB : (level + 1) * EMB, lower * LANES : (lower + 1) * LANES
            ].astype(BF)
        loop(1, devices, lambda hop: give_slots(step, hop, False).start())
        slots_got[step, me] = slots_out[step, me]

    loop(0, chunks, chunk)

    def collect(part):
        columns_here = pl.ds(part * LANES, LANES)
        wait(slot_landed.at[part], slots_got.at[part, others])

        def some(turn_no):
            steps = [turn_no * batch + i for i in range(batch)]
            peers = [lax.rem(me + devices - step, devices) for step in steps]
            index = jnp.concatenate([asked[peer, :, columns_here] for peer in peers], 1)
            values = jnp.concatenate([slots_got[part, peer] for peer in peers], 1).astype(F32)
            spots = as_low(spread(index & (KEYS - 1), KEYS, batch * LANES))
            table_grad[...] += mm(levels_of(values, index >> 8, blocks), spots, NT)

        loop(0, devices // batch, some, devices // batch)

    wait(sc_landed, core_got)
    for step in range(1, chips + 1):
        other = turned(chip, chips, step % chips, False)
        core_sum[other] = (
            grads[other * 2 + core].astype(F32) + core_got[other].astype(F32)
        ).astype(BF)
        if step < chips:
            sums_y(step, False).start()
    collect(0)
    wait(small_landed, small_got.at[others])
    small_got[me] = small_part[own_lines(me), :]
    small_sum[own_lines(me), :] = jnp.sum(small_got[...], 0)
    loop(1, devices, lambda step: give_whole(step, False).start())
    for part in range(1, chunks - 1):
        collect(part)
    wait(sy_landed, chip_got.at[other_chips])
    total = core_sum[chip].astype(F32)
    for step in range(1, chips):
        total = total + chip_got[step].astype(F32)
    chip_sum[...] = total.astype(BF)
    for step in range(1, experts):
        sums_z(step, False).start()
    collect(chunks - 1)
    wait(sz_landed, z_got.at[other_experts])
    total = chip_sum[expert_here].astype(F32)
    for step in range(1, experts):
        total = total + z_got[step].astype(F32)
    first_grad[...] = total[: size.first]
    second_grad[:half, :] = total[size.first :, :LANES]
    second_grad[half:, :] = total[size.first :, LANES:]

    other_lines = pl.ds(0, (devices - 1) * small_got.shape[1])
    wait(whole_landed, small_sum.at[other_lines, :])
    wait(whole_sent, small_sum.at[other_lines, :])
    wait(small_sent, small_part.at[other_lines, :])
    wait(ask_sent, message.at[others])
    wait(row_sent, rows.at[:, others])
    wait(slot_sent, slots_out.at[:, others])
    wait(gz_sent, gathered.at[0, other_experts])
    wait(gy_sent, gathered.at[other_chips])
    wait(gc_sent, gathered.at[pl.ds(0, chips)])
    wait(sc_sent, core_got)
    wait(sy_sent, core_sum.at[other_chips])
    wait(sz_sent, chip_sum.at[other_experts])


def update(size, *refs):
    grads, state, results = refs[:3], refs[3:12], refs[12:]
    table_grad = grads[0][...]
    wide = jnp.concatenate(
        [table_grad[b * EMB : (b + 1) * EMB] for b in range(size.rows // KEYS)], 1
    )
    for index, grad in enumerate((wide, grads[1][...], grads[2][...])):
        rate = 0.3 if index == 0 else 0.15
        values = [ref[...] for ref in state[3 * index : 3 * index + 3]]
        for ref, value in zip(results[3 * index : 3 * index + 3], adamw(*values, grad, rate)):
            ref[...] = value


def shape(dims, dtype=F32):
    return jax.ShapeDtypeStruct(dims, dtype)


def call(kernel, outs, scratch, remote=None):
    vmem = pl.BlockSpec(memory_space=pltpu.VMEM)
    params = dict(vmem_limit_bytes=56 * 2**20)
    if remote is not None:
        params.update(collective_id=remote, has_side_effects=True)
    return lambda *args: pl.pallas_call(
        kernel,
        out_shape=outs,
        in_specs=[vmem] * len(args),
        out_specs=[vmem] * len(outs),
        scratch_shapes=scratch,
        compiler_params=pltpu.CompilerParams(**params),
    )(*args)


def local(
    size,
    dense_feats,
    picks,
    labels,
    label_mask,
    requests,
    table,
    table_m,
    table_v,
    first_w,
    first_m,
    first_v,
    second_w,
    second_m,
    second_v,
    small,
    small_m,
    small_v,
):
    devices, experts, groups = size.devices, size.experts, size.groups
    chips = groups // 2
    chunks = size.tokens // CHUNK
    dma = pltpu.SemaphoreType.DMA
    vm = pltpu.VMEM
    message = size.slots + LANES
    count = small.shape[0]
    lines = -(-(count + 1) // (devices * 8 * LANES)) * 8
    flat_lines = -(-count // LANES)
    exchange = vm((chunks, devices, EMB, LANES), BF)
    weights = vm((groups, experts, size.pack, HID), BF)
    of_chips = vm((chips, experts, size.pack, HID), BF)
    of_chip = vm((experts, size.pack, HID), BF)
    table_grad, first_grad, second_grad, flat = call(
        functools.partial(step_kernel, size),
        [
            shape((size.rows // KEYS * EMB, KEYS)),
            shape((size.first, HID)),
            shape((size.second, OUT)),
            shape((devices * lines, LANES)),
        ],
        [
            vm((devices, 1, message), jnp.int32),
            vm((devices, 1, message), jnp.int32),
            vm((size.rows // KEYS * EMB, KEYS), BF),
        ]
        + [exchange] * 4
        + [weights, weights, of_chips, of_chips, of_chips, of_chip, of_chip]
        + [
            vm((LANES, LANES), F32),
            vm((16, LANES, LANES), F32),
            vm((INPUT + ONES, LANES), F32),
            vm((16, INPUT), BF),
            vm((TASKS * (OUT + 1) + 6, LANES), F32),
            vm((TASKS, OUT, TOWER), BF),
            vm((TASKS, TOWER, OUT), BF),
            vm((LANES, LANES), F32),
            vm((DOUT, 16), F32),
            vm((devices * lines, LANES), F32),
            vm((devices, lines, LANES), F32),
            vm((experts, HID, INPUT), BF),
            vm((experts, HID, OUT), BF),
            vm((experts, OUT, HID), BF),
            vm((INPUT, experts * HID + LANES), BF),
            vm((16, size.tokens), F32),
            vm((devices // 2 * EMB, KEYS), BF),
            vm((FIELDS, KEYS, CHUNK), BF),
            vm((INPUT + ONES, CHUNK), BF),
            vm((experts, HID, CHUNK), F32),
            vm((experts, OUT, CHUNK), F32),
            vm((experts, HID + ONES, CHUNK), BF),
            vm((experts, OUT, CHUNK), F32),
            vm((TASKS, OUT + ONES, CHUNK), BF),
            vm((experts * HID + LANES, CHUNK), BF),
            vm((INPUT, CHUNK), F32),
            vm((devices // 2 * EMB, KEYS), F32),
            vm((experts, INPUT + ONES, HID), F32),
            vm((experts, HID + ONES, OUT), F32),
            vm((INPUT + ONES, LANES), F32),
            vm((16, LANES), F32),
            vm((TASKS, OUT + ONES, TOWER), F32),
            vm((TASKS, 8, LANES), F32),
            vm((1, CHUNK), F32),
        ]
        + [dma, dma, dma, dma((chunks,)), dma, dma((chunks,))]
        + [dma] * 16,
        0,
    )(
        requests[0],
        picks.T,
        dense_feats.T,
        labels.T,
        label_mask.T,
        table.T,
        first_w[0],
        second_w[0],
        jnp.pad(small, (0, flat_lines * LANES - count)).reshape(flat_lines, LANES),
    )
    tables = (table.T, table_m.T, table_v.T)
    firsts = (first_w[0], first_m[0], first_v[0])
    seconds = (second_w[0], second_m[0], second_v[0])
    new = call(
        functools.partial(update, size),
        [shape(a.shape) for a in tables + firsts + seconds],
        [],
    )(table_grad, first_grad, second_grad, *tables, *firsts, *seconds)
    flat = flat.reshape(-1)
    new_small = adamw(small, small_m, small_v, flat[:count], 0.15)
    return (
        (flat[count],)
        + tuple(a.T for a in new[:3])
        + tuple(a[None] for a in new[3:])
        + tuple(new_small)
    )


def solution(mesh):
    both = P(("batch", "expert"), None)
    shard = P("expert", "batch", None)
    ins = (both,) * 4 + (P(("batch", "expert"), None, None, None),) + (both,) * 3
    ins = ins + (shard,) * 6 + (P(),) * 3

    def step(*args):
        devices = mesh.shape["batch"] * mesh.shape["expert"]
        size = sizes_of(
            mesh, args[0].shape[0] // devices, args[4].shape[-1], args[5].shape[0] // devices
        )
        return jax.shard_map(
            functools.partial(local, size) if fits(size) else plain,
            mesh=mesh,
            in_specs=ins,
            out_specs=(P(),) + (both,) * 3 + (shard,) * 6 + (P(),) * 3,
            check_vma=False,
        )(*args)

    return step
```

```python
import collections
import functools

import jax
import jax.numpy as jnp
from jax import lax
from jax.experimental import pallas as pl
from jax.experimental.pallas import tpu as pltpu
from jax.sharding import PartitionSpec as P

FIELDS = 26
EMB = 16
DENSE = 13
DOUT = 96
HID = 256
OUT = 128
TOWER = 64
TASKS = 2
STEP = 5
GROUP_TOK = 64
INPUT = 512


HI = lax.Precision.HIGHEST


def unpack(flat, experts):
    shapes = [
        (experts, HID),
        (experts, OUT),
        (DENSE + 1, DOUT),
        (INPUT + 1, TASKS * experts),
        (TASKS, OUT + 1, TOWER),
        (TASKS, TOWER + 1),
    ]
    parts = []
    offset = 0
    for shape in shapes:
        length = 1
        for extent in shape:
            length = length * extent
        parts.append(flat[offset : offset + length].reshape(shape))
        offset = offset + length
    return parts


def adamw(weight, first, second, grad, rate):
    first = 0.9 * first + 0.1 * grad
    second = 0.999 * second + 0.001 * grad * grad
    fix_one = 1.0 - 0.9**STEP
    fix_two = 1.0 - 0.999**STEP
    weight = weight - rate * (
        first / fix_one / (jnp.sqrt(second / fix_two) + 1e-08) + 0.01 * weight
    )
    return (weight, first, second)


def silu_slope(value):
    sig = jax.nn.sigmoid(value)
    return sig * (1.0 + value * (1.0 - sig))


def split_three(values):
    upper = values.astype(jnp.bfloat16)
    rest = values - upper.astype(jnp.float32)
    middle = rest.astype(jnp.bfloat16)
    lower_part = (rest - middle.astype(jnp.float32)).astype(jnp.bfloat16)
    return jnp.concatenate([upper, middle, lower_part], -1)


def join_three(values):
    return values[:, :EMB] + values[:, EMB : 2 * EMB] + values[:, 2 * EMB :]


def one_hot(index, extent):
    return (index[:, None] == jnp.arange(extent, dtype=jnp.int32)[None, :]).astype(jnp.bfloat16)


def pick_rows(index, source):
    return jnp.dot(
        one_hot(index, source.shape[0]), source, preferred_element_type=jnp.float32
    ).astype(jnp.bfloat16)


def add_rows(index, values, extent):
    spread = lax.dot_general(
        one_hot(index, extent),
        split_three(values),
        (((0,), (0,)), ((), ())),
        preferred_element_type=jnp.float32,
    )
    return join_three(spread)


def expert_forward(inputs, first_w, second_w, first_b, second_b):
    pre_one = (
        jnp.einsum("ti,eih->teh", inputs, first_w, preferred_element_type=jnp.float32)
        + first_b[None]
    )
    hidden = jax.nn.silu(pre_one).astype(jnp.bfloat16)
    pre_two = (
        jnp.einsum("teh,eho->teo", hidden, second_w, preferred_element_type=jnp.float32)
        + second_b[None]
    )
    return (pre_one, hidden, pre_two, jax.nn.silu(pre_two))


def expert_backward(inputs, first_w, second_w, pre_one, hidden, pre_two, d_out):
    d_two = (silu_slope(pre_two) * d_out).astype(jnp.bfloat16)
    d_second_w = jnp.einsum("teh,teo->eho", hidden, d_two, preferred_element_type=jnp.float32)
    d_second_b = jnp.sum(d_two, 0, dtype=jnp.float32)
    d_hidden = jnp.einsum("teo,eho->teh", d_two, second_w, preferred_element_type=jnp.float32)
    d_one = (silu_slope(pre_one) * d_hidden).astype(jnp.bfloat16)
    d_first_w = jnp.einsum("ti,teh->eih", inputs, d_one, preferred_element_type=jnp.float32)
    d_first_b = jnp.sum(d_one, 0, dtype=jnp.float32)
    d_inputs = jnp.einsum("teh,eih->ti", d_one, first_w, preferred_element_type=jnp.float32)
    return (d_first_w, d_second_w, d_first_b, d_second_b, d_inputs)


def plain(
    dense_feats,
    picks,
    labels,
    label_mask,
    requests,
    table,
    table_m,
    table_v,
    first_w,
    first_m,
    first_v,
    second_w,
    second_m,
    second_v,
    small,
    small_m,
    small_v,
):
    groups = lax.axis_size("batch")
    experts = lax.axis_size("expert")
    devices = groups * experts
    expert_idx = lax.axis_index("expert")
    tokens = dense_feats.shape[0]
    slots = requests.shape[-1]
    rows_dev = table.shape[0]
    tok_groups = tokens // GROUP_TOK
    sub_slots = slots // tok_groups
    group_slots = devices * sub_slots
    total_asked = devices * slots
    ask_block = min(1024, total_asked)
    bias_one, bias_two, dense_w, gate_w, tower_w, head_w = unpack(small, experts)
    first_full, second_full = (
        lax.all_gather(first_w.astype(jnp.bfloat16), "batch", axis=1, tiled=True),
        lax.all_gather(second_w.astype(jnp.bfloat16), "batch", axis=1, tiled=True),
    )
    asked = lax.all_to_all(
        lax.all_to_all(requests[0], "batch", split_axis=0, concat_axis=0, tiled=True),
        "expert",
        split_axis=1,
        concat_axis=1,
        tiled=True,
    )
    asked_blocks = asked.reshape(total_asked // ask_block, ask_block)
    table_low = table.astype(jnp.bfloat16)
    sent_rows = lax.map(lambda index: pick_rows(index, table_low), asked_blocks)
    sent_rows = sent_rows.reshape(groups, experts, slots * EMB)
    got_rows = lax.all_to_all(
        lax.all_to_all(sent_rows, "batch", split_axis=0, concat_axis=0, tiled=True),
        "expert",
        split_axis=1,
        concat_axis=1,
        tiled=True,
    )
    by_group = (
        got_rows.reshape(devices, tok_groups, sub_slots, EMB)
        .transpose(1, 0, 2, 3)
        .reshape(tok_groups, group_slots, EMB)
    )
    local_pick = (picks // slots * sub_slots + picks % sub_slots).reshape(
        tok_groups, GROUP_TOK * FIELDS
    )
    emb = lax.map(lambda item: pick_rows(item[0], item[1]), (local_pick, by_group)).reshape(
        tokens, FIELDS * EMB
    )
    dense_proj = jnp.dot(dense_feats, dense_w[:DENSE], precision=HI) + dense_w[DENSE]
    inputs = jnp.concatenate([emb, dense_proj.astype(jnp.bfloat16)], 1)
    gate_low = gate_w[:INPUT].astype(jnp.bfloat16)
    gate_logits = jnp.dot(inputs, gate_low, preferred_element_type=jnp.float32) + gate_w[INPUT]
    probs = jax.nn.softmax(gate_logits.reshape(tokens, TASKS, experts), axis=-1)
    gates = probs.astype(jnp.bfloat16)
    all_inputs, all_gates = (
        lax.all_gather(inputs, "expert", axis=0, tiled=True),
        lax.all_gather(gates.reshape(tokens, TASKS * experts), "expert", axis=0, tiled=True),
    )
    own_gates = lax.dynamic_slice_in_dim(
        all_gates.reshape(-1, TASKS, experts), expert_idx, 1, 2
    ).astype(jnp.float32)
    first_use, second_use = (first_full, second_full)
    first_b = lax.dynamic_slice_in_dim(bias_one, expert_idx, 1, 0)
    second_b = lax.dynamic_slice_in_dim(bias_two, expert_idx, 1, 0)
    pre_one, hidden, pre_two, expert_out = expert_forward(
        all_inputs, first_use, second_use, first_b, second_b
    )
    terms = jnp.einsum("tke,teo->tko", own_gates, expert_out, precision=HI).reshape(-1, TASKS * OUT)
    mixed = lax.psum_scatter(terms.astype(jnp.bfloat16), "expert", scatter_dimension=0, tiled=True)
    mask = label_mask.astype(jnp.float32)
    target = labels.astype(jnp.float32)
    counts = jnp.maximum(lax.psum(jnp.sum(mask, 0), ("batch", "expert")), 1.0)
    mixed_low = mixed.reshape(tokens, TASKS, OUT)
    tower_low = tower_w[:, :OUT].astype(jnp.bfloat16)
    tower_pre = (
        jnp.einsum("tko,koh->tkh", mixed_low, tower_low, preferred_element_type=jnp.float32)
        + tower_w[:, OUT][None]
    )
    tower_act = jax.nn.silu(tower_pre)
    logits = jnp.einsum("tkh,kh->tk", tower_act, head_w[:, :TOWER], precision=HI) + head_w[:, TOWER]
    loss_local = jnp.sum(mask * (jax.nn.softplus(logits) - target * logits) / counts)
    d_logits = mask * (jax.nn.sigmoid(logits) - target) / counts
    d_head = jnp.concatenate(
        [
            jnp.einsum("tkh,tk->kh", tower_act, d_logits, precision=HI),
            jnp.sum(d_logits, 0)[:, None],
        ],
        1,
    )
    d_act = d_logits[:, :, None] * head_w[None, :, :TOWER]
    d_tower_pre = (silu_slope(tower_pre) * d_act).astype(jnp.bfloat16)
    d_tower = jnp.concatenate(
        [
            jnp.einsum("tko,tkh->koh", mixed_low, d_tower_pre, preferred_element_type=jnp.float32),
            jnp.sum(d_tower_pre, 0, dtype=jnp.float32)[:, None, :],
        ],
        1,
    )
    d_mixed = jnp.einsum(
        "tkh,koh->tko", d_tower_pre, tower_low, preferred_element_type=jnp.float32
    ).astype(jnp.bfloat16)
    all_d_mixed = (
        lax.all_gather(d_mixed.reshape(tokens, TASKS * OUT), "expert", axis=0, tiled=True)
        .reshape(-1, TASKS, OUT)
        .astype(jnp.float32)
    )
    d_out = jnp.einsum("tke,tko->teo", own_gates, all_d_mixed, precision=HI)
    d_gate_col = jnp.einsum("teo,tko->tke", expert_out, all_d_mixed, precision=HI)
    d_first_w, d_second_w, d_first_b, d_second_b, d_rows = expert_backward(
        all_inputs, first_use, second_use, pre_one, hidden, pre_two, d_out
    )
    onehot = (jnp.arange(experts) == expert_idx).astype(jnp.float32)
    d_gate_full = (d_gate_col * onehot[None, None, :]).reshape(-1, TASKS * experts)
    d_inputs, d_gates = (
        lax.psum_scatter(
            d_rows.astype(jnp.bfloat16), "expert", scatter_dimension=0, tiled=True
        ).astype(jnp.float32),
        lax.psum_scatter(
            d_gate_full.astype(jnp.bfloat16), "expert", scatter_dimension=0, tiled=True
        ).astype(jnp.float32),
    )
    d_gates = d_gates.reshape(tokens, TASKS, experts)
    d_first_b = onehot[:, None] * d_first_b
    d_second_b = onehot[:, None] * d_second_b
    d_gate_logits = (
        (probs * (d_gates - jnp.sum(probs * d_gates, -1, keepdims=True)))
        .astype(jnp.bfloat16)
        .reshape(tokens, TASKS * experts)
    )
    d_gate_w = jnp.concatenate(
        [
            jnp.dot(inputs.T, d_gate_logits, preferred_element_type=jnp.float32),
            jnp.sum(d_gate_logits, 0, dtype=jnp.float32)[None],
        ],
        0,
    )
    d_x = d_inputs + jnp.dot(d_gate_logits, gate_low.T, preferred_element_type=jnp.float32)
    d_dense = d_x[:, FIELDS * EMB :]
    d_dense_w = jnp.concatenate(
        [jnp.dot(dense_feats.T, d_dense, precision=HI), jnp.sum(d_dense, 0)[None]], 0
    )
    d_emb = d_x[:, : FIELDS * EMB].reshape(tok_groups, GROUP_TOK * FIELDS, EMB)
    slot_grads = lax.map(lambda item: add_rows(item[0], item[1], group_slots), (local_pick, d_emb))
    slot_grads = (
        slot_grads.reshape(tok_groups, devices, sub_slots, EMB)
        .transpose(1, 0, 2, 3)
        .reshape(groups, experts, slots * EMB)
    )
    owner_grads = lax.all_to_all(
        lax.all_to_all(
            slot_grads.astype(jnp.bfloat16), "batch", split_axis=0, concat_axis=0, tiled=True
        ),
        "expert",
        split_axis=1,
        concat_axis=1,
        tiled=True,
    ).astype(slot_grads.dtype)
    owner_blocks = owner_grads.reshape(total_asked // ask_block, ask_block, EMB)

    def add_block(total, item):
        return (total + add_rows(item[0], item[1], rows_dev), None)

    table_grad, unused = lax.scan(
        add_block, jnp.zeros((rows_dev, EMB), jnp.float32), (asked_blocks, owner_blocks)
    )
    grad_first, grad_second = (
        lax.psum_scatter(
            d_first_w.astype(jnp.bfloat16), "batch", scatter_dimension=1, tiled=True
        ).astype(jnp.float32),
        lax.psum_scatter(
            d_second_w.astype(jnp.bfloat16), "batch", scatter_dimension=1, tiled=True
        ).astype(jnp.float32),
    )
    flat_grads = jnp.concatenate(
        [
            d_first_b.reshape(-1),
            d_second_b.reshape(-1),
            d_dense_w.reshape(-1),
            d_gate_w.reshape(-1),
            d_tower.reshape(-1),
            d_head.reshape(-1),
        ]
    )
    grad_small, loss = lax.psum((flat_grads, loss_local), ("batch", "expert"))
    new_table, new_table_m, new_table_v = adamw(table, table_m, table_v, table_grad, 0.3)
    new_first, new_first_m, new_first_v = adamw(first_w, first_m, first_v, grad_first, 0.15)
    new_second, new_second_m, new_second_v = adamw(second_w, second_m, second_v, grad_second, 0.15)
    new_small, new_small_m, new_small_v = adamw(small, small_m, small_v, grad_small, 0.15)
    return (
        loss,
        new_table,
        new_table_m,
        new_table_v,
        new_first,
        new_first_m,
        new_first_v,
        new_second,
        new_second_m,
        new_second_v,
        new_small,
        new_small_m,
        new_small_v,
    )


MESH = pl.DeviceIdType.MESH
BF = jnp.bfloat16
F32 = jnp.float32
NN = (((1,), (0,)), ((), ()))
NT = (((1,), (1,)), ((), ()))
KEYS = 256
CHUNK = 256
LANES = 128
ONES = 16

Sizes = collections.namedtuple(
    "Sizes",
    (
        "groups",
        "experts",
        "devices",
        "slots",
        "rows",
        "tokens",
        "first",
        "second",
        "pack",
        "span",
    ),
)


def sizes_of(mesh, tokens, slots, rows):
    groups = mesh.shape["batch"]
    experts = mesh.shape["expert"]
    first = INPUT // groups
    second = HID // groups
    span = tokens * LANES // slots
    return Sizes(
        groups,
        experts,
        groups * experts,
        slots,
        rows,
        tokens,
        first,
        second,
        first + second // 2,
        span,
    )


def fits(size):
    return (
        size.slots % LANES == 0
        and size.slots & (size.slots - 1) == 0
        and size.span == CHUNK
        and size.second % 32 == 0
        and size.first % 16 == 0
        and size.groups % 2 == 0
        and size.devices % 2 == 0
        and size.rows % KEYS == 0
        and size.experts == 4
    )


def mm(left, right, dims=NN, precision=None):
    return lax.dot_general(left, right, dims, preferred_element_type=F32, precision=precision)


def here(size):
    group = lax.axis_index("batch")
    expert = lax.axis_index("expert")
    return group, expert, group * size.experts + expert


def place(size, device):
    return (lax.div(device, size.experts), lax.rem(device, size.experts))


def greet(size, me):
    barrier = pltpu.get_barrier_semaphore()

    def one(step, carry):
        peer = lax.rem(me + step, size.devices)
        pl.semaphore_signal(barrier, inc=1, device_id=place(size, peer), device_id_type=MESH)
        return carry

    lax.fori_loop(1, size.devices, one, 0)
    return barrier


def push(source, target, sent, landed, where):
    return pltpu.make_async_remote_copy(
        src_ref=source,
        dst_ref=target,
        send_sem=sent,
        recv_sem=landed,
        device_id=where,
        device_id_type=MESH,
    )


def spread(index, extent, width):
    return lax.broadcasted_iota(jnp.int32, (extent, width), 0) == index


def as_low(flag):
    return jnp.where(flag, 1.0, 0.0).astype(BF)


def look_up(cells, key, high, levels):
    found = mm(cells, as_low(spread(key, KEYS, key.shape[1])))
    result = found[:EMB]
    for level in range(1, levels):
        result = jnp.where(high == level, found[level * EMB : (level + 1) * EMB], result)
    return result


def levels_of(values, high, levels):
    return jnp.concatenate(
        [jnp.where(high == level, values, 0.0) for level in range(levels)], 0
    ).astype(BF)


def sigmoid(value):
    return 0.5 + 0.5 * jnp.tanh(0.5 * value)


def lanes_of(rows=1):
    return lax.broadcasted_iota(jnp.int32, (rows, LANES), 1)


def turn(values, shift):
    shift = shift % LANES
    return pltpu.roll(values, shift, 1) if shift else values


def take(flat, offset, count):
    row, shift = offset // LANES, offset % LANES
    if shift == 0:
        return flat[row : row + count, :]
    return jnp.where(
        lanes_of(count) < LANES - shift,
        turn(flat[row : row + count, :], -shift),
        turn(flat[row + 1 : row + 1 + count, :], -shift),
    )


def put(flat, offset, values):
    row, shift = offset // LANES, offset % LANES
    count = values.shape[0]
    moved = turn(values, shift)
    if shift == 0:
        flat[row : row + count, :] += moved
        return
    flat[row : row + count, :] += jnp.where(lanes_of(count) >= shift, moved, 0.0)
    flat[row + 1 : row + 1 + count, :] += jnp.where(lanes_of(count) < shift, moved, 0.0)


def offsets(experts):
    sizes = [
        experts * HID,
        experts * OUT,
        (DENSE + 1) * DOUT,
        (INPUT + 1) * TASKS * experts,
        TASKS * (OUT + 1) * TOWER,
        TASKS * (TOWER + 1),
    ]
    return [sum(sizes[:index]) for index in range(len(sizes) + 1)]


def step_kernel(
    size,
    requests,
    picks,
    dense,
    labels,
    mask,
    table,
    first,
    second,
    small,
    table_grad,
    first_grad,
    second_grad,
    small_sum,
    message,
    asked,
    cells,
    rows,
    got,
    slots_out,
    slots_got,
    gathered,
    grads,
    core_got,
    core_sum,
    chip_got,
    chip_sum,
    z_got,
    vectors,
    columns,
    gate_rows,
    gate_t,
    tower_rows,
    tower_n,
    tower_t,
    dense_rows,
    dense_w,
    dense_low,
    small_part,
    small_got,
    first_t,
    second_n,
    second_t,
    wide,
    feats,
    feats_low,
    slot_cells_a,
    slot_cells_b,
    chosen_a,
    chosen_b,
    chosen_c,
    inputs_a,
    inputs_b,
    slope_one,
    slope_two,
    hidden,
    outs,
    mixes,
    deltas,
    d_inputs_a,
    d_inputs_b,
    slot_sum_a,
    slot_sum_b,
    sum_first,
    sum_second,
    sum_gate,
    sum_dense,
    sum_tower,
    sum_head,
    loss_sum,
    ask_sent,
    ask_landed,
    row_sent,
    row_landed,
    slot_sent,
    slot_landed,
    small_sent,
    small_landed,
    whole_sent,
    whole_landed,
    gz_sent,
    gz_landed,
    gy_sent,
    gy_landed,
    gc_sent,
    gc_landed,
    sz_sent,
    sz_landed,
    sy_sent,
    sy_landed,
    sc_sent,
    sc_landed,
):
    group, expert_here, me = here(size)
    slots, devices, experts = size.slots, size.devices, size.experts
    chips = size.groups // 2
    chip, core = lax.div(group, 2), lax.rem(group, 2)
    blocks = size.rows // KEYS
    half = size.second // 2
    levels = devices // 2
    shift = slots.bit_length() - 1
    chunks = size.tokens // CHUNK
    gates_wide = TASKS * experts
    at_one, at_two, at_dense, at_gate, at_tower, at_head, at_loss = offsets(experts)
    lane = lanes_of()
    barrier = greet(size, me)
    slot_cells = (slot_cells_a, slot_cells_b)
    chosen = (chosen_a, chosen_b, chosen_c)
    inputs = (inputs_a, inputs_b)
    d_inputs = (d_inputs_a, d_inputs_b)
    slot_sum = (slot_sum_a, slot_sum_b)

    def own_lines(device):
        count = small_got.shape[1]
        return pl.ds(pl.multiple_of(device * count, count), count)

    def to_all(source, target, sent, landed, step, receive):
        peer = lax.rem(me + (devices - step if receive else step), devices)
        return push(
            source(peer),
            target(peer if receive else me),
            sent,
            landed,
            place(size, peer),
        )

    def ask(step, receive):
        return to_all(
            lambda p: message.at[p], lambda p: asked.at[p], ask_sent, ask_landed, step, receive
        )

    def answer(part, step, receive):
        peer = lax.rem(me + (step if receive else devices - step), devices)
        return push(
            rows.at[part, peer],
            got.at[part, peer if receive else me],
            row_sent,
            row_landed.at[part],
            place(size, peer),
        )

    def give_slots(part, step, receive):
        return to_all(
            lambda p: slots_out.at[part, p],
            lambda p: slots_got.at[part, p],
            slot_sent,
            slot_landed.at[part],
            step,
            receive,
        )

    def give_small(step, receive):
        return to_all(
            lambda p: small_part.at[own_lines(p), :],
            lambda p: small_got.at[p],
            small_sent,
            small_landed,
            step,
            receive,
        )

    def give_whole(step, receive):
        return to_all(
            lambda p: small_sum.at[own_lines(me), :],
            lambda p: small_sum.at[own_lines(p), :],
            whole_sent,
            whole_landed,
            step,
            receive,
        )

    def turned(index, count, step, receive):
        return lax.rem(index + (count - step if receive else step), count)

    def weights_z(step):
        other = turned(expert_here, experts, step, False)
        block = gathered.at[group, expert_here]
        return push(block, block, gz_sent, gz_landed.at[step], (group, other))

    def weights_y(step, source):
        other = turned(chip, chips, step, False)
        block = gathered.at[group, source]
        return push(
            block, block, gy_sent, gy_landed, (other * 2 + core, expert_here)
        )

    def weights_c(step):
        other = turned(chip, chips, step, True)
        block = gathered.at[other * 2 + core]
        return push(
            block, block, gc_sent, gc_landed, (chip * 2 + 1 - core, expert_here)
        )

    def sums_c(step):
        other = turned(chip, chips, step, False)
        return push(
            grads.at[other * 2 + 1 - core],
            core_got.at[other],
            sc_sent,
            sc_landed,
            (chip * 2 + 1 - core, expert_here),
        )

    def sums_y(step, receive):
        other = turned(chip, chips, step, receive)
        return push(
            core_sum.at[other],
            chip_got.at[step],
            sy_sent,
            sy_landed,
            (other * 2 + core, expert_here),
        )

    def sums_z(step, receive):
        other = turned(expert_here, experts, step, receive)
        return push(
            chip_sum.at[other],
            z_got.at[step],
            sz_sent,
            sz_landed,
            (group, other),
        )

    def wait(semaphore, block):
        pltpu.make_async_copy(block, block, semaphore).wait()

    others = pl.ds(0, devices - 1)
    other_chips = pl.ds(0, chips - 1)
    other_experts = pl.ds(0, experts - 1)

    def loop(begin, end, body, unroll=1):
        def one(step, carry):
            body(step)
            return carry

        lax.fori_loop(begin, end, one, 0, unroll=unroll)

    valid = mask[...].astype(F32)
    count = jnp.where(
        lane == 0,
        jnp.sum(valid[0:1], 1, keepdims=True),
        jnp.where(lane == 1, jnp.sum(valid[1:2], 1, keepdims=True), 0.0),
    ).astype(jnp.int32)
    for part in range(size.groups):
        for one in range(experts):
            peer = part * experts + one
            message[peer, :, :slots] = requests[part, one : one + 1, :]
            message[peer, :, slots:] = count
    gathered[group, expert_here, : size.first, :] = first[...].astype(BF)
    gathered[group, expert_here, size.first :, :LANES] = second[:half].astype(BF)
    gathered[group, expert_here, size.first :, LANES:] = second[half:].astype(BF)
    for block in range(blocks):
        cells[block * EMB : (block + 1) * EMB, :] = table[
            :, block * KEYS : (block + 1) * KEYS
        ].astype(BF)
    pl.semaphore_wait(barrier, devices - 1)
    for step in range(1, experts):
        weights_z(step).start()
    for step in range(1, chips):
        weights_y(step, expert_here).start()
    loop(1, devices, lambda step: ask(step, False).start())

    vectors[...] = jnp.zeros_like(vectors)
    vectors[: at_dense // LANES, :] = small[: at_dense // LANES, :]
    lines = take(small, at_tower, TASKS * (OUT + 1) * TOWER // LANES)
    count_rows = lines.shape[0]
    tower_rows[pl.ds(0, count_rows, stride=2), :] = lines
    tower_rows[pl.ds(1, count_rows, stride=2), :] = turn(lines, TOWER)
    for task in range(TASKS):
        base = task * (OUT + 1)
        block = tower_rows[base : base + OUT, :]
        tower_n[task] = block[:, :TOWER].astype(BF)
        tower_t[task] = block.T[:TOWER].astype(BF)
    last = [tower_rows[k * (OUT + 1) + OUT : (k + 1) * (OUT + 1), :] for k in range(TASKS)]
    vectors[12:13, :] = jnp.where(lane < TOWER, last[0], turn(last[1], TOWER))
    heads = [take(small, at_head, 1)]
    end = at_head + TOWER + 1
    heads.append(turn(small[end // LANES : end // LANES + 1, :], -(end % LANES)))
    vectors[13:14, :] = jnp.where(lane < TOWER, heads[0], turn(heads[1], TOWER))
    vectors[15:16, :] = jnp.where(lane == 0, turn(heads[0], -TOWER), turn(heads[1], 1 - TOWER))
    per_line = LANES // gates_wide
    lines = take(small, at_gate, INPUT // per_line + 1)
    for spot in range(per_line):
        gate_rows[pl.ds(spot, lines.shape[0], stride=per_line), :] = jnp.where(
            lanes_of(lines.shape[0]) < gates_wide, turn(lines, -spot * gates_wide), 0.0
        )
    for block in range(INPUT // LANES):
        piece = gate_rows[block * LANES : (block + 1) * LANES, :]
        gate_t[:, block * LANES : (block + 1) * LANES] = piece.T[:16].astype(BF)
        wide[block * LANES : (block + 1) * LANES, experts * HID :] = piece.astype(BF)
    vectors[14:15, :] = gate_rows[INPUT : INPUT + 1, :]
    dense_rows[...] = jnp.zeros_like(dense_rows)
    for line in range(DENSE + 1):
        dense_rows[line : line + 1, :] = take(small, at_dense + line * DOUT, 1)
    dense_w[...] = dense_rows[...].T[:DOUT, :16]
    flipped = vectors[...].T
    for column in range(16):
        columns[column] = jnp.broadcast_to(flipped[:, column : column + 1], (LANES, LANES))
    feats[...] = jnp.ones_like(feats)
    feats[:DENSE, :] = dense[...]
    upper = feats[...].astype(BF)
    feats_low[:16, :] = upper
    feats_low[16:, :] = (feats[...] - upper.astype(F32)).astype(BF)
    dense_low[...] = mm(dense_w[...], feats[...], precision=HI).astype(BF)
    for buffer in inputs:
        buffer[INPUT:, :] = jnp.ones((ONES, CHUNK), BF)
    for expert in range(experts):
        hidden[expert, HID:, :] = jnp.ones((ONES, CHUNK), BF)
    for task in range(TASKS):
        mixes[task, OUT:, :] = jnp.ones((ONES, CHUNK), BF)
    deltas[experts * HID :, :] = jnp.zeros((LANES, CHUNK), BF)
    for total in (sum_gate, loss_sum, small_part, table_grad):
        total[...] = jnp.zeros_like(total)

    asked[me] = message[me]
    batch = 4

    def serve(part):
        columns_here = pl.ds(part * LANES, LANES)

        def some(turn_no, own):
            steps = [turn_no * batch + i for i in range(batch)]
            peers = [lax.rem(me + devices - step, devices) for step in steps]
            index = jnp.concatenate([asked[peer, :, columns_here] for peer in peers], 1)
            found = look_up(cells[...], index & (KEYS - 1), index >> 8, blocks).astype(BF)
            for i, peer in enumerate(peers):
                piece = found[:, i * LANES : (i + 1) * LANES]
                if own and i == 0:
                    got[part, peer] = piece
                else:
                    rows[part, peer] = piece
                    answer(part, steps[i], False).start()

        some(0, True)
        loop(1, devices // batch, lambda turn_no: some(turn_no, False), devices // batch - 1)

    wait(ask_landed, asked.at[others])
    for step in range(1, experts):
        source = turned(expert_here, experts, step, True)
        wait(gz_landed.at[step], gathered.at[group, source])
        for hop in range(1, chips):
            weights_y(hop, source).start()
    weights_c(0).start()
    serve(0)
    total = jnp.zeros((1, LANES), jnp.int32)
    for peer in range(devices):
        total = total + asked[peer, :, slots:]
    totals = jnp.maximum(total.astype(F32), 1.0)
    for part in range(1, chunks - 1):
        serve(part)
    wait(gy_landed, gathered.at[other_chips])
    for step in range(1, chips):
        weights_c(step).start()
    serve(chunks - 1)

    def column(index, begin=0, end=LANES):
        block = columns[index, begin:end, :]
        return jnp.concatenate([block] * (CHUNK // LANES), 1)

    def tokens_of(part):
        return slice(part * CHUNK, (part + 1) * CHUNK)

    def split(part, field):
        index = picks[field : field + 1, tokens_of(part)]
        owner = index >> shift
        return (owner & 1) * LANES + (index & (LANES - 1)), owner >> 1

    def fetch(part):
        wait(row_landed.at[part], got.at[part, others])
        for owner in range(devices):
            level, lower = owner // 2, owner % 2
            slot_cells[part % 2][
                level * EMB : (level + 1) * EMB, lower * LANES : (lower + 1) * LANES
            ] = got[part, owner]
        inputs[part % 2][FIELDS * EMB : INPUT, :] = dense_low[:, tokens_of(part)]

    def pick(part, field):
        key, high = split(part, field)
        flags = as_low(spread(key, KEYS, CHUNK))
        chosen[part % 3][field] = flags
        found = mm(slot_cells[part % 2][...], flags)
        result = found[:EMB]
        for level in range(1, levels):
            result = jnp.where(high == level, found[level * EMB : (level + 1) * EMB], result)
        inputs[part % 2][field * EMB : (field + 1) * EMB, :] = result.astype(BF)

    def give(part, field, first_time):
        places, flags = [], []
        for one in (field, field + 1):
            key, high = split(part, one)
            values = d_inputs[part % 2][one * EMB : (one + 1) * EMB, :]
            places.append(levels_of(values, high, levels))
            flags.append(chosen[part % 3][one])
        sums = mm(jnp.concatenate(places, 1), jnp.concatenate(flags, 1), NT)
        if first_time:
            slot_sum[part % 2][...] = sums
        else:
            slot_sum[part % 2][...] += sums

    def picks_of(part):
        return [functools.partial(pick, part, field) for field in range(FIELDS)]

    def gives_of(part):
        return [
            functools.partial(give, part, field, field == 0) for field in range(0, FIELDS, 2)
        ]

    def send_slots(part):
        for owner in range(devices):
            level, lower = owner // 2, owner % 2
            slots_out[part, owner] = slot_sum[part % 2][
                level * EMB : (level + 1) * EMB, lower * LANES : (lower + 1) * LANES
            ].astype(BF)
        loop(1, devices, lambda hop: give_slots(part, hop, False).start())
        slots_got[part, me] = slots_out[part, me]

    def train(part):
        here_tokens = tokens_of(part)
        first_time = part == 0
        whole_x = inputs[part % 2]

        def add(total, value):
            if first_time:
                total[...] = value
            else:
                total[...] += value

        x = whole_x[:INPUT, :]
        logits = mm(gate_t[...], x)[:gates_wide] + column(14, 0, gates_wide)
        probs, gates = [], []
        for task in range(TASKS):
            line = [logits[task * experts + e : task * experts + e + 1] for e in range(experts)]
            top = functools.reduce(jnp.maximum, line)
            powers = [jnp.exp(item - top) for item in line]
            whole = 1.0 / functools.reduce(jnp.add, powers)
            probs.append([item * whole for item in powers])
            gates.append([item.astype(BF).astype(F32) for item in probs[-1]])
        yield
        mixed = [None] * TASKS
        for expert in range(experts):
            pre = mm(first_t[expert], x) + jnp.concatenate(
                [column(2 * expert), column(2 * expert + 1)], 0
            )
            sig = sigmoid(pre)
            act = pre * sig
            slope_one[expert] = sig + act * (1.0 - sig)
            low = act.astype(BF)
            hidden[expert, :HID, :] = low
            yield
            pre = mm(second_t[expert], low) + column(8 + expert)
            sig = sigmoid(pre)
            act = pre * sig
            slope_two[expert] = sig + act * (1.0 - sig)
            outs[expert] = act
            for task in range(TASKS):
                term = gates[task][expert] * act
                mixed[task] = term if mixed[task] is None else mixed[task] + term
            yield
        d_mixed = []
        for task in range(TASKS):
            mix = mixed[task].astype(BF)
            mixes[task, :OUT, :] = mix
            low, high = task * TOWER, (task + 1) * TOWER
            pre = mm(tower_t[task], mix) + column(12, low, high)
            sig = sigmoid(pre)
            act = pre * sig
            head = column(13, low, high)
            logit = jnp.sum(act * head, 0, keepdims=True) + column(15, task, task + 1)
            scale = mask[task : task + 1, here_tokens].astype(F32) / totals[:, task : task + 1]
            target = labels[task : task + 1, here_tokens].astype(F32)
            soft = jnp.maximum(logit, 0.0) + jnp.log(1.0 + jnp.exp(-jnp.abs(logit)))
            loss_sum[...] += scale * (soft - target * logit)
            d_logit = scale * (sigmoid(logit) - target)
            yield
            d_pre = ((sig + act * (1.0 - sig)) * (d_logit * head)).astype(BF)
            d_upper = d_logit.astype(BF).astype(F32)
            d_both = jnp.concatenate(
                [
                    jnp.broadcast_to(d_upper, (8, CHUNK)),
                    jnp.broadcast_to(d_logit - d_upper, (8, CHUNK)),
                ],
                0,
            ).astype(BF)
            upper = act.astype(BF)
            rest = (act - upper.astype(F32)).astype(BF)
            ones = jnp.ones((16, CHUNK), BF)
            zeros = jnp.zeros((LANES - TOWER - 16, CHUNK), BF)
            both = mm(d_both, jnp.concatenate([upper, ones, zeros], 0), NT) + mm(
                d_both, jnp.concatenate([rest, zeros, jnp.zeros((16, CHUNK), BF)], 0), NT
            )
            add(sum_head.at[task], both[:8] + both[8:])
            add(sum_tower.at[task], mm(mixes[task], d_pre, NT))
            d_mixed.append(mm(tower_n[task], d_pre).astype(BF).astype(F32))
            yield
        d_gates = [[None] * experts for task in range(TASKS)]
        for expert in range(experts):
            d_out = gates[0][expert] * d_mixed[0] + gates[1][expert] * d_mixed[1]
            out = outs[expert]
            for task in range(TASKS):
                d_gates[task][expert] = jnp.sum(out * d_mixed[task], 0, keepdims=True)
            d_two = (slope_two[expert] * d_out).astype(BF)
            d_hidden = mm(second_n[expert], d_two)
            add(sum_second.at[expert], mm(hidden[expert], d_two, NT))
            yield
            d_one = (slope_one[expert] * d_hidden).astype(BF)
            deltas[expert * HID : (expert + 1) * HID, :] = d_one
            add(sum_first.at[expert], mm(whole_x[...], d_one, NT))
            yield
        lines = []
        for task in range(TASKS):
            inner = functools.reduce(
                jnp.add, [probs[task][e] * d_gates[task][e] for e in range(experts)]
            )
            lines += [probs[task][e] * (d_gates[task][e] - inner) for e in range(experts)]
        lines.append(jnp.zeros((16 - gates_wide, CHUNK), F32))
        d_gate = jnp.concatenate(lines, 0).astype(BF)
        deltas[experts * HID : experts * HID + 16, :] = d_gate
        add(sum_gate.at[:, : INPUT + ONES], mm(d_gate, whole_x[...], NT))
        yield
        d_x = mm(wide[...], deltas[...])
        d_inputs[part % 2][...] = d_x
        d_dense = d_x[INPUT - LANES :, :]
        upper = d_dense.astype(BF)
        rest = (d_dense - upper.astype(F32)).astype(BF)
        both = mm(feats_low[:, here_tokens], upper, NT)
        add(sum_dense, both[:16] + both[16:] + mm(feats_low[:16, here_tokens], rest, NT))
        yield

    stops = 2 + 2 * experts + 2 * TASKS + 2 * experts + 1

    def beside(main, jobs):
        jobs, done = list(jobs), 0
        for stop, _ in enumerate(main):
            until = len(jobs) * (stop + 1) // stops
            for job in jobs[done:until]:
                job()
            done = until
        for job in jobs[done:]:
            job()

    def mixed_jobs(*lists):
        spots = [
            ((index + 0.5) / len(jobs), job) for jobs in lists for index, job in enumerate(jobs)
        ]
        return [job for spot, job in sorted(spots, key=lambda pair: pair[0])]

    fetch(0)
    for job in picks_of(0):
        job()
    wait(gc_landed, gathered.at[pl.ds(0, chips)])
    for expert in range(experts):
        for part in range(size.groups):
            wide[
                part * size.first : (part + 1) * size.first, expert * HID : (expert + 1) * HID
            ] = gathered[part, expert, : size.first, :]
            base = part * size.second
            second_n[expert, base : base + half, :] = gathered[part, expert, size.first :, :LANES]
            second_n[expert, base + half : base + 2 * half, :] = gathered[
                part, expert, size.first :, LANES:
            ]
        first_t[expert] = wide[:, expert * HID : (expert + 1) * HID].T
        second_t[expert] = second_n[expert].T
    for part in range(chunks):
        jobs = []
        if part + 1 < chunks:
            fetch(part + 1)
            jobs.append(picks_of(part + 1))
        if part > 0:
            jobs.append(gives_of(part - 1))
        beside(train(part), mixed_jobs(*jobs))
        if part > 0:
            send_slots(part - 1)

    for part in range(size.groups):
        base = part * size.second
        for expert in range(experts):
            grads[part, expert, : size.first, :] = sum_first[
                expert, part * size.first : (part + 1) * size.first, :
            ].astype(BF)
            grads[part, expert, size.first :, :LANES] = sum_second[
                expert, base : base + half, :
            ].astype(BF)
            grads[part, expert, size.first :, LANES:] = sum_second[
                expert, base + half : base + 2 * half, :
            ].astype(BF)
    for step in range(1, chips + 1):
        sums_c(step % chips).start()
    for expert in range(experts):
        per = HID // LANES
        for piece in range(per):
            line = expert * per + piece
            small_part[line : line + 1, :] = sum_first[
                expert, INPUT : INPUT + 1, piece * LANES : (piece + 1) * LANES
            ]
        line = experts * per + expert
        small_part[line : line + 1, :] = sum_second[expert, HID : HID + 1, :]
    for line in range(DENSE + 1):
        values = jnp.where(lane < DOUT, turn(sum_dense[line : line + 1, :], DOUT - LANES), 0.0)
        put(small_part, at_dense + line * DOUT, values)
    fill = jnp.zeros((LANES - 16, LANES), F32)
    for block in range(INPUT // LANES):
        piece = jnp.concatenate([sum_gate[:, block * LANES : (block + 1) * LANES], fill], 0)
        gate_rows[block * LANES : (block + 1) * LANES, :] = piece.T
    gate_rows[INPUT:, :] = jnp.concatenate([sum_gate[:, INPUT:], fill], 0).T[:ONES]
    lines = INPUT // per_line + 1
    packed = jnp.zeros((lines, LANES), F32)
    for spot in range(per_line):
        packed = packed + turn(gate_rows[pl.ds(spot, lines, stride=per_line), :], spot * gates_wide)
    inside = lax.broadcasted_iota(jnp.int32, (lines, LANES), 0) < lines - 1
    put(
        small_part,
        at_gate,
        jnp.where(inside | (lanes_of(lines) < gates_wide), packed, 0.0),
    )
    tower_rows[...] = jnp.zeros_like(tower_rows)
    for task in range(TASKS):
        base = task * (OUT + 1)
        tower_rows[base : base + OUT + 1, :TOWER] = sum_tower[task, : OUT + 1, :]
    put(
        small_part,
        at_tower,
        tower_rows[pl.ds(0, count_rows, stride=2), :]
        + turn(tower_rows[pl.ds(1, count_rows, stride=2), :], TOWER),
    )
    for task in range(TASKS):
        put(
            small_part,
            at_head + task * (TOWER + 1),
            jnp.where(lane < TOWER + 1, sum_head[task, 0:1, :], 0.0),
        )
    whole_loss = jnp.sum(loss_sum[...], 1, keepdims=True)
    put(small_part, at_loss, jnp.where(lane == 0, whole_loss, 0.0))
    loop(1, devices, lambda step: give_small(step, False).start())
    for job in gives_of(chunks - 1):
        job()
    send_slots(chunks - 1)

    def collect(part):
        columns_here = pl.ds(part * LANES, LANES)
        wait(slot_landed.at[part], slots_got.at[part, others])

        def some(turn_no):
            steps = [turn_no * batch + i for i in range(batch)]
            peers = [lax.rem(me + devices - step, devices) for step in steps]
            index = jnp.concatenate([asked[peer, :, columns_here] for peer in peers], 1)
            values = jnp.concatenate([slots_got[part, peer] for peer in peers], 1).astype(F32)
            spots = as_low(spread(index & (KEYS - 1), KEYS, batch * LANES))
            table_grad[...] += mm(levels_of(values, index >> 8, blocks), spots, NT)

        loop(0, devices // batch, some, devices // batch)

    wait(sc_landed, core_got)
    for step in range(1, chips + 1):
        other = turned(chip, chips, step % chips, False)
        core_sum[other] = (
            grads[other * 2 + core].astype(F32) + core_got[other].astype(F32)
        ).astype(BF)
        if step < chips:
            sums_y(step, False).start()
    collect(0)
    wait(small_landed, small_got.at[others])
    small_got[me] = small_part[own_lines(me), :]
    small_sum[own_lines(me), :] = jnp.sum(small_got[...], 0)
    loop(1, devices, lambda step: give_whole(step, False).start())
    for part in range(1, chunks - 1):
        collect(part)
    wait(sy_landed, chip_got.at[other_chips])
    total = core_sum[chip].astype(F32)
    for step in range(1, chips):
        total = total + chip_got[step].astype(F32)
    chip_sum[...] = total.astype(BF)
    for step in range(1, experts):
        sums_z(step, False).start()
    collect(chunks - 1)
    wait(sz_landed, z_got.at[other_experts])
    total = chip_sum[expert_here].astype(F32)
    for step in range(1, experts):
        total = total + z_got[step].astype(F32)
    first_grad[...] = total[: size.first]
    second_grad[:half, :] = total[size.first :, :LANES]
    second_grad[half:, :] = total[size.first :, LANES:]

    other_lines = pl.ds(0, (devices - 1) * small_got.shape[1])
    wait(whole_landed, small_sum.at[other_lines, :])
    wait(whole_sent, small_sum.at[other_lines, :])
    wait(small_sent, small_part.at[other_lines, :])
    wait(ask_sent, message.at[others])
    wait(row_sent, rows.at[:, others])
    wait(slot_sent, slots_out.at[:, others])
    wait(gz_sent, gathered.at[0, other_experts])
    wait(gy_sent, gathered.at[other_chips])
    wait(gc_sent, gathered.at[pl.ds(0, chips)])
    wait(sc_sent, core_got)
    wait(sy_sent, core_sum.at[other_chips])
    wait(sz_sent, chip_sum.at[other_experts])


def update(size, *refs):
    grads, state, results = refs[:3], refs[3:12], refs[12:]
    table_grad = grads[0][...]
    wide = jnp.concatenate(
        [table_grad[b * EMB : (b + 1) * EMB] for b in range(size.rows // KEYS)], 1
    )
    for index, grad in enumerate((wide, grads[1][...], grads[2][...])):
        rate = 0.3 if index == 0 else 0.15
        values = [ref[...] for ref in state[3 * index : 3 * index + 3]]
        for ref, value in zip(results[3 * index : 3 * index + 3], adamw(*values, grad, rate)):
            ref[...] = value


def shape(dims, dtype=F32):
    return jax.ShapeDtypeStruct(dims, dtype)


def call(kernel, outs, scratch, remote=None):
    vmem = pl.BlockSpec(memory_space=pltpu.VMEM)
    params = dict(vmem_limit_bytes=56 * 2**20)
    if remote is not None:
        params.update(collective_id=remote, has_side_effects=True)
    return lambda *args: pl.pallas_call(
        kernel,
        out_shape=outs,
        in_specs=[vmem] * len(args),
        out_specs=[vmem] * len(outs),
        scratch_shapes=scratch,
        compiler_params=pltpu.CompilerParams(**params),
    )(*args)


def local(
    size,
    dense_feats,
    picks,
    labels,
    label_mask,
    requests,
    table,
    table_m,
    table_v,
    first_w,
    first_m,
    first_v,
    second_w,
    second_m,
    second_v,
    small,
    small_m,
    small_v,
):
    devices, experts, groups = size.devices, size.experts, size.groups
    chips = groups // 2
    chunks = size.tokens // CHUNK
    dma = pltpu.SemaphoreType.DMA
    vm = pltpu.VMEM
    message = size.slots + LANES
    count = small.shape[0]
    lines = -(-(count + 1) // (devices * 8 * LANES)) * 8
    flat_lines = -(-count // LANES)
    exchange = vm((chunks, devices, EMB, LANES), BF)
    weights = vm((groups, experts, size.pack, HID), BF)
    of_chips = vm((chips, experts, size.pack, HID), BF)
    of_chip = vm((experts, size.pack, HID), BF)
    table_grad, first_grad, second_grad, flat = call(
        functools.partial(step_kernel, size),
        [
            shape((size.rows // KEYS * EMB, KEYS)),
            shape((size.first, HID)),
            shape((size.second, OUT)),
            shape((devices * lines, LANES)),
        ],
        [
            vm((devices, 1, message), jnp.int32),
            vm((devices, 1, message), jnp.int32),
            vm((size.rows // KEYS * EMB, KEYS), BF),
        ]
        + [exchange] * 4
        + [weights, weights, of_chips, of_chips, of_chips, of_chip, of_chip]
        + [
            vm((LANES, LANES), F32),
            vm((16, LANES, LANES), F32),
            vm((INPUT + ONES, LANES), F32),
            vm((16, INPUT), BF),
            vm((TASKS * (OUT + 1) + 6, LANES), F32),
            vm((TASKS, OUT, TOWER), BF),
            vm((TASKS, TOWER, OUT), BF),
            vm((LANES, LANES), F32),
            vm((DOUT, 16), F32),
            vm((DOUT, size.tokens), BF),
            vm((devices * lines, LANES), F32),
            vm((devices, lines, LANES), F32),
            vm((experts, HID, INPUT), BF),
            vm((experts, HID, OUT), BF),
            vm((experts, OUT, HID), BF),
            vm((INPUT, experts * HID + LANES), BF),
            vm((16, size.tokens), F32),
            vm((32, size.tokens), BF),
            vm((devices // 2 * EMB, KEYS), BF),
            vm((devices // 2 * EMB, KEYS), BF),
            vm((FIELDS, KEYS, CHUNK), BF),
            vm((FIELDS, KEYS, CHUNK), BF),
            vm((FIELDS, KEYS, CHUNK), BF),
            vm((INPUT + ONES, CHUNK), BF),
            vm((INPUT + ONES, CHUNK), BF),
            vm((experts, HID, CHUNK), F32),
            vm((experts, OUT, CHUNK), F32),
            vm((experts, HID + ONES, CHUNK), BF),
            vm((experts, OUT, CHUNK), F32),
            vm((TASKS, OUT + ONES, CHUNK), BF),
            vm((experts * HID + LANES, CHUNK), BF),
            vm((INPUT, CHUNK), F32),
            vm((INPUT, CHUNK), F32),
            vm((devices // 2 * EMB, KEYS), F32),
            vm((devices // 2 * EMB, KEYS), F32),
            vm((experts, INPUT + ONES, HID), F32),
            vm((experts, HID + ONES, OUT), F32),
            vm((16, INPUT + LANES), F32),
            vm((16, LANES), F32),
            vm((TASKS, OUT + ONES, TOWER), F32),
            vm((TASKS, 8, LANES), F32),
            vm((1, CHUNK), F32),
        ]
        + [dma, dma, dma, dma((chunks,)), dma, dma((chunks,))]
        + [dma] * 5
        + [dma((experts,))]
        + [dma] * 10,
        0,
    )(
        requests[0],
        picks.T,
        dense_feats.T,
        labels.T,
        label_mask.T,
        table.T,
        first_w[0],
        second_w[0],
        jnp.pad(small, (0, flat_lines * LANES - count)).reshape(flat_lines, LANES),
    )
    tables = (table.T, table_m.T, table_v.T)
    firsts = (first_w[0], first_m[0], first_v[0])
    seconds = (second_w[0], second_m[0], second_v[0])
    new = call(
        functools.partial(update, size),
        [shape(a.shape) for a in tables + firsts + seconds],
        [],
    )(table_grad, first_grad, second_grad, *tables, *firsts, *seconds)
    flat = flat.reshape(-1)
    new_small = adamw(small, small_m, small_v, flat[:count], 0.15)
    return (
        (flat[count],)
        + tuple(a.T for a in new[:3])
        + tuple(a[None] for a in new[3:])
        + tuple(new_small)
    )


def solution(mesh):
    both = P(("batch", "expert"), None)
    shard = P("expert", "batch", None)
    ins = (both,) * 4 + (P(("batch", "expert"), None, None, None),) + (both,) * 3
    ins = ins + (shard,) * 6 + (P(),) * 3

    def step(*args):
        devices = mesh.shape["batch"] * mesh.shape["expert"]
        size = sizes_of(
            mesh, args[0].shape[0] // devices, args[4].shape[-1], args[5].shape[0] // devices
        )
        return jax.shard_map(
            functools.partial(local, size) if fits(size) else plain,
            mesh=mesh,
            in_specs=ins,
            out_specs=(P(),) + (both,) * 3 + (shard,) * 6 + (P(),) * 3,
            check_vma=False,
        )(*args)

    return step
```

```python
import collections
import functools

import jax
import jax.numpy as jnp
from jax import lax
from jax.experimental import pallas as pl
from jax.experimental.pallas import tpu as pltpu
from jax.sharding import PartitionSpec as P

FIELDS = 26
EMB = 16
DENSE = 13
DOUT = 96
HID = 256
OUT = 128
TOWER = 64
TASKS = 2
STEP = 5
GROUP_TOK = 64
INPUT = 512


HI = lax.Precision.HIGHEST


def unpack(flat, experts):
    shapes = [
        (experts, HID),
        (experts, OUT),
        (DENSE + 1, DOUT),
        (INPUT + 1, TASKS * experts),
        (TASKS, OUT + 1, TOWER),
        (TASKS, TOWER + 1),
    ]
    parts = []
    offset = 0
    for shape in shapes:
        length = 1
        for extent in shape:
            length = length * extent
        parts.append(flat[offset : offset + length].reshape(shape))
        offset = offset + length
    return parts


def adamw(weight, first, second, grad, rate):
    first = 0.9 * first + 0.1 * grad
    second = 0.999 * second + 0.001 * grad * grad
    fix_one = 1.0 - 0.9**STEP
    fix_two = 1.0 - 0.999**STEP
    weight = weight - rate * (
        first / fix_one / (jnp.sqrt(second / fix_two) + 1e-08) + 0.01 * weight
    )
    return (weight, first, second)


def silu_slope(value):
    sig = jax.nn.sigmoid(value)
    return sig * (1.0 + value * (1.0 - sig))


def split_three(values):
    upper = values.astype(jnp.bfloat16)
    rest = values - upper.astype(jnp.float32)
    middle = rest.astype(jnp.bfloat16)
    lower_part = (rest - middle.astype(jnp.float32)).astype(jnp.bfloat16)
    return jnp.concatenate([upper, middle, lower_part], -1)


def join_three(values):
    return values[:, :EMB] + values[:, EMB : 2 * EMB] + values[:, 2 * EMB :]


def one_hot(index, extent):
    return (index[:, None] == jnp.arange(extent, dtype=jnp.int32)[None, :]).astype(jnp.bfloat16)


def pick_rows(index, source):
    return jnp.dot(
        one_hot(index, source.shape[0]), source, preferred_element_type=jnp.float32
    ).astype(jnp.bfloat16)


def add_rows(index, values, extent):
    spread = lax.dot_general(
        one_hot(index, extent),
        split_three(values),
        (((0,), (0,)), ((), ())),
        preferred_element_type=jnp.float32,
    )
    return join_three(spread)


def expert_forward(inputs, first_w, second_w, first_b, second_b):
    pre_one = (
        jnp.einsum("ti,eih->teh", inputs, first_w, preferred_element_type=jnp.float32)
        + first_b[None]
    )
    hidden = jax.nn.silu(pre_one).astype(jnp.bfloat16)
    pre_two = (
        jnp.einsum("teh,eho->teo", hidden, second_w, preferred_element_type=jnp.float32)
        + second_b[None]
    )
    return (pre_one, hidden, pre_two, jax.nn.silu(pre_two))


def expert_backward(inputs, first_w, second_w, pre_one, hidden, pre_two, d_out):
    d_two = (silu_slope(pre_two) * d_out).astype(jnp.bfloat16)
    d_second_w = jnp.einsum("teh,teo->eho", hidden, d_two, preferred_element_type=jnp.float32)
    d_second_b = jnp.sum(d_two, 0, dtype=jnp.float32)
    d_hidden = jnp.einsum("teo,eho->teh", d_two, second_w, preferred_element_type=jnp.float32)
    d_one = (silu_slope(pre_one) * d_hidden).astype(jnp.bfloat16)
    d_first_w = jnp.einsum("ti,teh->eih", inputs, d_one, preferred_element_type=jnp.float32)
    d_first_b = jnp.sum(d_one, 0, dtype=jnp.float32)
    d_inputs = jnp.einsum("teh,eih->ti", d_one, first_w, preferred_element_type=jnp.float32)
    return (d_first_w, d_second_w, d_first_b, d_second_b, d_inputs)


def plain(
    dense_feats,
    picks,
    labels,
    label_mask,
    requests,
    table,
    table_m,
    table_v,
    first_w,
    first_m,
    first_v,
    second_w,
    second_m,
    second_v,
    small,
    small_m,
    small_v,
):
    groups = lax.axis_size("batch")
    experts = lax.axis_size("expert")
    devices = groups * experts
    expert_idx = lax.axis_index("expert")
    tokens = dense_feats.shape[0]
    slots = requests.shape[-1]
    rows_dev = table.shape[0]
    tok_groups = tokens // GROUP_TOK
    sub_slots = slots // tok_groups
    group_slots = devices * sub_slots
    total_asked = devices * slots
    ask_block = min(1024, total_asked)
    bias_one, bias_two, dense_w, gate_w, tower_w, head_w = unpack(small, experts)
    first_full, second_full = (
        lax.all_gather(first_w.astype(jnp.bfloat16), "batch", axis=1, tiled=True),
        lax.all_gather(second_w.astype(jnp.bfloat16), "batch", axis=1, tiled=True),
    )
    asked = lax.all_to_all(
        lax.all_to_all(requests[0], "batch", split_axis=0, concat_axis=0, tiled=True),
        "expert",
        split_axis=1,
        concat_axis=1,
        tiled=True,
    )
    asked_blocks = asked.reshape(total_asked // ask_block, ask_block)
    table_low = table.astype(jnp.bfloat16)
    sent_rows = lax.map(lambda index: pick_rows(index, table_low), asked_blocks)
    sent_rows = sent_rows.reshape(groups, experts, slots * EMB)
    got_rows = lax.all_to_all(
        lax.all_to_all(sent_rows, "batch", split_axis=0, concat_axis=0, tiled=True),
        "expert",
        split_axis=1,
        concat_axis=1,
        tiled=True,
    )
    by_group = (
        got_rows.reshape(devices, tok_groups, sub_slots, EMB)
        .transpose(1, 0, 2, 3)
        .reshape(tok_groups, group_slots, EMB)
    )
    local_pick = (picks // slots * sub_slots + picks % sub_slots).reshape(
        tok_groups, GROUP_TOK * FIELDS
    )
    emb = lax.map(lambda item: pick_rows(item[0], item[1]), (local_pick, by_group)).reshape(
        tokens, FIELDS * EMB
    )
    dense_proj = jnp.dot(dense_feats, dense_w[:DENSE], precision=HI) + dense_w[DENSE]
    inputs = jnp.concatenate([emb, dense_proj.astype(jnp.bfloat16)], 1)
    gate_low = gate_w[:INPUT].astype(jnp.bfloat16)
    gate_logits = jnp.dot(inputs, gate_low, preferred_element_type=jnp.float32) + gate_w[INPUT]
    probs = jax.nn.softmax(gate_logits.reshape(tokens, TASKS, experts), axis=-1)
    gates = probs.astype(jnp.bfloat16)
    all_inputs, all_gates = (
        lax.all_gather(inputs, "expert", axis=0, tiled=True),
        lax.all_gather(gates.reshape(tokens, TASKS * experts), "expert", axis=0, tiled=True),
    )
    own_gates = lax.dynamic_slice_in_dim(
        all_gates.reshape(-1, TASKS, experts), expert_idx, 1, 2
    ).astype(jnp.float32)
    first_use, second_use = (first_full, second_full)
    first_b = lax.dynamic_slice_in_dim(bias_one, expert_idx, 1, 0)
    second_b = lax.dynamic_slice_in_dim(bias_two, expert_idx, 1, 0)
    pre_one, hidden, pre_two, expert_out = expert_forward(
        all_inputs, first_use, second_use, first_b, second_b
    )
    terms = jnp.einsum("tke,teo->tko", own_gates, expert_out, precision=HI).reshape(-1, TASKS * OUT)
    mixed = lax.psum_scatter(terms.astype(jnp.bfloat16), "expert", scatter_dimension=0, tiled=True)
    mask = label_mask.astype(jnp.float32)
    target = labels.astype(jnp.float32)
    counts = jnp.maximum(lax.psum(jnp.sum(mask, 0), ("batch", "expert")), 1.0)
    mixed_low = mixed.reshape(tokens, TASKS, OUT)
    tower_low = tower_w[:, :OUT].astype(jnp.bfloat16)
    tower_pre = (
        jnp.einsum("tko,koh->tkh", mixed_low, tower_low, preferred_element_type=jnp.float32)
        + tower_w[:, OUT][None]
    )
    tower_act = jax.nn.silu(tower_pre)
    logits = jnp.einsum("tkh,kh->tk", tower_act, head_w[:, :TOWER], precision=HI) + head_w[:, TOWER]
    loss_local = jnp.sum(mask * (jax.nn.softplus(logits) - target * logits) / counts)
    d_logits = mask * (jax.nn.sigmoid(logits) - target) / counts
    d_head = jnp.concatenate(
        [
            jnp.einsum("tkh,tk->kh", tower_act, d_logits, precision=HI),
            jnp.sum(d_logits, 0)[:, None],
        ],
        1,
    )
    d_act = d_logits[:, :, None] * head_w[None, :, :TOWER]
    d_tower_pre = (silu_slope(tower_pre) * d_act).astype(jnp.bfloat16)
    d_tower = jnp.concatenate(
        [
            jnp.einsum("tko,tkh->koh", mixed_low, d_tower_pre, preferred_element_type=jnp.float32),
            jnp.sum(d_tower_pre, 0, dtype=jnp.float32)[:, None, :],
        ],
        1,
    )
    d_mixed = jnp.einsum(
        "tkh,koh->tko", d_tower_pre, tower_low, preferred_element_type=jnp.float32
    ).astype(jnp.bfloat16)
    all_d_mixed = (
        lax.all_gather(d_mixed.reshape(tokens, TASKS * OUT), "expert", axis=0, tiled=True)
        .reshape(-1, TASKS, OUT)
        .astype(jnp.float32)
    )
    d_out = jnp.einsum("tke,tko->teo", own_gates, all_d_mixed, precision=HI)
    d_gate_col = jnp.einsum("teo,tko->tke", expert_out, all_d_mixed, precision=HI)
    d_first_w, d_second_w, d_first_b, d_second_b, d_rows = expert_backward(
        all_inputs, first_use, second_use, pre_one, hidden, pre_two, d_out
    )
    onehot = (jnp.arange(experts) == expert_idx).astype(jnp.float32)
    d_gate_full = (d_gate_col * onehot[None, None, :]).reshape(-1, TASKS * experts)
    d_inputs, d_gates = (
        lax.psum_scatter(
            d_rows.astype(jnp.bfloat16), "expert", scatter_dimension=0, tiled=True
        ).astype(jnp.float32),
        lax.psum_scatter(
            d_gate_full.astype(jnp.bfloat16), "expert", scatter_dimension=0, tiled=True
        ).astype(jnp.float32),
    )
    d_gates = d_gates.reshape(tokens, TASKS, experts)
    d_first_b = onehot[:, None] * d_first_b
    d_second_b = onehot[:, None] * d_second_b
    d_gate_logits = (
        (probs * (d_gates - jnp.sum(probs * d_gates, -1, keepdims=True)))
        .astype(jnp.bfloat16)
        .reshape(tokens, TASKS * experts)
    )
    d_gate_w = jnp.concatenate(
        [
            jnp.dot(inputs.T, d_gate_logits, preferred_element_type=jnp.float32),
            jnp.sum(d_gate_logits, 0, dtype=jnp.float32)[None],
        ],
        0,
    )
    d_x = d_inputs + jnp.dot(d_gate_logits, gate_low.T, preferred_element_type=jnp.float32)
    d_dense = d_x[:, FIELDS * EMB :]
    d_dense_w = jnp.concatenate(
        [jnp.dot(dense_feats.T, d_dense, precision=HI), jnp.sum(d_dense, 0)[None]], 0
    )
    d_emb = d_x[:, : FIELDS * EMB].reshape(tok_groups, GROUP_TOK * FIELDS, EMB)
    slot_grads = lax.map(lambda item: add_rows(item[0], item[1], group_slots), (local_pick, d_emb))
    slot_grads = (
        slot_grads.reshape(tok_groups, devices, sub_slots, EMB)
        .transpose(1, 0, 2, 3)
        .reshape(groups, experts, slots * EMB)
    )
    owner_grads = lax.all_to_all(
        lax.all_to_all(
            slot_grads.astype(jnp.bfloat16), "batch", split_axis=0, concat_axis=0, tiled=True
        ),
        "expert",
        split_axis=1,
        concat_axis=1,
        tiled=True,
    ).astype(slot_grads.dtype)
    owner_blocks = owner_grads.reshape(total_asked // ask_block, ask_block, EMB)

    def add_block(total, item):
        return (total + add_rows(item[0], item[1], rows_dev), None)

    table_grad, unused = lax.scan(
        add_block, jnp.zeros((rows_dev, EMB), jnp.float32), (asked_blocks, owner_blocks)
    )
    grad_first, grad_second = (
        lax.psum_scatter(
            d_first_w.astype(jnp.bfloat16), "batch", scatter_dimension=1, tiled=True
        ).astype(jnp.float32),
        lax.psum_scatter(
            d_second_w.astype(jnp.bfloat16), "batch", scatter_dimension=1, tiled=True
        ).astype(jnp.float32),
    )
    flat_grads = jnp.concatenate(
        [
            d_first_b.reshape(-1),
            d_second_b.reshape(-1),
            d_dense_w.reshape(-1),
            d_gate_w.reshape(-1),
            d_tower.reshape(-1),
            d_head.reshape(-1),
        ]
    )
    grad_small, loss = lax.psum((flat_grads, loss_local), ("batch", "expert"))
    new_table, new_table_m, new_table_v = adamw(table, table_m, table_v, table_grad, 0.3)
    new_first, new_first_m, new_first_v = adamw(first_w, first_m, first_v, grad_first, 0.15)
    new_second, new_second_m, new_second_v = adamw(second_w, second_m, second_v, grad_second, 0.15)
    new_small, new_small_m, new_small_v = adamw(small, small_m, small_v, grad_small, 0.15)
    return (
        loss,
        new_table,
        new_table_m,
        new_table_v,
        new_first,
        new_first_m,
        new_first_v,
        new_second,
        new_second_m,
        new_second_v,
        new_small,
        new_small_m,
        new_small_v,
    )


MESH = pl.DeviceIdType.MESH
BF = jnp.bfloat16
F32 = jnp.float32
NN = (((1,), (0,)), ((), ()))
NT = (((1,), (1,)), ((), ()))
KEYS = 256
CHUNK = 256
LANES = 128
ONES = 16

Sizes = collections.namedtuple(
    "Sizes",
    (
        "groups",
        "experts",
        "devices",
        "slots",
        "rows",
        "tokens",
        "first",
        "second",
        "pack",
        "span",
    ),
)


def sizes_of(mesh, tokens, slots, rows):
    groups = mesh.shape["batch"]
    experts = mesh.shape["expert"]
    first = INPUT // groups
    second = HID // groups
    span = tokens * LANES // slots
    return Sizes(
        groups,
        experts,
        groups * experts,
        slots,
        rows,
        tokens,
        first,
        second,
        first + second // 2,
        span,
    )


def fits(size):
    return (
        size.slots % LANES == 0
        and size.slots & (size.slots - 1) == 0
        and size.span == CHUNK
        and size.second % 32 == 0
        and size.first % 16 == 0
        and size.groups == 8
        and size.devices % 2 == 0
        and size.rows % KEYS == 0
        and size.experts == 4
    )


def mm(left, right, dims=NN, precision=None):
    return lax.dot_general(left, right, dims, preferred_element_type=F32, precision=precision)


def here(size):
    group = lax.axis_index("batch")
    expert = lax.axis_index("expert")
    return group, expert, group * size.experts + expert


def place(size, device):
    return (lax.div(device, size.experts), lax.rem(device, size.experts))


def greet(size, me):
    barrier = pltpu.get_barrier_semaphore()

    def one(step, carry):
        peer = lax.rem(me + step, size.devices)
        pl.semaphore_signal(barrier, inc=1, device_id=place(size, peer), device_id_type=MESH)
        return carry

    lax.fori_loop(1, size.devices, one, 0)
    return barrier


def push(source, target, sent, landed, where):
    return pltpu.make_async_remote_copy(
        src_ref=source,
        dst_ref=target,
        send_sem=sent,
        recv_sem=landed,
        device_id=where,
        device_id_type=MESH,
    )


def spread(index, extent, width):
    return lax.broadcasted_iota(jnp.int32, (extent, width), 0) == index


def as_low(flag):
    return jnp.where(flag, 1.0, 0.0).astype(BF)


def look_up(cells, key, high, levels):
    found = mm(cells, as_low(spread(key, KEYS, key.shape[1])))
    result = found[:EMB]
    for level in range(1, levels):
        result = jnp.where(high == level, found[level * EMB : (level + 1) * EMB], result)
    return result


def levels_of(values, high, levels):
    return jnp.concatenate(
        [jnp.where(high == level, values, 0.0) for level in range(levels)], 0
    ).astype(BF)


def sigmoid(value):
    return 0.5 + 0.5 * jnp.tanh(0.5 * value)


def lanes_of(rows=1):
    return lax.broadcasted_iota(jnp.int32, (rows, LANES), 1)


def turn(values, shift):
    shift = shift % LANES
    return pltpu.roll(values, shift, 1) if shift else values


def take(flat, offset, count):
    row, shift = offset // LANES, offset % LANES
    if shift == 0:
        return flat[row : row + count, :]
    return jnp.where(
        lanes_of(count) < LANES - shift,
        turn(flat[row : row + count, :], -shift),
        turn(flat[row + 1 : row + 1 + count, :], -shift),
    )


def put(flat, offset, values):
    row, shift = offset // LANES, offset % LANES
    count = values.shape[0]
    moved = turn(values, shift)
    if shift == 0:
        flat[row : row + count, :] += moved
        return
    flat[row : row + count, :] += jnp.where(lanes_of(count) >= shift, moved, 0.0)
    flat[row + 1 : row + 1 + count, :] += jnp.where(lanes_of(count) < shift, moved, 0.0)


def offsets(experts):
    sizes = [
        experts * HID,
        experts * OUT,
        (DENSE + 1) * DOUT,
        (INPUT + 1) * TASKS * experts,
        TASKS * (OUT + 1) * TOWER,
        TASKS * (TOWER + 1),
    ]
    return [sum(sizes[:index]) for index in range(len(sizes) + 1)]


def step_kernel(
    size,
    requests,
    picks,
    dense,
    labels,
    mask,
    table,
    first,
    second,
    small,
    table_grad,
    first_grad,
    second_grad,
    small_sum,
    message,
    asked,
    cells,
    rows,
    got,
    slots_out,
    slots_got,
    gathered,
    grads,
    core_got,
    core_sum,
    chip_got,
    chip_sum,
    z_got,
    vectors,
    columns,
    gate_rows,
    gate_t,
    tower_rows,
    tower_n,
    tower_t,
    dense_rows,
    dense_w,
    dense_low,
    small_part,
    small_got,
    first_t,
    second_n,
    second_t,
    wide,
    feats,
    feats_low,
    slot_cells_a,
    slot_cells_b,
    chosen_a,
    chosen_b,
    chosen_c,
    inputs_a,
    inputs_b,
    slope_one,
    slope_two,
    hidden,
    outs,
    mixes,
    deltas,
    d_inputs_a,
    d_inputs_b,
    slot_sum_a,
    slot_sum_b,
    sum_first,
    sum_second,
    sum_gate,
    sum_dense,
    sum_tower,
    sum_head,
    loss_sum,
    ask_sent,
    ask_landed,
    row_sent,
    row_landed,
    slot_sent,
    slot_landed,
    small_sent,
    small_landed,
    whole_sent,
    whole_landed,
    gz_sent,
    gz_landed,
    gy_sent,
    gx_landed,
    gy_landed,
    gd_landed,
    gc_sent,
    gc_landed,
    sz_sent,
    sz_landed,
    sy_sent,
    sy_landed,
    sc_sent,
    sc_landed,
):
    group, expert_here, me = here(size)
    slots, devices, experts = size.slots, size.devices, size.experts
    chips = size.groups // 2
    chip, core = lax.div(group, 2), lax.rem(group, 2)
    blocks = size.rows // KEYS
    half = size.second // 2
    levels = devices // 2
    shift = slots.bit_length() - 1
    chunks = size.tokens // CHUNK
    gates_wide = TASKS * experts
    at_one, at_two, at_dense, at_gate, at_tower, at_head, at_loss = offsets(experts)
    lane = lanes_of()
    barrier = greet(size, me)
    slot_cells = (slot_cells_a, slot_cells_b)
    chosen = (chosen_a, chosen_b, chosen_c)
    inputs = (inputs_a, inputs_b)
    d_inputs = (d_inputs_a, d_inputs_b)
    slot_sum = (slot_sum_a, slot_sum_b)

    def own_lines(device):
        count = small_got.shape[1]
        return pl.ds(pl.multiple_of(device * count, count), count)

    def to_all(source, target, sent, landed, step, receive):
        peer = lax.rem(me + (devices - step if receive else step), devices)
        return push(
            source(peer),
            target(peer if receive else me),
            sent,
            landed,
            place(size, peer),
        )

    def ask(step, receive):
        return to_all(
            lambda p: message.at[p], lambda p: asked.at[p], ask_sent, ask_landed, step, receive
        )

    def answer(part, step, receive):
        peer = lax.rem(me + (step if receive else devices - step), devices)
        return push(
            rows.at[part, peer],
            got.at[part, peer if receive else me],
            row_sent,
            row_landed.at[part],
            place(size, peer),
        )

    def give_slots(part, step, receive):
        return to_all(
            lambda p: slots_out.at[part, p],
            lambda p: slots_got.at[part, p],
            slot_sent,
            slot_landed.at[part],
            step,
            receive,
        )

    def give_small(step, receive):
        return to_all(
            lambda p: small_part.at[own_lines(p), :],
            lambda p: small_got.at[p],
            small_sent,
            small_landed,
            step,
            receive,
        )

    def give_whole(step, receive):
        return to_all(
            lambda p: small_sum.at[own_lines(me), :],
            lambda p: small_sum.at[own_lines(p), :],
            whole_sent,
            whole_landed,
            step,
            receive,
        )

    def turned(index, count, step, receive):
        return lax.rem(index + (count - step if receive else step), count)

    def source_at(step):
        return turned(expert_here, experts, step, True)

    def weights_z(step):
        other = turned(expert_here, experts, step, False)
        block = gathered.at[group, expert_here]
        return push(block, block, gz_sent, gz_landed.at[step], (group, other))

    beside_x = chip + 1 - 2 * lax.rem(chip, 2)
    beside_y = lax.rem(chip + 2, 4)
    across_both = lax.rem(beside_x + 2, 4)

    def weights_x(step, owner):
        block = gathered.at[owner * 2 + core, source_at(step)]
        landed = (gx_landed if owner is chip else gd_landed).at[step]
        return push(block, block, gy_sent, landed, (beside_x * 2 + core, expert_here))

    def weights_y(step, owner):
        block = gathered.at[owner * 2 + core, source_at(step)]
        landed = (gy_landed if owner is chip else gd_landed).at[step]
        return push(block, block, gy_sent, landed, (beside_y * 2 + core, expert_here))

    def spread_weights(step):
        weights_x(step, chip).start()
        weights_y(step, chip).start()

    def forward_weights(step):
        wait(gx_landed.at[step], gathered.at[0, 0])
        wait(gy_landed.at[step], gathered.at[0, 0])
        if step % 2 == 0:
            weights_y(step, beside_x).start()
        else:
            weights_x(step, beside_y).start()

    def weights_c(owner):
        block = gathered.at[owner * 2 + core]
        return push(
            block, block, gc_sent, gc_landed, (chip * 2 + 1 - core, expert_here)
        )

    def expert_at(turn_no):
        return turned(expert_here, experts, turn_no + 1, False)

    def sums_c(turn_no, step):
        expert = expert_at(turn_no)
        other = turned(chip, chips, step, False)
        return push(
            grads.at[other * 2 + 1 - core, expert],
            core_got.at[expert, other],
            sc_sent,
            sc_landed.at[turn_no],
            (chip * 2 + 1 - core, expert_here),
        )

    def sums_y(turn_no, step):
        expert = expert_at(turn_no)
        other = turned(chip, chips, step, False)
        return push(
            core_sum.at[expert, other],
            chip_got.at[expert, step],
            sy_sent,
            sy_landed.at[turn_no],
            (other * 2 + core, expert_here),
        )

    def sums_z(turn_no):
        expert = expert_at(turn_no)
        return push(
            chip_sum.at[expert], z_got.at[turn_no], sz_sent, sz_landed, (group, expert)
        )

    def wait(semaphore, block):
        pltpu.make_async_copy(block, block, semaphore).wait()

    others = pl.ds(0, devices - 1)
    other_chips = pl.ds(0, chips - 1)
    other_experts = pl.ds(0, experts - 1)

    def loop(begin, end, body, unroll=1):
        def one(step, carry):
            body(step)
            return carry

        lax.fori_loop(begin, end, one, 0, unroll=unroll)

    valid = mask[...].astype(F32)
    count = jnp.where(
        lane == 0,
        jnp.sum(valid[0:1], 1, keepdims=True),
        jnp.where(lane == 1, jnp.sum(valid[1:2], 1, keepdims=True), 0.0),
    ).astype(jnp.int32)
    for part in range(size.groups):
        for one in range(experts):
            peer = part * experts + one
            message[peer, :, :slots] = requests[part, one : one + 1, :]
            message[peer, :, slots:] = count
    gathered[group, expert_here, : size.first, :] = first[...].astype(BF)
    gathered[group, expert_here, size.first :, :LANES] = second[:half].astype(BF)
    gathered[group, expert_here, size.first :, LANES:] = second[half:].astype(BF)
    for block in range(blocks):
        cells[block * EMB : (block + 1) * EMB, :] = table[
            :, block * KEYS : (block + 1) * KEYS
        ].astype(BF)
    pl.semaphore_wait(barrier, devices - 1)
    for step in range(1, experts):
        weights_z(step).start()
    spread_weights(0)
    loop(1, devices, lambda step: ask(step, False).start())

    vectors[...] = jnp.zeros_like(vectors)
    vectors[: at_dense // LANES, :] = small[: at_dense // LANES, :]
    lines = take(small, at_tower, TASKS * (OUT + 1) * TOWER // LANES)
    count_rows = lines.shape[0]
    tower_rows[pl.ds(0, count_rows, stride=2), :] = lines
    tower_rows[pl.ds(1, count_rows, stride=2), :] = turn(lines, TOWER)
    for task in range(TASKS):
        base = task * (OUT + 1)
        block = tower_rows[base : base + OUT, :]
        tower_n[task] = block[:, :TOWER].astype(BF)
        tower_t[task] = block.T[:TOWER].astype(BF)
    last = [tower_rows[k * (OUT + 1) + OUT : (k + 1) * (OUT + 1), :] for k in range(TASKS)]
    vectors[12:13, :] = jnp.where(lane < TOWER, last[0], turn(last[1], TOWER))
    heads = [take(small, at_head, 1)]
    end = at_head + TOWER + 1
    heads.append(turn(small[end // LANES : end // LANES + 1, :], -(end % LANES)))
    vectors[13:14, :] = jnp.where(lane < TOWER, heads[0], turn(heads[1], TOWER))
    vectors[15:16, :] = jnp.where(lane == 0, turn(heads[0], -TOWER), turn(heads[1], 1 - TOWER))
    per_line = LANES // gates_wide
    lines = take(small, at_gate, INPUT // per_line + 1)
    for spot in range(per_line):
        gate_rows[pl.ds(spot, lines.shape[0], stride=per_line), :] = jnp.where(
            lanes_of(lines.shape[0]) < gates_wide, turn(lines, -spot * gates_wide), 0.0
        )
    for block in range(INPUT // LANES):
        piece = gate_rows[block * LANES : (block + 1) * LANES, :]
        gate_t[:, block * LANES : (block + 1) * LANES] = piece.T[:16].astype(BF)
        wide[block * LANES : (block + 1) * LANES, experts * HID :] = piece.astype(BF)
    vectors[14:15, :] = gate_rows[INPUT : INPUT + 1, :]
    dense_rows[...] = jnp.zeros_like(dense_rows)
    for line in range(DENSE + 1):
        dense_rows[line : line + 1, :] = take(small, at_dense + line * DOUT, 1)
    dense_w[...] = dense_rows[...].T[:DOUT, :16]
    flipped = vectors[...].T
    for column in range(16):
        columns[column] = jnp.broadcast_to(flipped[:, column : column + 1], (LANES, LANES))
    feats[...] = jnp.ones_like(feats)
    feats[:DENSE, :] = dense[...]
    upper = feats[...].astype(BF)
    feats_low[:16, :] = upper
    feats_low[16:, :] = (feats[...] - upper.astype(F32)).astype(BF)
    dense_low[...] = mm(dense_w[...], feats[...], precision=HI).astype(BF)
    for buffer in inputs:
        buffer[INPUT:, :] = jnp.ones((ONES, CHUNK), BF)
    for expert in range(experts):
        hidden[expert, HID:, :] = jnp.ones((ONES, CHUNK), BF)
    for task in range(TASKS):
        mixes[task, OUT:, :] = jnp.ones((ONES, CHUNK), BF)
    deltas[experts * HID :, :] = jnp.zeros((LANES, CHUNK), BF)
    for total in (sum_gate, loss_sum, small_part, table_grad):
        total[...] = jnp.zeros_like(total)

    asked[me] = message[me]
    batch = 4

    def serve(part):
        columns_here = pl.ds(part * LANES, LANES)

        def some(turn_no, own):
            steps = [turn_no * batch + i for i in range(batch)]
            peers = [lax.rem(me + devices - step, devices) for step in steps]
            index = jnp.concatenate([asked[peer, :, columns_here] for peer in peers], 1)
            found = look_up(cells[...], index & (KEYS - 1), index >> 8, blocks).astype(BF)
            for i, peer in enumerate(peers):
                piece = found[:, i * LANES : (i + 1) * LANES]
                if own and i == 0:
                    got[part, peer] = piece
                else:
                    rows[part, peer] = piece
                    if part == 0:
                        answer(part, steps[i], False).start()

        some(0, True)
        loop(1, devices // batch, lambda turn_no: some(turn_no, False), devices // batch - 1)

    def send_rows(part):
        loop(1, devices, lambda step: answer(part, step, False).start())

    forward_weights(0)
    wait(ask_landed, asked.at[others])
    for step in range(1, experts):
        wait(gz_landed.at[step], gathered.at[0, 0])
        spread_weights(step)
    weights_c(chip).start()
    total = jnp.zeros((1, LANES), jnp.int32)
    for peer in range(devices):
        total = total + asked[peer, :, slots:]
    totals = jnp.maximum(total.astype(F32), 1.0)
    serve(0)
    serve(1)
    for step in range(1, experts):
        forward_weights(step)
    weights_c(beside_x).start()
    weights_c(beside_y).start()
    send_rows(1)
    for part in range(2, chunks):
        serve(part)
    for step in range(experts):
        wait(gd_landed.at[step], gathered.at[0, 0])
    weights_c(across_both).start()
    for part in range(2, chunks):
        send_rows(part)

    def column(index, begin=0, end=LANES):
        block = columns[index, begin:end, :]
        return jnp.concatenate([block] * (CHUNK // LANES), 1)

    def tokens_of(part):
        return slice(part * CHUNK, (part + 1) * CHUNK)

    def split(part, field):
        index = picks[field : field + 1, tokens_of(part)]
        owner = index >> shift
        return (owner & 1) * LANES + (index & (LANES - 1)), owner >> 1

    def fetch(part):
        wait(row_landed.at[part], got.at[part, others])
        for owner in range(devices):
            level, lower = owner // 2, owner % 2
            slot_cells[part % 2][
                level * EMB : (level + 1) * EMB, lower * LANES : (lower + 1) * LANES
            ] = got[part, owner]
        inputs[part % 2][FIELDS * EMB : INPUT, :] = dense_low[:, tokens_of(part)]

    def pick(part, field):
        key, high = split(part, field)
        flags = as_low(spread(key, KEYS, CHUNK))
        chosen[part % 3][field] = flags
        found = mm(slot_cells[part % 2][...], flags)
        result = found[:EMB]
        for level in range(1, levels):
            result = jnp.where(high == level, found[level * EMB : (level + 1) * EMB], result)
        inputs[part % 2][field * EMB : (field + 1) * EMB, :] = result.astype(BF)

    def give(part, field, first_time):
        places, flags = [], []
        for one in (field, field + 1):
            key, high = split(part, one)
            values = d_inputs[part % 2][one * EMB : (one + 1) * EMB, :]
            places.append(levels_of(values, high, levels))
            flags.append(chosen[part % 3][one])
        sums = mm(jnp.concatenate(places, 1), jnp.concatenate(flags, 1), NT)
        if first_time:
            slot_sum[part % 2][...] = sums
        else:
            slot_sum[part % 2][...] += sums

    def picks_of(part):
        return [functools.partial(pick, part, field) for field in range(FIELDS)]

    def gives_of(part):
        return [
            functools.partial(give, part, field, field == 0) for field in range(0, FIELDS, 2)
        ]

    def send_slots(part):
        for owner in range(devices):
            level, lower = owner // 2, owner % 2
            slots_out[part, owner] = slot_sum[part % 2][
                level * EMB : (level + 1) * EMB, lower * LANES : (lower + 1) * LANES
            ].astype(BF)
        loop(1, devices, lambda hop: give_slots(part, hop, False).start())
        slots_got[part, me] = slots_out[part, me]

    def train(part):
        here_tokens = tokens_of(part)
        first_time = part == 0
        whole_x = inputs[part % 2]

        def add(total, value):
            if first_time:
                total[...] = value
            else:
                total[...] += value

        x = whole_x[:INPUT, :]
        logits = mm(gate_t[...], x)[:gates_wide] + column(14, 0, gates_wide)
        probs, gates = [], []
        for task in range(TASKS):
            line = [logits[task * experts + e : task * experts + e + 1] for e in range(experts)]
            top = functools.reduce(jnp.maximum, line)
            powers = [jnp.exp(item - top) for item in line]
            whole = 1.0 / functools.reduce(jnp.add, powers)
            probs.append([item * whole for item in powers])
            gates.append([item.astype(BF).astype(F32) for item in probs[-1]])
        yield
        mixed = [None] * TASKS
        for expert in range(experts):
            pre = mm(first_t[expert], x) + jnp.concatenate(
                [column(2 * expert), column(2 * expert + 1)], 0
            )
            sig = sigmoid(pre)
            act = pre * sig
            slope_one[expert] = sig + act * (1.0 - sig)
            low = act.astype(BF)
            hidden[expert, :HID, :] = low
            yield
            pre = mm(second_t[expert], low) + column(8 + expert)
            sig = sigmoid(pre)
            act = pre * sig
            slope_two[expert] = sig + act * (1.0 - sig)
            outs[expert] = act
            for task in range(TASKS):
                term = gates[task][expert] * act
                mixed[task] = term if mixed[task] is None else mixed[task] + term
            yield
        d_mixed = []
        for task in range(TASKS):
            mix = mixed[task].astype(BF)
            mixes[task, :OUT, :] = mix
            low, high = task * TOWER, (task + 1) * TOWER
            pre = mm(tower_t[task], mix) + column(12, low, high)
            sig = sigmoid(pre)
            act = pre * sig
            head = column(13, low, high)
            logit = jnp.sum(act * head, 0, keepdims=True) + column(15, task, task + 1)
            scale = mask[task : task + 1, here_tokens].astype(F32) / totals[:, task : task + 1]
            target = labels[task : task + 1, here_tokens].astype(F32)
            soft = jnp.maximum(logit, 0.0) + jnp.log(1.0 + jnp.exp(-jnp.abs(logit)))
            loss_sum[...] += scale * (soft - target * logit)
            d_logit = scale * (sigmoid(logit) - target)
            yield
            d_pre = ((sig + act * (1.0 - sig)) * (d_logit * head)).astype(BF)
            d_upper = d_logit.astype(BF).astype(F32)
            d_both = jnp.concatenate(
                [
                    jnp.broadcast_to(d_upper, (8, CHUNK)),
                    jnp.broadcast_to(d_logit - d_upper, (8, CHUNK)),
                ],
                0,
            ).astype(BF)
            upper = act.astype(BF)
            rest = (act - upper.astype(F32)).astype(BF)
            ones = jnp.ones((16, CHUNK), BF)
            zeros = jnp.zeros((LANES - TOWER - 16, CHUNK), BF)
            both = mm(d_both, jnp.concatenate([upper, ones, zeros], 0), NT) + mm(
                d_both, jnp.concatenate([rest, zeros, jnp.zeros((16, CHUNK), BF)], 0), NT
            )
            add(sum_head.at[task], both[:8] + both[8:])
            add(sum_tower.at[task], mm(mixes[task], d_pre, NT))
            d_mixed.append(mm(tower_n[task], d_pre).astype(BF).astype(F32))
            yield
        d_gates = [[None] * experts for task in range(TASKS)]
        for expert in range(experts):
            d_out = gates[0][expert] * d_mixed[0] + gates[1][expert] * d_mixed[1]
            out = outs[expert]
            for task in range(TASKS):
                d_gates[task][expert] = jnp.sum(out * d_mixed[task], 0, keepdims=True)
            d_two = (slope_two[expert] * d_out).astype(BF)
            d_hidden = mm(second_n[expert], d_two)
            add(sum_second.at[expert], mm(hidden[expert], d_two, NT))
            yield
            d_one = (slope_one[expert] * d_hidden).astype(BF)
            deltas[expert * HID : (expert + 1) * HID, :] = d_one
            add(sum_first.at[expert], mm(whole_x[...], d_one, NT))
            yield
        lines = []
        for task in range(TASKS):
            inner = functools.reduce(
                jnp.add, [probs[task][e] * d_gates[task][e] for e in range(experts)]
            )
            lines += [probs[task][e] * (d_gates[task][e] - inner) for e in range(experts)]
        lines.append(jnp.zeros((16 - gates_wide, CHUNK), F32))
        d_gate = jnp.concatenate(lines, 0).astype(BF)
        deltas[experts * HID : experts * HID + 16, :] = d_gate
        add(sum_gate.at[:, : INPUT + ONES], mm(d_gate, whole_x[...], NT))
        yield
        d_x = mm(wide[...], deltas[...])
        d_inputs[part % 2][...] = d_x
        d_dense = d_x[INPUT - LANES :, :]
        upper = d_dense.astype(BF)
        rest = (d_dense - upper.astype(F32)).astype(BF)
        both = mm(feats_low[:, here_tokens], upper, NT)
        add(sum_dense, both[:16] + both[16:] + mm(feats_low[:16, here_tokens], rest, NT))
        yield

    stops = 2 + 2 * experts + 2 * TASKS + 2 * experts + 1

    def beside(main, jobs):
        jobs, done = list(jobs), 0
        for stop, _ in enumerate(main):
            until = len(jobs) * (stop + 1) // stops
            for job in jobs[done:until]:
                job()
            done = until
        for job in jobs[done:]:
            job()

    def mixed_jobs(*lists):
        spots = [
            ((index + 0.5) / len(jobs), job) for jobs in lists for index, job in enumerate(jobs)
        ]
        return [job for spot, job in sorted(spots, key=lambda pair: pair[0])]

    fetch(0)
    for job in picks_of(0):
        job()
    wait(gc_landed, gathered.at[pl.ds(0, chips)])
    for expert in range(experts):
        for part in range(size.groups):
            wide[
                part * size.first : (part + 1) * size.first, expert * HID : (expert + 1) * HID
            ] = gathered[part, expert, : size.first, :]
            base = part * size.second
            second_n[expert, base : base + half, :] = gathered[part, expert, size.first :, :LANES]
            second_n[expert, base + half : base + 2 * half, :] = gathered[
                part, expert, size.first :, LANES:
            ]
        first_t[expert] = wide[:, expert * HID : (expert + 1) * HID].T
        second_t[expert] = second_n[expert].T
    for part in range(chunks):
        jobs = []
        if part + 1 < chunks:
            fetch(part + 1)
            jobs.append(picks_of(part + 1))
        if part > 0:
            jobs.append(gives_of(part - 1))
        beside(train(part), mixed_jobs(*jobs))
        if 0 < part < chunks - 1:
            send_slots(part - 1)

    for turn_no in range(experts):
        expert = expert_at(turn_no)
        for part in range(size.groups):
            base = part * size.second
            grads[part, expert, : size.first, :] = sum_first[
                expert, part * size.first : (part + 1) * size.first, :
            ].astype(BF)
            grads[part, expert, size.first :, :LANES] = sum_second[
                expert, base : base + half, :
            ].astype(BF)
            grads[part, expert, size.first :, LANES:] = sum_second[
                expert, base + half : base + 2 * half, :
            ].astype(BF)
        for step in range(1, chips + 1):
            sums_c(turn_no, step % chips).start()
    for expert in range(experts):
        per = HID // LANES
        for piece in range(per):
            line = expert * per + piece
            small_part[line : line + 1, :] = sum_first[
                expert, INPUT : INPUT + 1, piece * LANES : (piece + 1) * LANES
            ]
        line = experts * per + expert
        small_part[line : line + 1, :] = sum_second[expert, HID : HID + 1, :]
    for line in range(DENSE + 1):
        values = jnp.where(lane < DOUT, turn(sum_dense[line : line + 1, :], DOUT - LANES), 0.0)
        put(small_part, at_dense + line * DOUT, values)
    fill = jnp.zeros((LANES - 16, LANES), F32)
    for block in range(INPUT // LANES):
        piece = jnp.concatenate([sum_gate[:, block * LANES : (block + 1) * LANES], fill], 0)
        gate_rows[block * LANES : (block + 1) * LANES, :] = piece.T
    gate_rows[INPUT:, :] = jnp.concatenate([sum_gate[:, INPUT:], fill], 0).T[:ONES]
    lines = INPUT // per_line + 1
    packed = jnp.zeros((lines, LANES), F32)
    for spot in range(per_line):
        packed = packed + turn(gate_rows[pl.ds(spot, lines, stride=per_line), :], spot * gates_wide)
    inside = lax.broadcasted_iota(jnp.int32, (lines, LANES), 0) < lines - 1
    put(
        small_part,
        at_gate,
        jnp.where(inside | (lanes_of(lines) < gates_wide), packed, 0.0),
    )
    tower_rows[...] = jnp.zeros_like(tower_rows)
    for task in range(TASKS):
        base = task * (OUT + 1)
        tower_rows[base : base + OUT + 1, :TOWER] = sum_tower[task, : OUT + 1, :]
    put(
        small_part,
        at_tower,
        tower_rows[pl.ds(0, count_rows, stride=2), :]
        + turn(tower_rows[pl.ds(1, count_rows, stride=2), :], TOWER),
    )
    for task in range(TASKS):
        put(
            small_part,
            at_head + task * (TOWER + 1),
            jnp.where(lane < TOWER + 1, sum_head[task, 0:1, :], 0.0),
        )
    whole_loss = jnp.sum(loss_sum[...], 1, keepdims=True)
    put(small_part, at_loss, jnp.where(lane == 0, whole_loss, 0.0))
    loop(1, devices, lambda step: give_small(step, False).start())
    for turn_no in range(experts):
        expert = expert_at(turn_no)
        wait(sc_landed.at[turn_no], core_got.at[expert])
        for step in range(1, chips + 1):
            other = turned(chip, chips, step % chips, False)
            core_sum[expert, other] = (
                grads[other * 2 + core, expert].astype(F32) + core_got[expert, other].astype(F32)
            ).astype(BF)
            if step < chips:
                sums_y(turn_no, step).start()
    send_slots(chunks - 2)
    for job in gives_of(chunks - 1):
        job()
    send_slots(chunks - 1)

    def collect(part):
        columns_here = pl.ds(part * LANES, LANES)
        wait(slot_landed.at[part], slots_got.at[part, others])

        def some(turn_no):
            steps = [turn_no * batch + i for i in range(batch)]
            peers = [lax.rem(me + devices - step, devices) for step in steps]
            index = jnp.concatenate([asked[peer, :, columns_here] for peer in peers], 1)
            values = jnp.concatenate([slots_got[part, peer] for peer in peers], 1).astype(F32)
            spots = as_low(spread(index & (KEYS - 1), KEYS, batch * LANES))
            table_grad[...] += mm(levels_of(values, index >> 8, blocks), spots, NT)

        loop(0, devices // batch, some, devices // batch)

    for part in range(chunks - 2):
        collect(part)
    for turn_no in range(experts):
        expert = expert_at(turn_no)
        wait(sy_landed.at[turn_no], chip_got.at[expert, other_chips])
        total = core_sum[expert, chip].astype(F32)
        for step in range(1, chips):
            total = total + chip_got[expert, step].astype(F32)
        if turn_no + 1 < experts:
            chip_sum[expert] = total.astype(BF)
            sums_z(turn_no).start()
        if turn_no == 0:
            wait(small_landed, small_got.at[others])
            small_got[me] = small_part[own_lines(me), :]
            small_sum[own_lines(me), :] = jnp.sum(small_got[...], 0)
            loop(1, devices, lambda step: give_whole(step, False).start())
    collect(chunks - 2)
    collect(chunks - 1)
    wait(sz_landed, z_got.at[other_experts])
    for turn_no in range(experts - 1):
        total = total + z_got[turn_no].astype(F32)
    first_grad[...] = total[: size.first]
    second_grad[:half, :] = total[size.first :, :LANES]
    second_grad[half:, :] = total[size.first :, LANES:]

    other_lines = pl.ds(0, (devices - 1) * small_got.shape[1])
    wait(whole_landed, small_sum.at[other_lines, :])
    wait(whole_sent, small_sum.at[other_lines, :])
    wait(small_sent, small_part.at[other_lines, :])
    wait(ask_sent, message.at[others])
    wait(row_sent, rows.at[:, others])
    wait(slot_sent, slots_out.at[:, others])
    wait(gz_sent, gathered.at[0, other_experts])
    wait(gy_sent, gathered.at[other_chips])
    wait(gc_sent, gathered.at[pl.ds(0, chips)])
    wait(sc_sent, core_got)
    wait(sy_sent, core_sum.at[:, other_chips])
    wait(sz_sent, chip_sum.at[other_experts])


def update(size, *refs):
    grads, state, results = refs[:3], refs[3:12], refs[12:]
    table_grad = grads[0][...]
    wide = jnp.concatenate(
        [table_grad[b * EMB : (b + 1) * EMB] for b in range(size.rows // KEYS)], 1
    )
    for index, grad in enumerate((wide, grads[1][...], grads[2][...])):
        rate = 0.3 if index == 0 else 0.15
        values = [ref[...] for ref in state[3 * index : 3 * index + 3]]
        for ref, value in zip(results[3 * index : 3 * index + 3], adamw(*values, grad, rate)):
            ref[...] = value


def shape(dims, dtype=F32):
    return jax.ShapeDtypeStruct(dims, dtype)


def call(kernel, outs, scratch, remote=None):
    vmem = pl.BlockSpec(memory_space=pltpu.VMEM)
    params = dict(vmem_limit_bytes=56 * 2**20)
    if remote is not None:
        params.update(collective_id=remote, has_side_effects=True)
    return lambda *args: pl.pallas_call(
        kernel,
        out_shape=outs,
        in_specs=[vmem] * len(args),
        out_specs=[vmem] * len(outs),
        scratch_shapes=scratch,
        compiler_params=pltpu.CompilerParams(**params),
    )(*args)


def local(
    size,
    dense_feats,
    picks,
    labels,
    label_mask,
    requests,
    table,
    table_m,
    table_v,
    first_w,
    first_m,
    first_v,
    second_w,
    second_m,
    second_v,
    small,
    small_m,
    small_v,
):
    devices, experts, groups = size.devices, size.experts, size.groups
    chips = groups // 2
    chunks = size.tokens // CHUNK
    dma = pltpu.SemaphoreType.DMA
    vm = pltpu.VMEM
    message = size.slots + LANES
    count = small.shape[0]
    lines = -(-(count + 1) // (devices * 8 * LANES)) * 8
    flat_lines = -(-count // LANES)
    exchange = vm((chunks, devices, EMB, LANES), BF)
    weights = vm((groups, experts, size.pack, HID), BF)
    of_chips = vm((experts, chips, size.pack, HID), BF)
    of_chip = vm((experts, size.pack, HID), BF)
    table_grad, first_grad, second_grad, flat = call(
        functools.partial(step_kernel, size),
        [
            shape((size.rows // KEYS * EMB, KEYS)),
            shape((size.first, HID)),
            shape((size.second, OUT)),
            shape((devices * lines, LANES)),
        ],
        [
            vm((devices, 1, message), jnp.int32),
            vm((devices, 1, message), jnp.int32),
            vm((size.rows // KEYS * EMB, KEYS), BF),
        ]
        + [exchange] * 4
        + [weights, weights, of_chips, of_chips, of_chips, of_chip, of_chip]
        + [
            vm((LANES, LANES), F32),
            vm((16, LANES, LANES), F32),
            vm((INPUT + ONES, LANES), F32),
            vm((16, INPUT), BF),
            vm((TASKS * (OUT + 1) + 6, LANES), F32),
            vm((TASKS, OUT, TOWER), BF),
            vm((TASKS, TOWER, OUT), BF),
            vm((LANES, LANES), F32),
            vm((DOUT, 16), F32),
            vm((DOUT, size.tokens), BF),
            vm((devices * lines, LANES), F32),
            vm((devices, lines, LANES), F32),
            vm((experts, HID, INPUT), BF),
            vm((experts, HID, OUT), BF),
            vm((experts, OUT, HID), BF),
            vm((INPUT, experts * HID + LANES), BF),
            vm((16, size.tokens), F32),
            vm((32, size.tokens), BF),
            vm((devices // 2 * EMB, KEYS), BF),
            vm((devices // 2 * EMB, KEYS), BF),
            vm((FIELDS, KEYS, CHUNK), BF),
            vm((FIELDS, KEYS, CHUNK), BF),
            vm((FIELDS, KEYS, CHUNK), BF),
            vm((INPUT + ONES, CHUNK), BF),
            vm((INPUT + ONES, CHUNK), BF),
            vm((experts, HID, CHUNK), F32),
            vm((experts, OUT, CHUNK), F32),
            vm((experts, HID + ONES, CHUNK), BF),
            vm((experts, OUT, CHUNK), F32),
            vm((TASKS, OUT + ONES, CHUNK), BF),
            vm((experts * HID + LANES, CHUNK), BF),
            vm((INPUT, CHUNK), F32),
            vm((INPUT, CHUNK), F32),
            vm((devices // 2 * EMB, KEYS), F32),
            vm((devices // 2 * EMB, KEYS), F32),
            vm((experts, INPUT + ONES, HID), F32),
            vm((experts, HID + ONES, OUT), F32),
            vm((16, INPUT + LANES), F32),
            vm((16, LANES), F32),
            vm((TASKS, OUT + ONES, TOWER), F32),
            vm((TASKS, 8, LANES), F32),
            vm((1, CHUNK), F32),
        ]
        + [dma, dma, dma, dma((chunks,)), dma, dma((chunks,))]
        + [dma] * 5
        + [dma((experts,)), dma, dma((experts,)), dma((experts,)), dma((experts,))]
        + [dma] * 5
        + [dma((experts,)), dma, dma((experts,))],
        0,
    )(
        requests[0],
        picks.T,
        dense_feats.T,
        labels.T,
        label_mask.T,
        table.T,
        first_w[0],
        second_w[0],
        jnp.pad(small, (0, flat_lines * LANES - count)).reshape(flat_lines, LANES),
    )
    tables = (table.T, table_m.T, table_v.T)
    firsts = (first_w[0], first_m[0], first_v[0])
    seconds = (second_w[0], second_m[0], second_v[0])
    new = call(
        functools.partial(update, size),
        [shape(a.shape) for a in tables + firsts + seconds],
        [],
    )(table_grad, first_grad, second_grad, *tables, *firsts, *seconds)
    flat = flat.reshape(-1)
    new_small = adamw(small, small_m, small_v, flat[:count], 0.15)
    return (
        (flat[count],)
        + tuple(a.T for a in new[:3])
        + tuple(a[None] for a in new[3:])
        + tuple(new_small)
    )


def solution(mesh):
    both = P(("batch", "expert"), None)
    shard = P("expert", "batch", None)
    ins = (both,) * 4 + (P(("batch", "expert"), None, None, None),) + (both,) * 3
    ins = ins + (shard,) * 6 + (P(),) * 3

    def step(*args):
        devices = mesh.shape["batch"] * mesh.shape["expert"]
        size = sizes_of(
            mesh, args[0].shape[0] // devices, args[4].shape[-1], args[5].shape[0] // devices
        )
        return jax.shard_map(
            functools.partial(local, size) if fits(size) else plain,
            mesh=mesh,
            in_specs=ins,
            out_specs=(P(),) + (both,) * 3 + (shard,) * 6 + (P(),) * 3,
            check_vma=False,
        )(*args)

    return step
```

```python
import collections
import functools

import jax
import jax.numpy as jnp
from jax import lax
from jax.experimental import pallas as pl
from jax.experimental.pallas import tpu as pltpu
from jax.sharding import PartitionSpec as P

FIELDS = 26
EMB = 16
DENSE = 13
DOUT = 96
HID = 256
OUT = 128
TOWER = 64
TASKS = 2
STEP = 5
GROUP_TOK = 64
INPUT = 512


HI = lax.Precision.HIGHEST


def unpack(flat, experts):
    shapes = [
        (experts, HID),
        (experts, OUT),
        (DENSE + 1, DOUT),
        (INPUT + 1, TASKS * experts),
        (TASKS, OUT + 1, TOWER),
        (TASKS, TOWER + 1),
    ]
    parts = []
    offset = 0
    for shape in shapes:
        length = 1
        for extent in shape:
            length = length * extent
        parts.append(flat[offset : offset + length].reshape(shape))
        offset = offset + length
    return parts


def adamw(weight, first, second, grad, rate):
    first = 0.9 * first + 0.1 * grad
    second = 0.999 * second + 0.001 * grad * grad
    fix_one = 1.0 - 0.9**STEP
    fix_two = 1.0 - 0.999**STEP
    weight = weight - rate * (
        first / fix_one / (jnp.sqrt(second / fix_two) + 1e-08) + 0.01 * weight
    )
    return (weight, first, second)


def silu_slope(value):
    sig = jax.nn.sigmoid(value)
    return sig * (1.0 + value * (1.0 - sig))


def split_three(values):
    upper = values.astype(jnp.bfloat16)
    rest = values - upper.astype(jnp.float32)
    middle = rest.astype(jnp.bfloat16)
    lower_part = (rest - middle.astype(jnp.float32)).astype(jnp.bfloat16)
    return jnp.concatenate([upper, middle, lower_part], -1)


def join_three(values):
    return values[:, :EMB] + values[:, EMB : 2 * EMB] + values[:, 2 * EMB :]


def one_hot(index, extent):
    return (index[:, None] == jnp.arange(extent, dtype=jnp.int32)[None, :]).astype(jnp.bfloat16)


def pick_rows(index, source):
    return jnp.dot(
        one_hot(index, source.shape[0]), source, preferred_element_type=jnp.float32
    ).astype(jnp.bfloat16)


def add_rows(index, values, extent):
    spread = lax.dot_general(
        one_hot(index, extent),
        split_three(values),
        (((0,), (0,)), ((), ())),
        preferred_element_type=jnp.float32,
    )
    return join_three(spread)


def expert_forward(inputs, first_w, second_w, first_b, second_b):
    pre_one = (
        jnp.einsum("ti,eih->teh", inputs, first_w, preferred_element_type=jnp.float32)
        + first_b[None]
    )
    hidden = jax.nn.silu(pre_one).astype(jnp.bfloat16)
    pre_two = (
        jnp.einsum("teh,eho->teo", hidden, second_w, preferred_element_type=jnp.float32)
        + second_b[None]
    )
    return (pre_one, hidden, pre_two, jax.nn.silu(pre_two))


def expert_backward(inputs, first_w, second_w, pre_one, hidden, pre_two, d_out):
    d_two = (silu_slope(pre_two) * d_out).astype(jnp.bfloat16)
    d_second_w = jnp.einsum("teh,teo->eho", hidden, d_two, preferred_element_type=jnp.float32)
    d_second_b = jnp.sum(d_two, 0, dtype=jnp.float32)
    d_hidden = jnp.einsum("teo,eho->teh", d_two, second_w, preferred_element_type=jnp.float32)
    d_one = (silu_slope(pre_one) * d_hidden).astype(jnp.bfloat16)
    d_first_w = jnp.einsum("ti,teh->eih", inputs, d_one, preferred_element_type=jnp.float32)
    d_first_b = jnp.sum(d_one, 0, dtype=jnp.float32)
    d_inputs = jnp.einsum("teh,eih->ti", d_one, first_w, preferred_element_type=jnp.float32)
    return (d_first_w, d_second_w, d_first_b, d_second_b, d_inputs)


def plain(
    dense_feats,
    picks,
    labels,
    label_mask,
    requests,
    table,
    table_m,
    table_v,
    first_w,
    first_m,
    first_v,
    second_w,
    second_m,
    second_v,
    small,
    small_m,
    small_v,
):
    groups = lax.axis_size("batch")
    experts = lax.axis_size("expert")
    devices = groups * experts
    expert_idx = lax.axis_index("expert")
    tokens = dense_feats.shape[0]
    slots = requests.shape[-1]
    rows_dev = table.shape[0]
    tok_groups = tokens // GROUP_TOK
    sub_slots = slots // tok_groups
    group_slots = devices * sub_slots
    total_asked = devices * slots
    ask_block = min(1024, total_asked)
    bias_one, bias_two, dense_w, gate_w, tower_w, head_w = unpack(small, experts)
    first_full, second_full = (
        lax.all_gather(first_w.astype(jnp.bfloat16), "batch", axis=1, tiled=True),
        lax.all_gather(second_w.astype(jnp.bfloat16), "batch", axis=1, tiled=True),
    )
    asked = lax.all_to_all(
        lax.all_to_all(requests[0], "batch", split_axis=0, concat_axis=0, tiled=True),
        "expert",
        split_axis=1,
        concat_axis=1,
        tiled=True,
    )
    asked_blocks = asked.reshape(total_asked // ask_block, ask_block)
    table_low = table.astype(jnp.bfloat16)
    sent_rows = lax.map(lambda index: pick_rows(index, table_low), asked_blocks)
    sent_rows = sent_rows.reshape(groups, experts, slots * EMB)
    got_rows = lax.all_to_all(
        lax.all_to_all(sent_rows, "batch", split_axis=0, concat_axis=0, tiled=True),
        "expert",
        split_axis=1,
        concat_axis=1,
        tiled=True,
    )
    by_group = (
        got_rows.reshape(devices, tok_groups, sub_slots, EMB)
        .transpose(1, 0, 2, 3)
        .reshape(tok_groups, group_slots, EMB)
    )
    local_pick = (picks // slots * sub_slots + picks % sub_slots).reshape(
        tok_groups, GROUP_TOK * FIELDS
    )
    emb = lax.map(lambda item: pick_rows(item[0], item[1]), (local_pick, by_group)).reshape(
        tokens, FIELDS * EMB
    )
    dense_proj = jnp.dot(dense_feats, dense_w[:DENSE], precision=HI) + dense_w[DENSE]
    inputs = jnp.concatenate([emb, dense_proj.astype(jnp.bfloat16)], 1)
    gate_low = gate_w[:INPUT].astype(jnp.bfloat16)
    gate_logits = jnp.dot(inputs, gate_low, preferred_element_type=jnp.float32) + gate_w[INPUT]
    probs = jax.nn.softmax(gate_logits.reshape(tokens, TASKS, experts), axis=-1)
    gates = probs.astype(jnp.bfloat16)
    all_inputs, all_gates = (
        lax.all_gather(inputs, "expert", axis=0, tiled=True),
        lax.all_gather(gates.reshape(tokens, TASKS * experts), "expert", axis=0, tiled=True),
    )
    own_gates = lax.dynamic_slice_in_dim(
        all_gates.reshape(-1, TASKS, experts), expert_idx, 1, 2
    ).astype(jnp.float32)
    first_use, second_use = (first_full, second_full)
    first_b = lax.dynamic_slice_in_dim(bias_one, expert_idx, 1, 0)
    second_b = lax.dynamic_slice_in_dim(bias_two, expert_idx, 1, 0)
    pre_one, hidden, pre_two, expert_out = expert_forward(
        all_inputs, first_use, second_use, first_b, second_b
    )
    terms = jnp.einsum("tke,teo->tko", own_gates, expert_out, precision=HI).reshape(-1, TASKS * OUT)
    mixed = lax.psum_scatter(terms.astype(jnp.bfloat16), "expert", scatter_dimension=0, tiled=True)
    mask = label_mask.astype(jnp.float32)
    target = labels.astype(jnp.float32)
    counts = jnp.maximum(lax.psum(jnp.sum(mask, 0), ("batch", "expert")), 1.0)
    mixed_low = mixed.reshape(tokens, TASKS, OUT)
    tower_low = tower_w[:, :OUT].astype(jnp.bfloat16)
    tower_pre = (
        jnp.einsum("tko,koh->tkh", mixed_low, tower_low, preferred_element_type=jnp.float32)
        + tower_w[:, OUT][None]
    )
    tower_act = jax.nn.silu(tower_pre)
    logits = jnp.einsum("tkh,kh->tk", tower_act, head_w[:, :TOWER], precision=HI) + head_w[:, TOWER]
    loss_local = jnp.sum(mask * (jax.nn.softplus(logits) - target * logits) / counts)
    d_logits = mask * (jax.nn.sigmoid(logits) - target) / counts
    d_head = jnp.concatenate(
        [
            jnp.einsum("tkh,tk->kh", tower_act, d_logits, precision=HI),
            jnp.sum(d_logits, 0)[:, None],
        ],
        1,
    )
    d_act = d_logits[:, :, None] * head_w[None, :, :TOWER]
    d_tower_pre = (silu_slope(tower_pre) * d_act).astype(jnp.bfloat16)
    d_tower = jnp.concatenate(
        [
            jnp.einsum("tko,tkh->koh", mixed_low, d_tower_pre, preferred_element_type=jnp.float32),
            jnp.sum(d_tower_pre, 0, dtype=jnp.float32)[:, None, :],
        ],
        1,
    )
    d_mixed = jnp.einsum(
        "tkh,koh->tko", d_tower_pre, tower_low, preferred_element_type=jnp.float32
    ).astype(jnp.bfloat16)
    all_d_mixed = (
        lax.all_gather(d_mixed.reshape(tokens, TASKS * OUT), "expert", axis=0, tiled=True)
        .reshape(-1, TASKS, OUT)
        .astype(jnp.float32)
    )
    d_out = jnp.einsum("tke,tko->teo", own_gates, all_d_mixed, precision=HI)
    d_gate_col = jnp.einsum("teo,tko->tke", expert_out, all_d_mixed, precision=HI)
    d_first_w, d_second_w, d_first_b, d_second_b, d_rows = expert_backward(
        all_inputs, first_use, second_use, pre_one, hidden, pre_two, d_out
    )
    onehot = (jnp.arange(experts) == expert_idx).astype(jnp.float32)
    d_gate_full = (d_gate_col * onehot[None, None, :]).reshape(-1, TASKS * experts)
    d_inputs, d_gates = (
        lax.psum_scatter(
            d_rows.astype(jnp.bfloat16), "expert", scatter_dimension=0, tiled=True
        ).astype(jnp.float32),
        lax.psum_scatter(
            d_gate_full.astype(jnp.bfloat16), "expert", scatter_dimension=0, tiled=True
        ).astype(jnp.float32),
    )
    d_gates = d_gates.reshape(tokens, TASKS, experts)
    d_first_b = onehot[:, None] * d_first_b
    d_second_b = onehot[:, None] * d_second_b
    d_gate_logits = (
        (probs * (d_gates - jnp.sum(probs * d_gates, -1, keepdims=True)))
        .astype(jnp.bfloat16)
        .reshape(tokens, TASKS * experts)
    )
    d_gate_w = jnp.concatenate(
        [
            jnp.dot(inputs.T, d_gate_logits, preferred_element_type=jnp.float32),
            jnp.sum(d_gate_logits, 0, dtype=jnp.float32)[None],
        ],
        0,
    )
    d_x = d_inputs + jnp.dot(d_gate_logits, gate_low.T, preferred_element_type=jnp.float32)
    d_dense = d_x[:, FIELDS * EMB :]
    d_dense_w = jnp.concatenate(
        [jnp.dot(dense_feats.T, d_dense, precision=HI), jnp.sum(d_dense, 0)[None]], 0
    )
    d_emb = d_x[:, : FIELDS * EMB].reshape(tok_groups, GROUP_TOK * FIELDS, EMB)
    slot_grads = lax.map(lambda item: add_rows(item[0], item[1], group_slots), (local_pick, d_emb))
    slot_grads = (
        slot_grads.reshape(tok_groups, devices, sub_slots, EMB)
        .transpose(1, 0, 2, 3)
        .reshape(groups, experts, slots * EMB)
    )
    owner_grads = lax.all_to_all(
        lax.all_to_all(
            slot_grads.astype(jnp.bfloat16), "batch", split_axis=0, concat_axis=0, tiled=True
        ),
        "expert",
        split_axis=1,
        concat_axis=1,
        tiled=True,
    ).astype(slot_grads.dtype)
    owner_blocks = owner_grads.reshape(total_asked // ask_block, ask_block, EMB)

    def add_block(total, item):
        return (total + add_rows(item[0], item[1], rows_dev), None)

    table_grad, unused = lax.scan(
        add_block, jnp.zeros((rows_dev, EMB), jnp.float32), (asked_blocks, owner_blocks)
    )
    grad_first, grad_second = (
        lax.psum_scatter(
            d_first_w.astype(jnp.bfloat16), "batch", scatter_dimension=1, tiled=True
        ).astype(jnp.float32),
        lax.psum_scatter(
            d_second_w.astype(jnp.bfloat16), "batch", scatter_dimension=1, tiled=True
        ).astype(jnp.float32),
    )
    flat_grads = jnp.concatenate(
        [
            d_first_b.reshape(-1),
            d_second_b.reshape(-1),
            d_dense_w.reshape(-1),
            d_gate_w.reshape(-1),
            d_tower.reshape(-1),
            d_head.reshape(-1),
        ]
    )
    grad_small, loss = lax.psum((flat_grads, loss_local), ("batch", "expert"))
    new_table, new_table_m, new_table_v = adamw(table, table_m, table_v, table_grad, 0.3)
    new_first, new_first_m, new_first_v = adamw(first_w, first_m, first_v, grad_first, 0.15)
    new_second, new_second_m, new_second_v = adamw(second_w, second_m, second_v, grad_second, 0.15)
    new_small, new_small_m, new_small_v = adamw(small, small_m, small_v, grad_small, 0.15)
    return (
        loss,
        new_table,
        new_table_m,
        new_table_v,
        new_first,
        new_first_m,
        new_first_v,
        new_second,
        new_second_m,
        new_second_v,
        new_small,
        new_small_m,
        new_small_v,
    )


MESH = pl.DeviceIdType.MESH
BF = jnp.bfloat16
F32 = jnp.float32
NN = (((1,), (0,)), ((), ()))
NT = (((1,), (1,)), ((), ()))
KEYS = 256
CHUNK = 256
LANES = 128
ONES = 16

Sizes = collections.namedtuple(
    "Sizes",
    (
        "groups",
        "experts",
        "devices",
        "slots",
        "rows",
        "tokens",
        "first",
        "second",
        "pack",
        "span",
    ),
)


def sizes_of(mesh, tokens, slots, rows):
    groups = mesh.shape["batch"]
    experts = mesh.shape["expert"]
    first = INPUT // groups
    second = HID // groups
    span = tokens * LANES // slots
    return Sizes(
        groups,
        experts,
        groups * experts,
        slots,
        rows,
        tokens,
        first,
        second,
        first + second // 2,
        span,
    )


def fits(size):
    return (
        size.slots % LANES == 0
        and size.slots & (size.slots - 1) == 0
        and size.span == CHUNK
        and size.second % 32 == 0
        and size.first % 16 == 0
        and size.groups == 8
        and size.devices % 2 == 0
        and size.rows % KEYS == 0
        and size.experts == 4
    )


def mm(left, right, dims=NN, precision=None):
    return lax.dot_general(left, right, dims, preferred_element_type=F32, precision=precision)


def here(size):
    group = lax.axis_index("batch")
    expert = lax.axis_index("expert")
    return group, expert, group * size.experts + expert


def place(size, device):
    return (lax.div(device, size.experts), lax.rem(device, size.experts))


def greet(size, me):
    barrier = pltpu.get_barrier_semaphore()

    def one(step, carry):
        peer = lax.rem(me + step, size.devices)
        pl.semaphore_signal(barrier, inc=1, device_id=place(size, peer), device_id_type=MESH)
        return carry

    lax.fori_loop(1, size.devices, one, 0)
    return barrier


def push(source, target, sent, landed, where):
    return pltpu.make_async_remote_copy(
        src_ref=source,
        dst_ref=target,
        send_sem=sent,
        recv_sem=landed,
        device_id=where,
        device_id_type=MESH,
    )


def spread(index, extent, width):
    lines = lax.broadcasted_iota(jnp.int32, (extent, width), 0).astype(F32).astype(BF)
    return lines == index.astype(F32).astype(BF)


def as_low(flag):
    return jnp.where(flag, jnp.ones((), BF), jnp.zeros((), BF))


def look_up(cells, key, high, levels):
    found = mm(cells, as_low(spread(key, KEYS, key.shape[1])))
    result = found[:EMB]
    for level in range(1, levels):
        result = jnp.where(high == level, found[level * EMB : (level + 1) * EMB], result)
    return result


def levels_of(values, high, levels):
    return jnp.concatenate(
        [jnp.where(high == level, values, 0.0) for level in range(levels)], 0
    ).astype(BF)


def sigmoid(value):
    return 0.5 + 0.5 * jnp.tanh(0.5 * value)


def lanes_of(rows=1):
    return lax.broadcasted_iota(jnp.int32, (rows, LANES), 1)


def turn(values, shift):
    shift = shift % LANES
    return pltpu.roll(values, shift, 1) if shift else values


def take(flat, offset, count):
    row, shift = offset // LANES, offset % LANES
    if shift == 0:
        return flat[row : row + count, :]
    return jnp.where(
        lanes_of(count) < LANES - shift,
        turn(flat[row : row + count, :], -shift),
        turn(flat[row + 1 : row + 1 + count, :], -shift),
    )


def put(flat, offset, values):
    row, shift = offset // LANES, offset % LANES
    count = values.shape[0]
    moved = turn(values, shift)
    if shift == 0:
        flat[row : row + count, :] += moved
        return
    flat[row : row + count, :] += jnp.where(lanes_of(count) >= shift, moved, 0.0)
    flat[row + 1 : row + 1 + count, :] += jnp.where(lanes_of(count) < shift, moved, 0.0)


def offsets(experts):
    sizes = [
        experts * HID,
        experts * OUT,
        (DENSE + 1) * DOUT,
        (INPUT + 1) * TASKS * experts,
        TASKS * (OUT + 1) * TOWER,
        TASKS * (TOWER + 1),
    ]
    return [sum(sizes[:index]) for index in range(len(sizes) + 1)]


def step_kernel(
    size,
    requests,
    picks,
    dense,
    labels,
    mask,
    table,
    first,
    second,
    small,
    table_grad,
    first_grad,
    second_grad,
    small_sum,
    message,
    asked,
    cells,
    rows,
    got,
    slots_out,
    slots_got,
    gathered,
    grads,
    core_got,
    core_sum,
    chip_got,
    chip_sum,
    z_got,
    vectors,
    columns,
    gate_rows,
    gate_t,
    tower_rows,
    tower_n,
    tower_t,
    dense_rows,
    dense_w,
    dense_low,
    small_part,
    small_got,
    first_t,
    second_n,
    second_t,
    wide,
    feats,
    feats_low,
    slot_cells_a,
    slot_cells_b,
    chosen_a,
    chosen_b,
    chosen_c,
    inputs_a,
    inputs_b,
    slope_one,
    slope_two,
    hidden,
    outs,
    mixes,
    deltas,
    d_inputs_a,
    d_inputs_b,
    slot_sum_a,
    slot_sum_b,
    sum_first,
    sum_second,
    sum_gate,
    sum_dense,
    sum_tower,
    sum_head,
    loss_sum,
    ask_sent,
    ask_landed,
    row_sent,
    row_landed,
    slot_sent,
    slot_landed,
    small_sent,
    small_landed,
    whole_sent,
    whole_landed,
    gz_sent,
    gz_landed,
    gy_sent,
    gx_landed,
    gy_landed,
    gd_landed,
    gc_sent,
    gc_landed,
    sz_sent,
    sz_landed,
    sy_sent,
    sy_landed,
    sc_sent,
    sc_landed,
):
    group, expert_here, me = here(size)
    slots, devices, experts = size.slots, size.devices, size.experts
    chips = size.groups // 2
    chip, core = lax.div(group, 2), lax.rem(group, 2)
    blocks = size.rows // KEYS
    half = size.second // 2
    levels = devices // 2
    shift = slots.bit_length() - 1
    chunks = size.tokens // CHUNK
    gates_wide = TASKS * experts
    at_one, at_two, at_dense, at_gate, at_tower, at_head, at_loss = offsets(experts)
    lane = lanes_of()
    barrier = greet(size, me)
    slot_cells = (slot_cells_a, slot_cells_b)
    chosen = (chosen_a, chosen_b, chosen_c)
    inputs = (inputs_a, inputs_b)
    d_inputs = (d_inputs_a, d_inputs_b)
    slot_sum = (slot_sum_a, slot_sum_b)

    def own_lines(device):
        count = small_got.shape[1]
        return pl.ds(pl.multiple_of(device * count, count), count)

    def to_all(source, target, sent, landed, step, receive):
        peer = lax.rem(me + (devices - step if receive else step), devices)
        return push(
            source(peer),
            target(peer if receive else me),
            sent,
            landed,
            place(size, peer),
        )

    def ask(step, receive):
        return to_all(
            lambda p: message.at[p], lambda p: asked.at[p], ask_sent, ask_landed, step, receive
        )

    def answer(part, step, receive):
        peer = lax.rem(me + (step if receive else devices - step), devices)
        return push(
            rows.at[part, peer],
            got.at[part, peer if receive else me],
            row_sent,
            row_landed.at[part],
            place(size, peer),
        )

    def give_slots(part, step, receive):
        return to_all(
            lambda p: slots_out.at[part, p],
            lambda p: slots_got.at[part, p],
            slot_sent,
            slot_landed.at[part],
            step,
            receive,
        )

    def give_small(step, receive):
        return to_all(
            lambda p: small_part.at[own_lines(p), :],
            lambda p: small_got.at[p],
            small_sent,
            small_landed,
            step,
            receive,
        )

    def give_whole(step, receive):
        return to_all(
            lambda p: small_sum.at[own_lines(me), :],
            lambda p: small_sum.at[own_lines(p), :],
            whole_sent,
            whole_landed,
            step,
            receive,
        )

    def turned(index, count, step, receive):
        return lax.rem(index + (count - step if receive else step), count)

    def source_at(step):
        return turned(expert_here, experts, step, True)

    def weights_z(step):
        other = turned(expert_here, experts, step, False)
        block = gathered.at[group, expert_here]
        return push(block, block, gz_sent, gz_landed.at[step], (group, other))

    beside_x = chip + 1 - 2 * lax.rem(chip, 2)
    beside_y = lax.rem(chip + 2, 4)
    across_both = lax.rem(beside_x + 2, 4)

    def weights_x(step, owner):
        block = gathered.at[owner * 2 + core, source_at(step)]
        landed = (gx_landed if owner is chip else gd_landed).at[step]
        return push(block, block, gy_sent, landed, (beside_x * 2 + core, expert_here))

    def weights_y(step, owner):
        block = gathered.at[owner * 2 + core, source_at(step)]
        landed = (gy_landed if owner is chip else gd_landed).at[step]
        return push(block, block, gy_sent, landed, (beside_y * 2 + core, expert_here))

    def spread_weights(step):
        weights_x(step, chip).start()
        weights_y(step, chip).start()

    def forward_weights(step):
        wait(gx_landed.at[step], gathered.at[0, 0])
        wait(gy_landed.at[step], gathered.at[0, 0])
        if step % 2 == 0:
            weights_y(step, beside_x).start()
        else:
            weights_x(step, beside_y).start()

    def weights_c(owner):
        block = gathered.at[owner * 2 + core]
        return push(
            block, block, gc_sent, gc_landed, (chip * 2 + 1 - core, expert_here)
        )

    def expert_at(turn_no):
        return turned(expert_here, experts, turn_no + 1, False)

    def sums_c(turn_no, step):
        expert = expert_at(turn_no)
        other = turned(chip, chips, step, False)
        return push(
            grads.at[other * 2 + 1 - core, expert],
            core_got.at[expert, other],
            sc_sent,
            sc_landed.at[turn_no],
            (chip * 2 + 1 - core, expert_here),
        )

    def sums_y(turn_no, step):
        expert = expert_at(turn_no)
        other = turned(chip, chips, step, False)
        return push(
            core_sum.at[expert, other],
            chip_got.at[expert, step],
            sy_sent,
            sy_landed.at[turn_no],
            (other * 2 + core, expert_here),
        )

    def sums_z(turn_no):
        expert = expert_at(turn_no)
        return push(
            chip_sum.at[expert], z_got.at[turn_no], sz_sent, sz_landed, (group, expert)
        )

    def wait(semaphore, block):
        pltpu.make_async_copy(block, block, semaphore).wait()

    others = pl.ds(0, devices - 1)
    other_chips = pl.ds(0, chips - 1)
    other_experts = pl.ds(0, experts - 1)

    def loop(begin, end, body, unroll=1):
        def one(step, carry):
            body(step)
            return carry

        lax.fori_loop(begin, end, one, 0, unroll=unroll)

    valid = mask[...].astype(F32)
    count = jnp.where(
        lane == 0,
        jnp.sum(valid[0:1], 1, keepdims=True),
        jnp.where(lane == 1, jnp.sum(valid[1:2], 1, keepdims=True), 0.0),
    ).astype(jnp.int32)
    for part in range(size.groups):
        for one in range(experts):
            peer = part * experts + one
            message[peer, :, :slots] = requests[part, one : one + 1, :]
            message[peer, :, slots:] = count
    gathered[group, expert_here, : size.first, :] = first[...].astype(BF)
    gathered[group, expert_here, size.first :, :LANES] = second[:half].astype(BF)
    gathered[group, expert_here, size.first :, LANES:] = second[half:].astype(BF)
    for block in range(blocks):
        cells[block * EMB : (block + 1) * EMB, :] = table[
            :, block * KEYS : (block + 1) * KEYS
        ].astype(BF)
    pl.semaphore_wait(barrier, devices - 1)
    for step in range(1, experts):
        weights_z(step).start()
    spread_weights(0)
    loop(1, devices, lambda step: ask(step, False).start())

    vectors[...] = jnp.zeros_like(vectors)
    vectors[: at_dense // LANES, :] = small[: at_dense // LANES, :]
    lines = take(small, at_tower, TASKS * (OUT + 1) * TOWER // LANES)
    count_rows = lines.shape[0]
    tower_rows[pl.ds(0, count_rows, stride=2), :] = lines
    tower_rows[pl.ds(1, count_rows, stride=2), :] = turn(lines, TOWER)
    for task in range(TASKS):
        base = task * (OUT + 1)
        block = tower_rows[base : base + OUT, :]
        tower_n[task] = block[:, :TOWER].astype(BF)
        tower_t[task] = block.T[:TOWER].astype(BF)
    last = [tower_rows[k * (OUT + 1) + OUT : (k + 1) * (OUT + 1), :] for k in range(TASKS)]
    vectors[12:13, :] = jnp.where(lane < TOWER, last[0], turn(last[1], TOWER))
    heads = [take(small, at_head, 1)]
    end = at_head + TOWER + 1
    heads.append(turn(small[end // LANES : end // LANES + 1, :], -(end % LANES)))
    vectors[13:14, :] = jnp.where(lane < TOWER, heads[0], turn(heads[1], TOWER))
    vectors[15:16, :] = jnp.where(lane == 0, turn(heads[0], -TOWER), turn(heads[1], 1 - TOWER))
    per_line = LANES // gates_wide
    lines = take(small, at_gate, INPUT // per_line + 1)
    for spot in range(per_line):
        gate_rows[pl.ds(spot, lines.shape[0], stride=per_line), :] = jnp.where(
            lanes_of(lines.shape[0]) < gates_wide, turn(lines, -spot * gates_wide), 0.0
        )
    for block in range(INPUT // LANES):
        piece = gate_rows[block * LANES : (block + 1) * LANES, :]
        gate_t[:, block * LANES : (block + 1) * LANES] = piece.T[:16].astype(BF)
        wide[block * LANES : (block + 1) * LANES, experts * HID :] = piece.astype(BF)
    vectors[14:15, :] = gate_rows[INPUT : INPUT + 1, :]
    dense_rows[...] = jnp.zeros_like(dense_rows)
    for line in range(DENSE + 1):
        dense_rows[line : line + 1, :] = take(small, at_dense + line * DOUT, 1)
    dense_w[...] = dense_rows[...].T[:DOUT, :16]
    flipped = vectors[...].T
    for column in range(16):
        columns[column] = jnp.broadcast_to(flipped[:, column : column + 1], (LANES, LANES))
    feats[...] = jnp.ones_like(feats)
    feats[:DENSE, :] = dense[...]
    upper = feats[...].astype(BF)
    feats_low[:16, :] = upper
    feats_low[16:, :] = (feats[...] - upper.astype(F32)).astype(BF)
    dense_low[...] = mm(dense_w[...], feats[...], precision=HI).astype(BF)
    for buffer in inputs:
        buffer[INPUT:, :] = jnp.ones((ONES, CHUNK), BF)
    for expert in range(experts):
        hidden[expert, HID:, :] = jnp.ones((ONES, CHUNK), BF)
    for task in range(TASKS):
        mixes[task, OUT:, :] = jnp.ones((ONES, CHUNK), BF)
    deltas[experts * HID :, :] = jnp.zeros((LANES, CHUNK), BF)
    for total in (sum_gate, loss_sum, small_part, table_grad):
        total[...] = jnp.zeros_like(total)

    asked[me] = message[me]
    batch = 4

    def serve(part):
        columns_here = pl.ds(part * LANES, LANES)

        def some(turn_no, own):
            steps = [turn_no * batch + i for i in range(batch)]
            peers = [lax.rem(me + devices - step, devices) for step in steps]
            index = jnp.concatenate([asked[peer, :, columns_here] for peer in peers], 1)
            found = look_up(cells[...], index & (KEYS - 1), index >> 8, blocks).astype(BF)
            for i, peer in enumerate(peers):
                piece = found[:, i * LANES : (i + 1) * LANES]
                if own and i == 0:
                    got[part, peer] = piece
                else:
                    rows[part, peer] = piece
                    if part == 0:
                        answer(part, steps[i], False).start()

        some(0, True)
        loop(1, devices // batch, lambda turn_no: some(turn_no, False), devices // batch - 1)

    def send_rows(part):
        loop(1, devices, lambda step: answer(part, step, False).start())

    forward_weights(0)
    wait(ask_landed, asked.at[others])
    for step in range(1, experts):
        wait(gz_landed.at[step], gathered.at[0, 0])
        spread_weights(step)
    weights_c(chip).start()
    total = jnp.zeros((1, LANES), jnp.int32)
    for peer in range(devices):
        total = total + asked[peer, :, slots:]
    totals = jnp.maximum(total.astype(F32), 1.0)
    serve(0)
    serve(1)
    for step in range(1, experts):
        forward_weights(step)
    weights_c(beside_x).start()
    weights_c(beside_y).start()
    send_rows(1)
    for part in range(2, chunks):
        serve(part)
    for step in range(experts):
        wait(gd_landed.at[step], gathered.at[0, 0])
    weights_c(across_both).start()
    for part in range(2, chunks):
        send_rows(part)

    def column(index, begin=0, end=LANES):
        block = columns[index, begin:end, :]
        return jnp.concatenate([block] * (CHUNK // LANES), 1)

    def tokens_of(part):
        return slice(part * CHUNK, (part + 1) * CHUNK)

    def split(part, field):
        index = picks[field : field + 1, tokens_of(part)]
        owner = index >> shift
        return (owner & 1) * LANES + (index & (LANES - 1)), owner >> 1

    def fetch(part):
        wait(row_landed.at[part], got.at[part, others])
        for owner in range(devices):
            level, lower = owner // 2, owner % 2
            slot_cells[part % 2][
                level * EMB : (level + 1) * EMB, lower * LANES : (lower + 1) * LANES
            ] = got[part, owner]
        inputs[part % 2][FIELDS * EMB : INPUT, :] = dense_low[:, tokens_of(part)]

    def pick(part, field):
        key, high = split(part, field)
        flags = as_low(spread(key, KEYS, CHUNK))
        chosen[part % 3][field] = flags
        found = mm(slot_cells[part % 2][...], flags)
        result = found[:EMB]
        for level in range(1, levels):
            result = jnp.where(high == level, found[level * EMB : (level + 1) * EMB], result)
        inputs[part % 2][field * EMB : (field + 1) * EMB, :] = result.astype(BF)

    def give(part, field, first_time):
        places, flags = [], []
        for one in (field, field + 1):
            key, high = split(part, one)
            values = d_inputs[part % 2][one * EMB : (one + 1) * EMB, :]
            places.append(levels_of(values, high, levels))
            flags.append(chosen[part % 3][one])
        sums = mm(jnp.concatenate(places, 1), jnp.concatenate(flags, 1), NT)
        if first_time:
            slot_sum[part % 2][...] = sums
        else:
            slot_sum[part % 2][...] += sums

    def picks_of(part):
        return [functools.partial(pick, part, field) for field in range(FIELDS)]

    def gives_of(part):
        return [
            functools.partial(give, part, field, field == 0) for field in range(0, FIELDS, 2)
        ]

    def send_slots(part):
        for owner in range(devices):
            level, lower = owner // 2, owner % 2
            slots_out[part, owner] = slot_sum[part % 2][
                level * EMB : (level + 1) * EMB, lower * LANES : (lower + 1) * LANES
            ].astype(BF)
        loop(1, devices, lambda hop: give_slots(part, hop, False).start())
        slots_got[part, me] = slots_out[part, me]

    def train(part):
        here_tokens = tokens_of(part)
        first_time = part == 0
        whole_x = inputs[part % 2]

        def add(total, value):
            if first_time:
                total[...] = value
            else:
                total[...] += value

        x = whole_x[:INPUT, :]
        logits = mm(gate_t[...], x)[:gates_wide] + column(14, 0, gates_wide)
        probs, gates = [], []
        for task in range(TASKS):
            line = [logits[task * experts + e : task * experts + e + 1] for e in range(experts)]
            top = functools.reduce(jnp.maximum, line)
            powers = [jnp.exp(item - top) for item in line]
            whole = 1.0 / functools.reduce(jnp.add, powers)
            probs.append([item * whole for item in powers])
            gates.append([item.astype(BF).astype(F32) for item in probs[-1]])
        yield
        mixed = [None] * TASKS
        for expert in range(experts):
            pre = mm(first_t[expert], x) + jnp.concatenate(
                [column(2 * expert), column(2 * expert + 1)], 0
            )
            sig = sigmoid(pre)
            act = pre * sig
            slope_one[expert] = sig + act * (1.0 - sig)
            low = act.astype(BF)
            hidden[expert, :HID, :] = low
            yield
            pre = mm(second_t[expert], low) + column(8 + expert)
            sig = sigmoid(pre)
            act = pre * sig
            slope_two[expert] = sig + act * (1.0 - sig)
            outs[expert] = act
            for task in range(TASKS):
                term = gates[task][expert] * act
                mixed[task] = term if mixed[task] is None else mixed[task] + term
            yield
        d_mixed = []
        for task in range(TASKS):
            mix = mixed[task].astype(BF)
            mixes[task, :OUT, :] = mix
            low, high = task * TOWER, (task + 1) * TOWER
            pre = mm(tower_t[task], mix) + column(12, low, high)
            sig = sigmoid(pre)
            act = pre * sig
            head = column(13, low, high)
            logit = jnp.sum(act * head, 0, keepdims=True) + column(15, task, task + 1)
            scale = mask[task : task + 1, here_tokens].astype(F32) / totals[:, task : task + 1]
            target = labels[task : task + 1, here_tokens].astype(F32)
            soft = jnp.maximum(logit, 0.0) + jnp.log(1.0 + jnp.exp(-jnp.abs(logit)))
            loss_sum[...] += scale * (soft - target * logit)
            d_logit = scale * (sigmoid(logit) - target)
            yield
            d_pre = ((sig + act * (1.0 - sig)) * (d_logit * head)).astype(BF)
            d_upper = d_logit.astype(BF).astype(F32)
            d_both = jnp.concatenate(
                [
                    jnp.broadcast_to(d_upper, (8, CHUNK)),
                    jnp.broadcast_to(d_logit - d_upper, (8, CHUNK)),
                ],
                0,
            ).astype(BF)
            upper = act.astype(BF)
            rest = (act - upper.astype(F32)).astype(BF)
            ones = jnp.ones((16, CHUNK), BF)
            zeros = jnp.zeros((LANES - TOWER - 16, CHUNK), BF)
            both = mm(d_both, jnp.concatenate([upper, ones, zeros], 0), NT) + mm(
                d_both, jnp.concatenate([rest, zeros, jnp.zeros((16, CHUNK), BF)], 0), NT
            )
            add(sum_head.at[task], both[:8] + both[8:])
            add(sum_tower.at[task], mm(mixes[task], d_pre, NT))
            d_mixed.append(mm(tower_n[task], d_pre).astype(BF).astype(F32))
            yield
        d_gates = [[None] * experts for task in range(TASKS)]
        for expert in range(experts):
            d_out = gates[0][expert] * d_mixed[0] + gates[1][expert] * d_mixed[1]
            out = outs[expert]
            for task in range(TASKS):
                d_gates[task][expert] = jnp.sum(out * d_mixed[task], 0, keepdims=True)
            d_two = (slope_two[expert] * d_out).astype(BF)
            d_hidden = mm(second_n[expert], d_two)
            add(sum_second.at[expert], mm(hidden[expert], d_two, NT))
            yield
            d_one = (slope_one[expert] * d_hidden).astype(BF)
            deltas[expert * HID : (expert + 1) * HID, :] = d_one
            add(sum_first.at[expert], mm(whole_x[...], d_one, NT))
            yield
        lines = []
        for task in range(TASKS):
            inner = functools.reduce(
                jnp.add, [probs[task][e] * d_gates[task][e] for e in range(experts)]
            )
            lines += [probs[task][e] * (d_gates[task][e] - inner) for e in range(experts)]
        lines.append(jnp.zeros((16 - gates_wide, CHUNK), F32))
        d_gate = jnp.concatenate(lines, 0).astype(BF)
        deltas[experts * HID : experts * HID + 16, :] = d_gate
        add(sum_gate.at[:, : INPUT + ONES], mm(d_gate, whole_x[...], NT))
        yield
        d_x = mm(wide[...], deltas[...])
        d_inputs[part % 2][...] = d_x
        d_dense = d_x[INPUT - LANES :, :]
        upper = d_dense.astype(BF)
        rest = (d_dense - upper.astype(F32)).astype(BF)
        both = mm(feats_low[:, here_tokens], upper, NT)
        add(sum_dense, both[:16] + both[16:] + mm(feats_low[:16, here_tokens], rest, NT))
        yield

    stops = 2 + 2 * experts + 2 * TASKS + 2 * experts + 1

    def beside(main, jobs):
        jobs, done = list(jobs), 0
        for stop, _ in enumerate(main):
            until = len(jobs) * (stop + 1) // stops
            for job in jobs[done:until]:
                job()
            done = until
        for job in jobs[done:]:
            job()

    def mixed_jobs(*lists):
        spots = [
            ((index + 0.5) / len(jobs), job) for jobs in lists for index, job in enumerate(jobs)
        ]
        return [job for spot, job in sorted(spots, key=lambda pair: pair[0])]

    fetch(0)
    for job in picks_of(0):
        job()
    wait(gc_landed, gathered.at[pl.ds(0, chips)])
    for expert in range(experts):
        for part in range(size.groups):
            wide[
                part * size.first : (part + 1) * size.first, expert * HID : (expert + 1) * HID
            ] = gathered[part, expert, : size.first, :]
            base = part * size.second
            second_n[expert, base : base + half, :] = gathered[part, expert, size.first :, :LANES]
            second_n[expert, base + half : base + 2 * half, :] = gathered[
                part, expert, size.first :, LANES:
            ]
        first_t[expert] = wide[:, expert * HID : (expert + 1) * HID].T
        second_t[expert] = second_n[expert].T
    for part in range(chunks):
        jobs = []
        if part + 1 < chunks:
            fetch(part + 1)
            jobs.append(picks_of(part + 1))
        if part > 0:
            jobs.append(gives_of(part - 1))
        beside(train(part), mixed_jobs(*jobs))
        if 0 < part < chunks - 1:
            send_slots(part - 1)

    for turn_no in range(experts):
        expert = expert_at(turn_no)
        for part in range(size.groups):
            base = part * size.second
            grads[part, expert, : size.first, :] = sum_first[
                expert, part * size.first : (part + 1) * size.first, :
            ].astype(BF)
            grads[part, expert, size.first :, :LANES] = sum_second[
                expert, base : base + half, :
            ].astype(BF)
            grads[part, expert, size.first :, LANES:] = sum_second[
                expert, base + half : base + 2 * half, :
            ].astype(BF)
        for step in range(1, chips + 1):
            sums_c(turn_no, step % chips).start()
    for expert in range(experts):
        per = HID // LANES
        for piece in range(per):
            line = expert * per + piece
            small_part[line : line + 1, :] = sum_first[
                expert, INPUT : INPUT + 1, piece * LANES : (piece + 1) * LANES
            ]
        line = experts * per + expert
        small_part[line : line + 1, :] = sum_second[expert, HID : HID + 1, :]
    for line in range(DENSE + 1):
        values = jnp.where(lane < DOUT, turn(sum_dense[line : line + 1, :], DOUT - LANES), 0.0)
        put(small_part, at_dense + line * DOUT, values)
    fill = jnp.zeros((LANES - 16, LANES), F32)
    for block in range(INPUT // LANES):
        piece = jnp.concatenate([sum_gate[:, block * LANES : (block + 1) * LANES], fill], 0)
        gate_rows[block * LANES : (block + 1) * LANES, :] = piece.T
    gate_rows[INPUT:, :] = jnp.concatenate([sum_gate[:, INPUT:], fill], 0).T[:ONES]
    lines = INPUT // per_line + 1
    packed = jnp.zeros((lines, LANES), F32)
    for spot in range(per_line):
        packed = packed + turn(gate_rows[pl.ds(spot, lines, stride=per_line), :], spot * gates_wide)
    inside = lax.broadcasted_iota(jnp.int32, (lines, LANES), 0) < lines - 1
    put(
        small_part,
        at_gate,
        jnp.where(inside | (lanes_of(lines) < gates_wide), packed, 0.0),
    )
    tower_rows[...] = jnp.zeros_like(tower_rows)
    for task in range(TASKS):
        base = task * (OUT + 1)
        tower_rows[base : base + OUT + 1, :TOWER] = sum_tower[task, : OUT + 1, :]
    put(
        small_part,
        at_tower,
        tower_rows[pl.ds(0, count_rows, stride=2), :]
        + turn(tower_rows[pl.ds(1, count_rows, stride=2), :], TOWER),
    )
    for task in range(TASKS):
        put(
            small_part,
            at_head + task * (TOWER + 1),
            jnp.where(lane < TOWER + 1, sum_head[task, 0:1, :], 0.0),
        )
    whole_loss = jnp.sum(loss_sum[...], 1, keepdims=True)
    put(small_part, at_loss, jnp.where(lane == 0, whole_loss, 0.0))
    loop(1, devices, lambda step: give_small(step, False).start())
    for turn_no in range(experts):
        expert = expert_at(turn_no)
        wait(sc_landed.at[turn_no], core_got.at[expert])
        for step in range(1, chips + 1):
            other = turned(chip, chips, step % chips, False)
            core_sum[expert, other] = (
                grads[other * 2 + core, expert].astype(F32) + core_got[expert, other].astype(F32)
            ).astype(BF)
            if step < chips:
                sums_y(turn_no, step).start()
    send_slots(chunks - 2)
    for job in gives_of(chunks - 1):
        job()
    send_slots(chunks - 1)

    def collect(part):
        columns_here = pl.ds(part * LANES, LANES)
        wait(slot_landed.at[part], slots_got.at[part, others])

        def some(turn_no):
            steps = [turn_no * batch + i for i in range(batch)]
            peers = [lax.rem(me + devices - step, devices) for step in steps]
            index = jnp.concatenate([asked[peer, :, columns_here] for peer in peers], 1)
            values = jnp.concatenate([slots_got[part, peer] for peer in peers], 1).astype(F32)
            spots = as_low(spread(index & (KEYS - 1), KEYS, batch * LANES))
            table_grad[...] += mm(levels_of(values, index >> 8, blocks), spots, NT)

        loop(0, devices // batch, some, devices // batch)

    for part in range(chunks - 2):
        collect(part)
    for turn_no in range(experts):
        expert = expert_at(turn_no)
        wait(sy_landed.at[turn_no], chip_got.at[expert, other_chips])
        total = core_sum[expert, chip].astype(F32)
        for step in range(1, chips):
            total = total + chip_got[expert, step].astype(F32)
        if turn_no + 1 < experts:
            chip_sum[expert] = total.astype(BF)
            sums_z(turn_no).start()
        if turn_no == 0:
            wait(small_landed, small_got.at[others])
            small_got[me] = small_part[own_lines(me), :]
            small_sum[own_lines(me), :] = jnp.sum(small_got[...], 0)
            loop(1, devices, lambda step: give_whole(step, False).start())
    collect(chunks - 2)
    collect(chunks - 1)
    wait(sz_landed, z_got.at[other_experts])
    for turn_no in range(experts - 1):
        total = total + z_got[turn_no].astype(F32)
    first_grad[...] = total[: size.first]
    second_grad[:half, :] = total[size.first :, :LANES]
    second_grad[half:, :] = total[size.first :, LANES:]

    other_lines = pl.ds(0, (devices - 1) * small_got.shape[1])
    wait(whole_landed, small_sum.at[other_lines, :])
    wait(whole_sent, small_sum.at[other_lines, :])
    wait(small_sent, small_part.at[other_lines, :])
    wait(ask_sent, message.at[others])
    wait(row_sent, rows.at[:, others])
    wait(slot_sent, slots_out.at[:, others])
    wait(gz_sent, gathered.at[0, other_experts])
    wait(gy_sent, gathered.at[other_chips])
    wait(gc_sent, gathered.at[pl.ds(0, chips)])
    wait(sc_sent, core_got)
    wait(sy_sent, core_sum.at[:, other_chips])
    wait(sz_sent, chip_sum.at[other_experts])


def update(size, *refs):
    grads, state, flat, results, loss = refs[:3], refs[3:12], refs[12], refs[13:22], refs[22]
    spot = offsets(size.experts)[-1]
    loss[...] = flat[spot // LANES : spot // LANES + 1, spot % LANES : spot % LANES + 1]
    table_grad = grads[0][...]
    wide = jnp.concatenate(
        [table_grad[b * EMB : (b + 1) * EMB] for b in range(size.rows // KEYS)], 1
    )
    for index, grad in enumerate((wide, grads[1][...], grads[2][...])):
        rate = 0.3 if index == 0 else 0.15
        values = [ref[...] for ref in state[3 * index : 3 * index + 3]]
        for ref, value in zip(results[3 * index : 3 * index + 3], adamw(*values, grad, rate)):
            ref[...] = value


def shape(dims, dtype=F32):
    return jax.ShapeDtypeStruct(dims, dtype)


def call(kernel, outs, scratch, remote=None):
    vmem = pl.BlockSpec(memory_space=pltpu.VMEM)
    params = dict(vmem_limit_bytes=56 * 2**20)
    if remote is not None:
        params.update(collective_id=remote, has_side_effects=True)
    return lambda *args: pl.pallas_call(
        kernel,
        out_shape=outs,
        in_specs=[vmem] * len(args),
        out_specs=[vmem] * len(outs),
        scratch_shapes=scratch,
        compiler_params=pltpu.CompilerParams(**params),
    )(*args)


def local(
    size,
    dense_feats,
    picks,
    labels,
    label_mask,
    requests,
    table,
    table_m,
    table_v,
    first_w,
    first_m,
    first_v,
    second_w,
    second_m,
    second_v,
    small,
    small_m,
    small_v,
):
    devices, experts, groups = size.devices, size.experts, size.groups
    chips = groups // 2
    chunks = size.tokens // CHUNK
    dma = pltpu.SemaphoreType.DMA
    vm = pltpu.VMEM
    message = size.slots + LANES
    count = small.shape[0]
    lines = -(-(count + 1) // (devices * 8 * LANES)) * 8
    flat_lines = -(-count // LANES)
    exchange = vm((chunks, devices, EMB, LANES), BF)
    weights = vm((groups, experts, size.pack, HID), BF)
    of_chips = vm((experts, chips, size.pack, HID), BF)
    of_chip = vm((experts, size.pack, HID), BF)
    table_grad, first_grad, second_grad, flat = call(
        functools.partial(step_kernel, size),
        [
            shape((size.rows // KEYS * EMB, KEYS)),
            shape((size.first, HID)),
            shape((size.second, OUT)),
            shape((devices * lines, LANES)),
        ],
        [
            vm((devices, 1, message), jnp.int32),
            vm((devices, 1, message), jnp.int32),
            vm((size.rows // KEYS * EMB, KEYS), BF),
        ]
        + [exchange] * 4
        + [weights, weights, of_chips, of_chips, of_chips, of_chip, of_chip]
        + [
            vm((LANES, LANES), F32),
            vm((16, LANES, LANES), F32),
            vm((INPUT + ONES, LANES), F32),
            vm((16, INPUT), BF),
            vm((TASKS * (OUT + 1) + 6, LANES), F32),
            vm((TASKS, OUT, TOWER), BF),
            vm((TASKS, TOWER, OUT), BF),
            vm((LANES, LANES), F32),
            vm((DOUT, 16), F32),
            vm((DOUT, size.tokens), BF),
            vm((devices * lines, LANES), F32),
            vm((devices, lines, LANES), F32),
            vm((experts, HID, INPUT), BF),
            vm((experts, HID, OUT), BF),
            vm((experts, OUT, HID), BF),
            vm((INPUT, experts * HID + LANES), BF),
            vm((16, size.tokens), F32),
            vm((32, size.tokens), BF),
            vm((devices // 2 * EMB, KEYS), BF),
            vm((devices // 2 * EMB, KEYS), BF),
            vm((FIELDS, KEYS, CHUNK), BF),
            vm((FIELDS, KEYS, CHUNK), BF),
            vm((FIELDS, KEYS, CHUNK), BF),
            vm((INPUT + ONES, CHUNK), BF),
            vm((INPUT + ONES, CHUNK), BF),
            vm((experts, HID, CHUNK), F32),
            vm((experts, OUT, CHUNK), F32),
            vm((experts, HID + ONES, CHUNK), BF),
            vm((experts, OUT, CHUNK), F32),
            vm((TASKS, OUT + ONES, CHUNK), BF),
            vm((experts * HID + LANES, CHUNK), BF),
            vm((INPUT, CHUNK), F32),
            vm((INPUT, CHUNK), F32),
            vm((devices // 2 * EMB, KEYS), F32),
            vm((devices // 2 * EMB, KEYS), F32),
            vm((experts, INPUT + ONES, HID), F32),
            vm((experts, HID + ONES, OUT), F32),
            vm((16, INPUT + LANES), F32),
            vm((16, LANES), F32),
            vm((TASKS, OUT + ONES, TOWER), F32),
            vm((TASKS, 8, LANES), F32),
            vm((1, CHUNK), F32),
        ]
        + [dma, dma, dma, dma((chunks,)), dma, dma((chunks,))]
        + [dma] * 5
        + [dma((experts,)), dma, dma((experts,)), dma((experts,)), dma((experts,))]
        + [dma] * 5
        + [dma((experts,)), dma, dma((experts,))],
        0,
    )(
        requests[0],
        picks.T,
        dense_feats.T,
        labels.T,
        label_mask.T,
        table.T,
        first_w[0],
        second_w[0],
        jnp.pad(small, (0, flat_lines * LANES - count)).reshape(flat_lines, LANES),
    )
    tables = (table.T, table_m.T, table_v.T)
    firsts = (first_w[0], first_m[0], first_v[0])
    seconds = (second_w[0], second_m[0], second_v[0])
    new = call(
        functools.partial(update, size),
        [shape(a.shape) for a in tables + firsts + seconds] + [shape((1, 1))],
        [],
    )(table_grad, first_grad, second_grad, *tables, *firsts, *seconds, flat)
    flat = flat.reshape(-1)
    new_small = adamw(small, small_m, small_v, flat[:count], 0.15)
    return (
        (new[9].reshape(()),)
        + tuple(a.T for a in new[:3])
        + tuple(a[None] for a in new[3:9])
        + tuple(new_small)
    )


def solution(mesh):
    both = P(("batch", "expert"), None)
    shard = P("expert", "batch", None)
    ins = (both,) * 4 + (P(("batch", "expert"), None, None, None),) + (both,) * 3
    ins = ins + (shard,) * 6 + (P(),) * 3

    def step(*args):
        devices = mesh.shape["batch"] * mesh.shape["expert"]
        size = sizes_of(
            mesh, args[0].shape[0] // devices, args[4].shape[-1], args[5].shape[0] // devices
        )
        return jax.shard_map(
            functools.partial(local, size) if fits(size) else plain,
            mesh=mesh,
            in_specs=ins,
            out_specs=(P(),) + (both,) * 3 + (shard,) * 6 + (P(),) * 3,
            check_vma=False,
        )(*args)

    return step
```

```python
import collections
import functools

import jax
import jax.numpy as jnp
from jax import lax
from jax.experimental import pallas as pl
from jax.experimental.pallas import tpu as pltpu
from jax.sharding import PartitionSpec as P

FIELDS = 26
EMB = 16
DENSE = 13
DOUT = 96
HID = 256
OUT = 128
TOWER = 64
TASKS = 2
STEP = 5
GROUP_TOK = 64
INPUT = 512


HI = lax.Precision.HIGHEST


def unpack(flat, experts):
    shapes = [
        (experts, HID),
        (experts, OUT),
        (DENSE + 1, DOUT),
        (INPUT + 1, TASKS * experts),
        (TASKS, OUT + 1, TOWER),
        (TASKS, TOWER + 1),
    ]
    parts = []
    offset = 0
    for shape in shapes:
        length = 1
        for extent in shape:
            length = length * extent
        parts.append(flat[offset : offset + length].reshape(shape))
        offset = offset + length
    return parts


def adamw(weight, first, second, grad, rate):
    first = 0.9 * first + 0.1 * grad
    second = 0.999 * second + 0.001 * grad * grad
    fix_one = 1.0 - 0.9**STEP
    fix_two = 1.0 - 0.999**STEP
    weight = weight - rate * (
        first / fix_one / (jnp.sqrt(second / fix_two) + 1e-08) + 0.01 * weight
    )
    return (weight, first, second)


def silu_slope(value):
    sig = jax.nn.sigmoid(value)
    return sig * (1.0 + value * (1.0 - sig))


def split_three(values):
    upper = values.astype(jnp.bfloat16)
    rest = values - upper.astype(jnp.float32)
    middle = rest.astype(jnp.bfloat16)
    lower_part = (rest - middle.astype(jnp.float32)).astype(jnp.bfloat16)
    return jnp.concatenate([upper, middle, lower_part], -1)


def join_three(values):
    return values[:, :EMB] + values[:, EMB : 2 * EMB] + values[:, 2 * EMB :]


def one_hot(index, extent):
    return (index[:, None] == jnp.arange(extent, dtype=jnp.int32)[None, :]).astype(jnp.bfloat16)


def pick_rows(index, source):
    return jnp.dot(
        one_hot(index, source.shape[0]), source, preferred_element_type=jnp.float32
    ).astype(jnp.bfloat16)


def add_rows(index, values, extent):
    spread = lax.dot_general(
        one_hot(index, extent),
        split_three(values),
        (((0,), (0,)), ((), ())),
        preferred_element_type=jnp.float32,
    )
    return join_three(spread)


def expert_forward(inputs, first_w, second_w, first_b, second_b):
    pre_one = (
        jnp.einsum("ti,eih->teh", inputs, first_w, preferred_element_type=jnp.float32)
        + first_b[None]
    )
    hidden = jax.nn.silu(pre_one).astype(jnp.bfloat16)
    pre_two = (
        jnp.einsum("teh,eho->teo", hidden, second_w, preferred_element_type=jnp.float32)
        + second_b[None]
    )
    return (pre_one, hidden, pre_two, jax.nn.silu(pre_two))


def expert_backward(inputs, first_w, second_w, pre_one, hidden, pre_two, d_out):
    d_two = (silu_slope(pre_two) * d_out).astype(jnp.bfloat16)
    d_second_w = jnp.einsum("teh,teo->eho", hidden, d_two, preferred_element_type=jnp.float32)
    d_second_b = jnp.sum(d_two, 0, dtype=jnp.float32)
    d_hidden = jnp.einsum("teo,eho->teh", d_two, second_w, preferred_element_type=jnp.float32)
    d_one = (silu_slope(pre_one) * d_hidden).astype(jnp.bfloat16)
    d_first_w = jnp.einsum("ti,teh->eih", inputs, d_one, preferred_element_type=jnp.float32)
    d_first_b = jnp.sum(d_one, 0, dtype=jnp.float32)
    d_inputs = jnp.einsum("teh,eih->ti", d_one, first_w, preferred_element_type=jnp.float32)
    return (d_first_w, d_second_w, d_first_b, d_second_b, d_inputs)


def plain(
    dense_feats,
    picks,
    labels,
    label_mask,
    requests,
    table,
    table_m,
    table_v,
    first_w,
    first_m,
    first_v,
    second_w,
    second_m,
    second_v,
    small,
    small_m,
    small_v,
):
    groups = lax.axis_size("batch")
    experts = lax.axis_size("expert")
    devices = groups * experts
    expert_idx = lax.axis_index("expert")
    tokens = dense_feats.shape[0]
    slots = requests.shape[-1]
    rows_dev = table.shape[0]
    tok_groups = tokens // GROUP_TOK
    sub_slots = slots // tok_groups
    group_slots = devices * sub_slots
    total_asked = devices * slots
    ask_block = min(1024, total_asked)
    bias_one, bias_two, dense_w, gate_w, tower_w, head_w = unpack(small, experts)
    first_full, second_full = (
        lax.all_gather(first_w.astype(jnp.bfloat16), "batch", axis=1, tiled=True),
        lax.all_gather(second_w.astype(jnp.bfloat16), "batch", axis=1, tiled=True),
    )
    asked = lax.all_to_all(
        lax.all_to_all(requests[0], "batch", split_axis=0, concat_axis=0, tiled=True),
        "expert",
        split_axis=1,
        concat_axis=1,
        tiled=True,
    )
    asked_blocks = asked.reshape(total_asked // ask_block, ask_block)
    table_low = table.astype(jnp.bfloat16)
    sent_rows = lax.map(lambda index: pick_rows(index, table_low), asked_blocks)
    sent_rows = sent_rows.reshape(groups, experts, slots * EMB)
    got_rows = lax.all_to_all(
        lax.all_to_all(sent_rows, "batch", split_axis=0, concat_axis=0, tiled=True),
        "expert",
        split_axis=1,
        concat_axis=1,
        tiled=True,
    )
    by_group = (
        got_rows.reshape(devices, tok_groups, sub_slots, EMB)
        .transpose(1, 0, 2, 3)
        .reshape(tok_groups, group_slots, EMB)
    )
    local_pick = (picks // slots * sub_slots + picks % sub_slots).reshape(
        tok_groups, GROUP_TOK * FIELDS
    )
    emb = lax.map(lambda item: pick_rows(item[0], item[1]), (local_pick, by_group)).reshape(
        tokens, FIELDS * EMB
    )
    dense_proj = jnp.dot(dense_feats, dense_w[:DENSE], precision=HI) + dense_w[DENSE]
    inputs = jnp.concatenate([emb, dense_proj.astype(jnp.bfloat16)], 1)
    gate_low = gate_w[:INPUT].astype(jnp.bfloat16)
    gate_logits = jnp.dot(inputs, gate_low, preferred_element_type=jnp.float32) + gate_w[INPUT]
    probs = jax.nn.softmax(gate_logits.reshape(tokens, TASKS, experts), axis=-1)
    gates = probs.astype(jnp.bfloat16)
    all_inputs, all_gates = (
        lax.all_gather(inputs, "expert", axis=0, tiled=True),
        lax.all_gather(gates.reshape(tokens, TASKS * experts), "expert", axis=0, tiled=True),
    )
    own_gates = lax.dynamic_slice_in_dim(
        all_gates.reshape(-1, TASKS, experts), expert_idx, 1, 2
    ).astype(jnp.float32)
    first_use, second_use = (first_full, second_full)
    first_b = lax.dynamic_slice_in_dim(bias_one, expert_idx, 1, 0)
    second_b = lax.dynamic_slice_in_dim(bias_two, expert_idx, 1, 0)
    pre_one, hidden, pre_two, expert_out = expert_forward(
        all_inputs, first_use, second_use, first_b, second_b
    )
    terms = jnp.einsum("tke,teo->tko", own_gates, expert_out, precision=HI).reshape(-1, TASKS * OUT)
    mixed = lax.psum_scatter(terms.astype(jnp.bfloat16), "expert", scatter_dimension=0, tiled=True)
    mask = label_mask.astype(jnp.float32)
    target = labels.astype(jnp.float32)
    counts = jnp.maximum(lax.psum(jnp.sum(mask, 0), ("batch", "expert")), 1.0)
    mixed_low = mixed.reshape(tokens, TASKS, OUT)
    tower_low = tower_w[:, :OUT].astype(jnp.bfloat16)
    tower_pre = (
        jnp.einsum("tko,koh->tkh", mixed_low, tower_low, preferred_element_type=jnp.float32)
        + tower_w[:, OUT][None]
    )
    tower_act = jax.nn.silu(tower_pre)
    logits = jnp.einsum("tkh,kh->tk", tower_act, head_w[:, :TOWER], precision=HI) + head_w[:, TOWER]
    loss_local = jnp.sum(mask * (jax.nn.softplus(logits) - target * logits) / counts)
    d_logits = mask * (jax.nn.sigmoid(logits) - target) / counts
    d_head = jnp.concatenate(
        [
            jnp.einsum("tkh,tk->kh", tower_act, d_logits, precision=HI),
            jnp.sum(d_logits, 0)[:, None],
        ],
        1,
    )
    d_act = d_logits[:, :, None] * head_w[None, :, :TOWER]
    d_tower_pre = (silu_slope(tower_pre) * d_act).astype(jnp.bfloat16)
    d_tower = jnp.concatenate(
        [
            jnp.einsum("tko,tkh->koh", mixed_low, d_tower_pre, preferred_element_type=jnp.float32),
            jnp.sum(d_tower_pre, 0, dtype=jnp.float32)[:, None, :],
        ],
        1,
    )
    d_mixed = jnp.einsum(
        "tkh,koh->tko", d_tower_pre, tower_low, preferred_element_type=jnp.float32
    ).astype(jnp.bfloat16)
    all_d_mixed = (
        lax.all_gather(d_mixed.reshape(tokens, TASKS * OUT), "expert", axis=0, tiled=True)
        .reshape(-1, TASKS, OUT)
        .astype(jnp.float32)
    )
    d_out = jnp.einsum("tke,tko->teo", own_gates, all_d_mixed, precision=HI)
    d_gate_col = jnp.einsum("teo,tko->tke", expert_out, all_d_mixed, precision=HI)
    d_first_w, d_second_w, d_first_b, d_second_b, d_rows = expert_backward(
        all_inputs, first_use, second_use, pre_one, hidden, pre_two, d_out
    )
    onehot = (jnp.arange(experts) == expert_idx).astype(jnp.float32)
    d_gate_full = (d_gate_col * onehot[None, None, :]).reshape(-1, TASKS * experts)
    d_inputs, d_gates = (
        lax.psum_scatter(
            d_rows.astype(jnp.bfloat16), "expert", scatter_dimension=0, tiled=True
        ).astype(jnp.float32),
        lax.psum_scatter(
            d_gate_full.astype(jnp.bfloat16), "expert", scatter_dimension=0, tiled=True
        ).astype(jnp.float32),
    )
    d_gates = d_gates.reshape(tokens, TASKS, experts)
    d_first_b = onehot[:, None] * d_first_b
    d_second_b = onehot[:, None] * d_second_b
    d_gate_logits = (
        (probs * (d_gates - jnp.sum(probs * d_gates, -1, keepdims=True)))
        .astype(jnp.bfloat16)
        .reshape(tokens, TASKS * experts)
    )
    d_gate_w = jnp.concatenate(
        [
            jnp.dot(inputs.T, d_gate_logits, preferred_element_type=jnp.float32),
            jnp.sum(d_gate_logits, 0, dtype=jnp.float32)[None],
        ],
        0,
    )
    d_x = d_inputs + jnp.dot(d_gate_logits, gate_low.T, preferred_element_type=jnp.float32)
    d_dense = d_x[:, FIELDS * EMB :]
    d_dense_w = jnp.concatenate(
        [jnp.dot(dense_feats.T, d_dense, precision=HI), jnp.sum(d_dense, 0)[None]], 0
    )
    d_emb = d_x[:, : FIELDS * EMB].reshape(tok_groups, GROUP_TOK * FIELDS, EMB)
    slot_grads = lax.map(lambda item: add_rows(item[0], item[1], group_slots), (local_pick, d_emb))
    slot_grads = (
        slot_grads.reshape(tok_groups, devices, sub_slots, EMB)
        .transpose(1, 0, 2, 3)
        .reshape(groups, experts, slots * EMB)
    )
    owner_grads = lax.all_to_all(
        lax.all_to_all(
            slot_grads.astype(jnp.bfloat16), "batch", split_axis=0, concat_axis=0, tiled=True
        ),
        "expert",
        split_axis=1,
        concat_axis=1,
        tiled=True,
    ).astype(slot_grads.dtype)
    owner_blocks = owner_grads.reshape(total_asked // ask_block, ask_block, EMB)

    def add_block(total, item):
        return (total + add_rows(item[0], item[1], rows_dev), None)

    table_grad, unused = lax.scan(
        add_block, jnp.zeros((rows_dev, EMB), jnp.float32), (asked_blocks, owner_blocks)
    )
    grad_first, grad_second = (
        lax.psum_scatter(
            d_first_w.astype(jnp.bfloat16), "batch", scatter_dimension=1, tiled=True
        ).astype(jnp.float32),
        lax.psum_scatter(
            d_second_w.astype(jnp.bfloat16), "batch", scatter_dimension=1, tiled=True
        ).astype(jnp.float32),
    )
    flat_grads = jnp.concatenate(
        [
            d_first_b.reshape(-1),
            d_second_b.reshape(-1),
            d_dense_w.reshape(-1),
            d_gate_w.reshape(-1),
            d_tower.reshape(-1),
            d_head.reshape(-1),
        ]
    )
    grad_small, loss = lax.psum((flat_grads, loss_local), ("batch", "expert"))
    new_table, new_table_m, new_table_v = adamw(table, table_m, table_v, table_grad, 0.3)
    new_first, new_first_m, new_first_v = adamw(first_w, first_m, first_v, grad_first, 0.15)
    new_second, new_second_m, new_second_v = adamw(second_w, second_m, second_v, grad_second, 0.15)
    new_small, new_small_m, new_small_v = adamw(small, small_m, small_v, grad_small, 0.15)
    return (
        loss,
        new_table,
        new_table_m,
        new_table_v,
        new_first,
        new_first_m,
        new_first_v,
        new_second,
        new_second_m,
        new_second_v,
        new_small,
        new_small_m,
        new_small_v,
    )


MESH = pl.DeviceIdType.MESH
BF = jnp.bfloat16
F32 = jnp.float32
NN = (((1,), (0,)), ((), ()))
NT = (((1,), (1,)), ((), ()))
KEYS = 256
CHUNK = 256
LANES = 128
ONES = 16

Sizes = collections.namedtuple(
    "Sizes",
    (
        "groups",
        "experts",
        "devices",
        "slots",
        "rows",
        "tokens",
        "first",
        "second",
        "pack",
        "span",
    ),
)


def sizes_of(mesh, tokens, slots, rows):
    groups = mesh.shape["batch"]
    experts = mesh.shape["expert"]
    first = INPUT // groups
    second = HID // groups
    span = tokens * LANES // slots
    return Sizes(
        groups,
        experts,
        groups * experts,
        slots,
        rows,
        tokens,
        first,
        second,
        first + second // 2,
        span,
    )


def fits(size):
    return (
        size.slots % LANES == 0
        and size.slots & (size.slots - 1) == 0
        and size.span == CHUNK
        and size.second % 32 == 0
        and size.first % 16 == 0
        and size.groups == 8
        and size.devices % 2 == 0
        and size.rows % KEYS == 0
        and size.experts == 4
    )


def mm(left, right, dims=NN, precision=None):
    return lax.dot_general(left, right, dims, preferred_element_type=F32, precision=precision)


def here(size):
    group = lax.axis_index("batch")
    expert = lax.axis_index("expert")
    return group, expert, group * size.experts + expert


def place(size, device):
    return (lax.div(device, size.experts), lax.rem(device, size.experts))


def greet(size, me):
    barrier = pltpu.get_barrier_semaphore()

    def one(step, carry):
        peer = lax.rem(me + step, size.devices)
        pl.semaphore_signal(barrier, inc=1, device_id=place(size, peer), device_id_type=MESH)
        return carry

    lax.fori_loop(1, size.devices, one, 0)
    return barrier


def push(source, target, sent, landed, where):
    return pltpu.make_async_remote_copy(
        src_ref=source,
        dst_ref=target,
        send_sem=sent,
        recv_sem=landed,
        device_id=where,
        device_id_type=MESH,
    )


def spread(index, extent, width):
    lines = lax.broadcasted_iota(jnp.int32, (extent, width), 0).astype(F32).astype(BF)
    return lines == index.astype(F32).astype(BF)


def as_low(flag):
    return jnp.where(flag, jnp.ones((), BF), jnp.zeros((), BF))


def look_up(cells, key, high, levels):
    found = mm(cells, as_low(spread(key, KEYS, key.shape[1])))
    result = found[:EMB]
    for level in range(1, levels):
        result = jnp.where(high == level, found[level * EMB : (level + 1) * EMB], result)
    return result


def levels_of(values, high, levels):
    return jnp.concatenate(
        [jnp.where(high == level, values, 0.0) for level in range(levels)], 0
    ).astype(BF)


def sigmoid(value):
    return 0.5 + 0.5 * jnp.tanh(0.5 * value)


def lanes_of(rows=1):
    return lax.broadcasted_iota(jnp.int32, (rows, LANES), 1)


def turn(values, shift):
    shift = shift % LANES
    return pltpu.roll(values, shift, 1) if shift else values


def take(flat, offset, count):
    row, shift = offset // LANES, offset % LANES
    if shift == 0:
        return flat[row : row + count, :]
    return jnp.where(
        lanes_of(count) < LANES - shift,
        turn(flat[row : row + count, :], -shift),
        turn(flat[row + 1 : row + 1 + count, :], -shift),
    )


def put(flat, offset, values):
    row, shift = offset // LANES, offset % LANES
    count = values.shape[0]
    moved = turn(values, shift)
    if shift == 0:
        flat[row : row + count, :] += moved
        return
    flat[row : row + count, :] += jnp.where(lanes_of(count) >= shift, moved, 0.0)
    flat[row + 1 : row + 1 + count, :] += jnp.where(lanes_of(count) < shift, moved, 0.0)


def offsets(experts):
    sizes = [
        experts * HID,
        experts * OUT,
        (DENSE + 1) * DOUT,
        (INPUT + 1) * TASKS * experts,
        TASKS * (OUT + 1) * TOWER,
        TASKS * (TOWER + 1),
    ]
    return [sum(sizes[:index]) for index in range(len(sizes) + 1)]


def step_kernel(
    size,
    requests,
    picks,
    dense,
    labels,
    mask,
    table,
    first,
    second,
    small,
    table_grad,
    first_grad,
    second_grad,
    small_sum,
    message,
    asked,
    cells,
    rows,
    got,
    slots_out,
    slots_got,
    gathered,
    grads,
    core_got,
    core_sum,
    chip_got,
    chip_sum,
    z_got,
    vectors,
    columns,
    gate_rows,
    gate_t,
    tower_rows,
    tower_n,
    tower_t,
    dense_rows,
    dense_w,
    dense_low,
    small_part,
    small_got,
    first_t,
    second_n,
    second_t,
    wide,
    feats,
    feats_low,
    slot_cells_a,
    slot_cells_b,
    chosen_a,
    chosen_b,
    chosen_c,
    inputs_a,
    inputs_b,
    slope_one,
    slope_two,
    hidden,
    outs,
    mixes,
    deltas,
    d_inputs_a,
    d_inputs_b,
    slot_sum_a,
    slot_sum_b,
    sum_first,
    sum_second,
    sum_gate,
    sum_dense,
    sum_tower,
    sum_head,
    loss_sum,
    ask_sent,
    ask_landed,
    row_sent,
    row_landed,
    slot_sent,
    slot_landed,
    small_sent,
    small_landed,
    whole_sent,
    whole_landed,
    gz_sent,
    gz_landed,
    gy_sent,
    gx_landed,
    gy_landed,
    gd_landed,
    gc_sent,
    gc_landed,
    sz_sent,
    sz_landed,
    sy_sent,
    sy_landed,
    sc_sent,
    sc_landed,
):
    group, expert_here, me = here(size)
    slots, devices, experts = size.slots, size.devices, size.experts
    chips = size.groups // 2
    chip, core = lax.div(group, 2), lax.rem(group, 2)
    blocks = size.rows // KEYS
    half = size.second // 2
    levels = devices // 2
    shift = slots.bit_length() - 1
    chunks = size.tokens // CHUNK
    gates_wide = TASKS * experts
    at_one, at_two, at_dense, at_gate, at_tower, at_head, at_loss = offsets(experts)
    lane = lanes_of()
    barrier = greet(size, me)
    slot_cells = (slot_cells_a, slot_cells_b)
    chosen = (chosen_a, chosen_b, chosen_c)
    inputs = (inputs_a, inputs_b)
    d_inputs = (d_inputs_a, d_inputs_b)
    slot_sum = (slot_sum_a, slot_sum_b)

    def own_lines(device):
        count = small_got.shape[1]
        return pl.ds(pl.multiple_of(device * count, count), count)

    def to_all(source, target, sent, landed, step, receive):
        peer = lax.rem(me + (devices - step if receive else step), devices)
        return push(
            source(peer),
            target(peer if receive else me),
            sent,
            landed,
            place(size, peer),
        )

    def ask(step, receive):
        return to_all(
            lambda p: message.at[p], lambda p: asked.at[p], ask_sent, ask_landed, step, receive
        )

    def answer(part, step, receive):
        peer = lax.rem(me + (step if receive else devices - step), devices)
        return push(
            rows.at[part, peer],
            got.at[part, peer if receive else me],
            row_sent,
            row_landed.at[part],
            place(size, peer),
        )

    def give_slots(part, step, receive):
        return to_all(
            lambda p: slots_out.at[part, p],
            lambda p: slots_got.at[part, p],
            slot_sent,
            slot_landed.at[part],
            step,
            receive,
        )

    def give_small(step, receive):
        return to_all(
            lambda p: small_part.at[own_lines(p), :],
            lambda p: small_got.at[p],
            small_sent,
            small_landed,
            step,
            receive,
        )

    def give_whole(step, receive):
        return to_all(
            lambda p: small_sum.at[own_lines(me), :],
            lambda p: small_sum.at[own_lines(p), :],
            whole_sent,
            whole_landed,
            step,
            receive,
        )

    def turned(index, count, step, receive):
        return lax.rem(index + (count - step if receive else step), count)

    def source_at(step):
        return turned(expert_here, experts, step, True)

    def weights_z(step):
        other = turned(expert_here, experts, step, False)
        block = gathered.at[group, expert_here]
        return push(block, block, gz_sent, gz_landed.at[step], (group, other))

    beside_x = chip + 1 - 2 * lax.rem(chip, 2)
    beside_y = lax.rem(chip + 2, 4)
    across_both = lax.rem(beside_x + 2, 4)

    def weights_x(step, owner):
        block = gathered.at[owner * 2 + core, source_at(step)]
        landed = (gx_landed if owner is chip else gd_landed).at[step]
        return push(block, block, gy_sent, landed, (beside_x * 2 + core, expert_here))

    def weights_y(step, owner):
        block = gathered.at[owner * 2 + core, source_at(step)]
        landed = (gy_landed if owner is chip else gd_landed).at[step]
        return push(block, block, gy_sent, landed, (beside_y * 2 + core, expert_here))

    def spread_weights(step):
        weights_x(step, chip).start()
        weights_y(step, chip).start()

    def forward_weights(step):
        wait(gx_landed.at[step], gathered.at[0, 0])
        wait(gy_landed.at[step], gathered.at[0, 0])
        if step % 2 == 0:
            weights_y(step, beside_x).start()
        else:
            weights_x(step, beside_y).start()

    def weights_c(owner):
        block = gathered.at[owner * 2 + core]
        return push(
            block, block, gc_sent, gc_landed, (chip * 2 + 1 - core, expert_here)
        )

    def expert_at(turn_no):
        return turned(expert_here, experts, turn_no + 1, False)

    def sums_c(turn_no, step):
        expert = expert_at(turn_no)
        other = turned(chip, chips, step, False)
        return push(
            grads.at[other * 2 + 1 - core, expert],
            core_got.at[expert, other],
            sc_sent,
            sc_landed.at[turn_no],
            (chip * 2 + 1 - core, expert_here),
        )

    def sums_y(turn_no, step):
        expert = expert_at(turn_no)
        other = turned(chip, chips, step, False)
        return push(
            core_sum.at[expert, other],
            chip_got.at[expert, step],
            sy_sent,
            sy_landed.at[turn_no],
            (other * 2 + core, expert_here),
        )

    def sums_z(turn_no):
        expert = expert_at(turn_no)
        return push(
            chip_sum.at[expert], z_got.at[turn_no], sz_sent, sz_landed, (group, expert)
        )

    def wait(semaphore, block):
        pltpu.make_async_copy(block, block, semaphore).wait()

    others = pl.ds(0, devices - 1)
    other_chips = pl.ds(0, chips - 1)
    other_experts = pl.ds(0, experts - 1)

    def loop(begin, end, body, unroll=1):
        def one(step, carry):
            body(step)
            return carry

        lax.fori_loop(begin, end, one, 0, unroll=unroll)

    valid = mask[...].astype(F32)
    count = jnp.where(
        lane == 0,
        jnp.sum(valid[0:1], 1, keepdims=True),
        jnp.where(lane == 1, jnp.sum(valid[1:2], 1, keepdims=True), 0.0),
    ).astype(jnp.int32)
    for part in range(size.groups):
        for one in range(experts):
            peer = part * experts + one
            message[peer, :, :slots] = requests[part, one : one + 1, :]
            message[peer, :, slots:] = count
    gathered[group, expert_here, : size.first, :] = first[...].astype(BF)
    gathered[group, expert_here, size.first :, :LANES] = second[:half].astype(BF)
    gathered[group, expert_here, size.first :, LANES:] = second[half:].astype(BF)
    for block in range(blocks):
        cells[block * EMB : (block + 1) * EMB, :] = table[
            :, block * KEYS : (block + 1) * KEYS
        ].astype(BF)
    pl.semaphore_wait(barrier, devices - 1)
    loop(1, devices, lambda step: ask(step, False).start())
    for step in range(1, experts):
        weights_z(step).start()
    spread_weights(0)

    vectors[...] = jnp.zeros_like(vectors)
    vectors[: at_dense // LANES, :] = small[: at_dense // LANES, :]
    lines = take(small, at_tower, TASKS * (OUT + 1) * TOWER // LANES)
    count_rows = lines.shape[0]
    tower_rows[pl.ds(0, count_rows, stride=2), :] = lines
    tower_rows[pl.ds(1, count_rows, stride=2), :] = turn(lines, TOWER)
    for task in range(TASKS):
        base = task * (OUT + 1)
        block = tower_rows[base : base + OUT, :]
        tower_n[task] = block[:, :TOWER].astype(BF)
        tower_t[task] = block.T[:TOWER].astype(BF)
    last = [tower_rows[k * (OUT + 1) + OUT : (k + 1) * (OUT + 1), :] for k in range(TASKS)]
    vectors[12:13, :] = jnp.where(lane < TOWER, last[0], turn(last[1], TOWER))
    heads = [take(small, at_head, 1)]
    end = at_head + TOWER + 1
    heads.append(turn(small[end // LANES : end // LANES + 1, :], -(end % LANES)))
    vectors[13:14, :] = jnp.where(lane < TOWER, heads[0], turn(heads[1], TOWER))
    vectors[15:16, :] = jnp.where(lane == 0, turn(heads[0], -TOWER), turn(heads[1], 1 - TOWER))
    per_line = LANES // gates_wide
    lines = take(small, at_gate, INPUT // per_line + 1)
    for spot in range(per_line):
        gate_rows[pl.ds(spot, lines.shape[0], stride=per_line), :] = jnp.where(
            lanes_of(lines.shape[0]) < gates_wide, turn(lines, -spot * gates_wide), 0.0
        )
    for block in range(INPUT // LANES):
        piece = gate_rows[block * LANES : (block + 1) * LANES, :]
        gate_t[:, block * LANES : (block + 1) * LANES] = piece.T[:16].astype(BF)
        wide[block * LANES : (block + 1) * LANES, experts * HID :] = piece.astype(BF)
    vectors[14:15, :] = gate_rows[INPUT : INPUT + 1, :]
    dense_rows[...] = jnp.zeros_like(dense_rows)
    for line in range(DENSE + 1):
        dense_rows[line : line + 1, :] = take(small, at_dense + line * DOUT, 1)
    dense_w[...] = dense_rows[...].T[:DOUT, :16]
    flipped = vectors[...].T
    for column in range(16):
        columns[column] = jnp.broadcast_to(flipped[:, column : column + 1], (LANES, LANES))
    feats[...] = jnp.ones_like(feats)
    feats[:DENSE, :] = dense[...]
    upper = feats[...].astype(BF)
    feats_low[:16, :] = upper
    feats_low[16:, :] = (feats[...] - upper.astype(F32)).astype(BF)
    dense_low[...] = mm(dense_w[...], feats[...], precision=HI).astype(BF)
    for buffer in inputs:
        buffer[INPUT:, :] = jnp.ones((ONES, CHUNK), BF)
    for expert in range(experts):
        hidden[expert, HID:, :] = jnp.ones((ONES, CHUNK), BF)
    for task in range(TASKS):
        mixes[task, OUT:, :] = jnp.ones((ONES, CHUNK), BF)
    deltas[experts * HID :, :] = jnp.zeros((LANES, CHUNK), BF)
    for total in (sum_gate, loss_sum, small_part, table_grad):
        total[...] = jnp.zeros_like(total)

    asked[me] = message[me]
    batch = 4

    def serve(part):
        columns_here = pl.ds(part * LANES, LANES)

        def some(turn_no, own):
            steps = [turn_no * batch + i for i in range(batch)]
            peers = [lax.rem(me + devices - step, devices) for step in steps]
            index = jnp.concatenate([asked[peer, :, columns_here] for peer in peers], 1)
            found = look_up(cells[...], index & (KEYS - 1), index >> 8, blocks).astype(BF)
            for i, peer in enumerate(peers):
                piece = found[:, i * LANES : (i + 1) * LANES]
                if own and i == 0:
                    got[part, peer] = piece
                else:
                    rows[part, peer] = piece
                    if part == 0:
                        answer(part, steps[i], False).start()

        some(0, True)
        loop(1, devices // batch, lambda turn_no: some(turn_no, False), devices // batch - 1)

    def send_rows(part):
        loop(1, devices, lambda step: answer(part, step, False).start())

    forward_weights(0)
    wait(ask_landed, asked.at[others])
    for step in range(1, experts):
        wait(gz_landed.at[step], gathered.at[0, 0])
        spread_weights(step)
    weights_c(chip).start()
    total = jnp.zeros((1, LANES), jnp.int32)
    for peer in range(devices):
        total = total + asked[peer, :, slots:]
    totals = jnp.maximum(total.astype(F32), 1.0)
    serve(0)
    serve(1)
    for step in range(1, experts):
        forward_weights(step)
    weights_c(beside_x).start()
    weights_c(beside_y).start()
    send_rows(1)
    for part in range(2, chunks):
        serve(part)
    for step in range(experts):
        wait(gd_landed.at[step], gathered.at[0, 0])
    weights_c(across_both).start()
    for part in range(2, chunks):
        send_rows(part)

    def column(index, begin=0, end=LANES):
        block = columns[index, begin:end, :]
        return jnp.concatenate([block] * (CHUNK // LANES), 1)

    def tokens_of(part):
        return slice(part * CHUNK, (part + 1) * CHUNK)

    def split(part, field):
        index = picks[field : field + 1, tokens_of(part)]
        owner = index >> shift
        return (owner & 1) * LANES + (index & (LANES - 1)), owner >> 1

    def fetch(part):
        wait(row_landed.at[part], got.at[part, others])
        for owner in range(devices):
            level, lower = owner // 2, owner % 2
            slot_cells[part % 2][
                level * EMB : (level + 1) * EMB, lower * LANES : (lower + 1) * LANES
            ] = got[part, owner]
        inputs[part % 2][FIELDS * EMB : INPUT, :] = dense_low[:, tokens_of(part)]

    def pick(part, field):
        key, high = split(part, field)
        flags = as_low(spread(key, KEYS, CHUNK))
        chosen[part % 3][field] = flags
        found = mm(slot_cells[part % 2][...], flags)
        result = found[:EMB]
        for level in range(1, levels):
            result = jnp.where(high == level, found[level * EMB : (level + 1) * EMB], result)
        inputs[part % 2][field * EMB : (field + 1) * EMB, :] = result.astype(BF)

    def give(part, field, first_time):
        places, flags = [], []
        for one in (field, field + 1):
            key, high = split(part, one)
            values = d_inputs[part % 2][one * EMB : (one + 1) * EMB, :]
            places.append(levels_of(values, high, levels))
            flags.append(chosen[part % 3][one])
        sums = mm(jnp.concatenate(places, 1), jnp.concatenate(flags, 1), NT)
        if first_time:
            slot_sum[part % 2][...] = sums
        else:
            slot_sum[part % 2][...] += sums

    def picks_of(part):
        return [functools.partial(pick, part, field) for field in range(FIELDS)]

    def gives_of(part):
        return [
            functools.partial(give, part, field, field == 0) for field in range(0, FIELDS, 2)
        ]

    def send_slots(part):
        for owner in range(devices):
            level, lower = owner // 2, owner % 2
            slots_out[part, owner] = slot_sum[part % 2][
                level * EMB : (level + 1) * EMB, lower * LANES : (lower + 1) * LANES
            ].astype(BF)
        loop(1, devices, lambda hop: give_slots(part, hop, False).start())
        slots_got[part, me] = slots_out[part, me]

    def train(part):
        here_tokens = tokens_of(part)
        first_time = part == 0
        whole_x = inputs[part % 2]

        def add(total, value):
            if first_time:
                total[...] = value
            else:
                total[...] += value

        x = whole_x[:INPUT, :]
        logits = mm(gate_t[...], x)[:gates_wide] + column(14, 0, gates_wide)
        probs, gates = [], []
        for task in range(TASKS):
            line = [logits[task * experts + e : task * experts + e + 1] for e in range(experts)]
            top = functools.reduce(jnp.maximum, line)
            powers = [jnp.exp(item - top) for item in line]
            whole = 1.0 / functools.reduce(jnp.add, powers)
            probs.append([item * whole for item in powers])
            gates.append([item.astype(BF).astype(F32) for item in probs[-1]])
        yield
        mixed = [None] * TASKS
        for expert in range(experts):
            pre = mm(first_t[expert], x) + jnp.concatenate(
                [column(2 * expert), column(2 * expert + 1)], 0
            )
            sig = sigmoid(pre)
            act = pre * sig
            slope_one[expert] = sig + act * (1.0 - sig)
            low = act.astype(BF)
            hidden[expert, :HID, :] = low
            yield
            pre = mm(second_t[expert], low) + column(8 + expert)
            sig = sigmoid(pre)
            act = pre * sig
            slope_two[expert] = sig + act * (1.0 - sig)
            outs[expert] = act
            for task in range(TASKS):
                term = gates[task][expert] * act
                mixed[task] = term if mixed[task] is None else mixed[task] + term
            yield
        d_mixed = []
        for task in range(TASKS):
            mix = mixed[task].astype(BF)
            mixes[task, :OUT, :] = mix
            low, high = task * TOWER, (task + 1) * TOWER
            pre = mm(tower_t[task], mix) + column(12, low, high)
            sig = sigmoid(pre)
            act = pre * sig
            head = column(13, low, high)
            logit = jnp.sum(act * head, 0, keepdims=True) + column(15, task, task + 1)
            scale = mask[task : task + 1, here_tokens].astype(F32) / totals[:, task : task + 1]
            target = labels[task : task + 1, here_tokens].astype(F32)
            soft = jnp.maximum(logit, 0.0) + jnp.log(1.0 + jnp.exp(-jnp.abs(logit)))
            loss_sum[...] += scale * (soft - target * logit)
            d_logit = scale * (sigmoid(logit) - target)
            yield
            d_pre = ((sig + act * (1.0 - sig)) * (d_logit * head)).astype(BF)
            d_upper = d_logit.astype(BF).astype(F32)
            d_both = jnp.concatenate(
                [
                    jnp.broadcast_to(d_upper, (8, CHUNK)),
                    jnp.broadcast_to(d_logit - d_upper, (8, CHUNK)),
                ],
                0,
            ).astype(BF)
            upper = act.astype(BF)
            rest = (act - upper.astype(F32)).astype(BF)
            ones = jnp.ones((16, CHUNK), BF)
            zeros = jnp.zeros((LANES - TOWER - 16, CHUNK), BF)
            both = mm(d_both, jnp.concatenate([upper, ones, zeros], 0), NT) + mm(
                d_both, jnp.concatenate([rest, zeros, jnp.zeros((16, CHUNK), BF)], 0), NT
            )
            add(sum_head.at[task], both[:8] + both[8:])
            add(sum_tower.at[task], mm(mixes[task], d_pre, NT))
            d_mixed.append(mm(tower_n[task], d_pre).astype(BF).astype(F32))
            yield
        d_gates = [[None] * experts for task in range(TASKS)]
        for expert in range(experts):
            d_out = gates[0][expert] * d_mixed[0] + gates[1][expert] * d_mixed[1]
            out = outs[expert]
            for task in range(TASKS):
                d_gates[task][expert] = jnp.sum(out * d_mixed[task], 0, keepdims=True)
            d_two = (slope_two[expert] * d_out).astype(BF)
            d_hidden = mm(second_n[expert], d_two)
            add(sum_second.at[expert], mm(hidden[expert], d_two, NT))
            yield
            d_one = (slope_one[expert] * d_hidden).astype(BF)
            deltas[expert * HID : (expert + 1) * HID, :] = d_one
            add(sum_first.at[expert], mm(whole_x[...], d_one, NT))
            yield
        lines = []
        for task in range(TASKS):
            inner = functools.reduce(
                jnp.add, [probs[task][e] * d_gates[task][e] for e in range(experts)]
            )
            lines += [probs[task][e] * (d_gates[task][e] - inner) for e in range(experts)]
        lines.append(jnp.zeros((16 - gates_wide, CHUNK), F32))
        d_gate = jnp.concatenate(lines, 0).astype(BF)
        deltas[experts * HID : experts * HID + 16, :] = d_gate
        add(sum_gate.at[:, : INPUT + ONES], mm(d_gate, whole_x[...], NT))
        yield
        d_x = mm(wide[...], deltas[...])
        d_inputs[part % 2][...] = d_x
        d_dense = d_x[INPUT - LANES :, :]
        upper = d_dense.astype(BF)
        rest = (d_dense - upper.astype(F32)).astype(BF)
        both = mm(feats_low[:, here_tokens], upper, NT)
        add(sum_dense, both[:16] + both[16:] + mm(feats_low[:16, here_tokens], rest, NT))
        yield

    stops = 2 + 2 * experts + 2 * TASKS + 2 * experts + 1

    def beside(main, jobs):
        jobs, done = list(jobs), 0
        for stop, _ in enumerate(main):
            until = len(jobs) * (stop + 1) // stops
            for job in jobs[done:until]:
                job()
            done = until
        for job in jobs[done:]:
            job()

    def mixed_jobs(*lists):
        spots = [
            ((index + 0.5) / len(jobs), job) for jobs in lists for index, job in enumerate(jobs)
        ]
        return [job for spot, job in sorted(spots, key=lambda pair: pair[0])]

    fetch(0)
    for job in picks_of(0):
        job()
    wait(gc_landed, gathered.at[pl.ds(0, chips)])
    for expert in range(experts):
        for part in range(size.groups):
            wide[
                part * size.first : (part + 1) * size.first, expert * HID : (expert + 1) * HID
            ] = gathered[part, expert, : size.first, :]
            base = part * size.second
            second_n[expert, base : base + half, :] = gathered[part, expert, size.first :, :LANES]
            second_n[expert, base + half : base + 2 * half, :] = gathered[
                part, expert, size.first :, LANES:
            ]
        first_t[expert] = wide[:, expert * HID : (expert + 1) * HID].T
        second_t[expert] = second_n[expert].T
    for part in range(chunks):
        jobs = []
        if part + 1 < chunks:
            fetch(part + 1)
            jobs.append(picks_of(part + 1))
        if part > 0:
            jobs.append(gives_of(part - 1))
        beside(train(part), mixed_jobs(*jobs))
        if 0 < part < chunks - 1:
            send_slots(part - 1)

    for turn_no in range(experts):
        expert = expert_at(turn_no)
        for part in range(size.groups):
            base = part * size.second
            grads[part, expert, : size.first, :] = sum_first[
                expert, part * size.first : (part + 1) * size.first, :
            ].astype(BF)
            grads[part, expert, size.first :, :LANES] = sum_second[
                expert, base : base + half, :
            ].astype(BF)
            grads[part, expert, size.first :, LANES:] = sum_second[
                expert, base + half : base + 2 * half, :
            ].astype(BF)
        for step in range(1, chips + 1):
            sums_c(turn_no, step % chips).start()
    for expert in range(experts):
        per = HID // LANES
        for piece in range(per):
            line = expert * per + piece
            small_part[line : line + 1, :] = sum_first[
                expert, INPUT : INPUT + 1, piece * LANES : (piece + 1) * LANES
            ]
        line = experts * per + expert
        small_part[line : line + 1, :] = sum_second[expert, HID : HID + 1, :]
    for line in range(DENSE + 1):
        values = jnp.where(lane < DOUT, turn(sum_dense[line : line + 1, :], DOUT - LANES), 0.0)
        put(small_part, at_dense + line * DOUT, values)
    fill = jnp.zeros((LANES - 16, LANES), F32)
    for block in range(INPUT // LANES):
        piece = jnp.concatenate([sum_gate[:, block * LANES : (block + 1) * LANES], fill], 0)
        gate_rows[block * LANES : (block + 1) * LANES, :] = piece.T
    gate_rows[INPUT:, :] = jnp.concatenate([sum_gate[:, INPUT:], fill], 0).T[:ONES]
    lines = INPUT // per_line + 1
    packed = jnp.zeros((lines, LANES), F32)
    for spot in range(per_line):
        packed = packed + turn(gate_rows[pl.ds(spot, lines, stride=per_line), :], spot * gates_wide)
    inside = lax.broadcasted_iota(jnp.int32, (lines, LANES), 0) < lines - 1
    put(
        small_part,
        at_gate,
        jnp.where(inside | (lanes_of(lines) < gates_wide), packed, 0.0),
    )
    tower_rows[...] = jnp.zeros_like(tower_rows)
    for task in range(TASKS):
        base = task * (OUT + 1)
        tower_rows[base : base + OUT + 1, :TOWER] = sum_tower[task, : OUT + 1, :]
    put(
        small_part,
        at_tower,
        tower_rows[pl.ds(0, count_rows, stride=2), :]
        + turn(tower_rows[pl.ds(1, count_rows, stride=2), :], TOWER),
    )
    for task in range(TASKS):
        put(
            small_part,
            at_head + task * (TOWER + 1),
            jnp.where(lane < TOWER + 1, sum_head[task, 0:1, :], 0.0),
        )
    whole_loss = jnp.sum(loss_sum[...], 1, keepdims=True)
    put(small_part, at_loss, jnp.where(lane == 0, whole_loss, 0.0))
    loop(1, devices, lambda step: give_small(step, False).start())
    for turn_no in range(experts):
        expert = expert_at(turn_no)
        wait(sc_landed.at[turn_no], core_got.at[expert])
        for step in range(1, chips + 1):
            other = turned(chip, chips, step % chips, False)
            core_sum[expert, other] = (
                grads[other * 2 + core, expert].astype(F32) + core_got[expert, other].astype(F32)
            ).astype(BF)
            if step < chips:
                sums_y(turn_no, step).start()
    send_slots(chunks - 2)
    for job in gives_of(chunks - 1):
        job()
    send_slots(chunks - 1)

    def collect(part):
        columns_here = pl.ds(part * LANES, LANES)
        wait(slot_landed.at[part], slots_got.at[part, others])

        def some(turn_no):
            steps = [turn_no * batch + i for i in range(batch)]
            peers = [lax.rem(me + devices - step, devices) for step in steps]
            index = jnp.concatenate([asked[peer, :, columns_here] for peer in peers], 1)
            values = jnp.concatenate([slots_got[part, peer] for peer in peers], 1).astype(F32)
            spots = as_low(spread(index & (KEYS - 1), KEYS, batch * LANES))
            table_grad[...] += mm(levels_of(values, index >> 8, blocks), spots, NT)

        loop(0, devices // batch, some, devices // batch)

    for part in range(chunks - 2):
        collect(part)
    for turn_no in range(experts):
        expert = expert_at(turn_no)
        wait(sy_landed.at[turn_no], chip_got.at[expert, other_chips])
        total = core_sum[expert, chip].astype(F32)
        for step in range(1, chips):
            total = total + chip_got[expert, step].astype(F32)
        if turn_no + 1 < experts:
            chip_sum[expert] = total.astype(BF)
            sums_z(turn_no).start()
        if turn_no == 0:
            wait(small_landed, small_got.at[others])
            small_got[me] = small_part[own_lines(me), :]
            small_sum[own_lines(me), :] = jnp.sum(small_got[...], 0)
            loop(1, devices, lambda step: give_whole(step, False).start())
    collect(chunks - 2)
    collect(chunks - 1)
    wait(sz_landed, z_got.at[other_experts])
    for turn_no in range(experts - 1):
        total = total + z_got[turn_no].astype(F32)
    first_grad[...] = total[: size.first]
    second_grad[:half, :] = total[size.first :, :LANES]
    second_grad[half:, :] = total[size.first :, LANES:]

    other_lines = pl.ds(0, (devices - 1) * small_got.shape[1])
    wait(whole_landed, small_sum.at[other_lines, :])
    wait(whole_sent, small_sum.at[other_lines, :])
    wait(small_sent, small_part.at[other_lines, :])
    wait(ask_sent, message.at[others])
    wait(row_sent, rows.at[:, others])
    wait(slot_sent, slots_out.at[:, others])
    wait(gz_sent, gathered.at[0, other_experts])
    wait(gy_sent, gathered.at[other_chips])
    wait(gc_sent, gathered.at[pl.ds(0, chips)])
    wait(sc_sent, core_got)
    wait(sy_sent, core_sum.at[:, other_chips])
    wait(sz_sent, chip_sum.at[other_experts])


def update(size, *refs):
    grads, state, flat, results, loss = refs[:3], refs[3:12], refs[12], refs[13:22], refs[22]
    spot = offsets(size.experts)[-1]
    loss[...] = flat[spot // LANES : spot // LANES + 1, spot % LANES : spot % LANES + 1]
    table_grad = grads[0][...]
    wide = jnp.concatenate(
        [table_grad[b * EMB : (b + 1) * EMB] for b in range(size.rows // KEYS)], 1
    )
    for index, grad in enumerate((wide, grads[1][...], grads[2][...])):
        rate = 0.3 if index == 0 else 0.15
        values = [ref[...] for ref in state[3 * index : 3 * index + 3]]
        for ref, value in zip(results[3 * index : 3 * index + 3], adamw(*values, grad, rate)):
            ref[...] = value


def shape(dims, dtype=F32):
    return jax.ShapeDtypeStruct(dims, dtype)


def call(kernel, outs, scratch, remote=None):
    vmem = pl.BlockSpec(memory_space=pltpu.VMEM)
    params = dict(vmem_limit_bytes=56 * 2**20)
    if remote is not None:
        params.update(collective_id=remote, has_side_effects=True)
    return lambda *args: pl.pallas_call(
        kernel,
        out_shape=outs,
        in_specs=[vmem] * len(args),
        out_specs=[vmem] * len(outs),
        scratch_shapes=scratch,
        compiler_params=pltpu.CompilerParams(**params),
    )(*args)


def local(
    size,
    dense_feats,
    picks,
    labels,
    label_mask,
    requests,
    table,
    table_m,
    table_v,
    first_w,
    first_m,
    first_v,
    second_w,
    second_m,
    second_v,
    small,
    small_m,
    small_v,
):
    devices, experts, groups = size.devices, size.experts, size.groups
    chips = groups // 2
    chunks = size.tokens // CHUNK
    dma = pltpu.SemaphoreType.DMA
    vm = pltpu.VMEM
    message = size.slots + LANES
    count = small.shape[0]
    lines = -(-(count + 1) // (devices * 8 * LANES)) * 8
    flat_lines = -(-count // LANES)
    exchange = vm((chunks, devices, EMB, LANES), BF)
    weights = vm((groups, experts, size.pack, HID), BF)
    of_chips = vm((experts, chips, size.pack, HID), BF)
    of_chip = vm((experts, size.pack, HID), BF)
    table_grad, first_grad, second_grad, flat = call(
        functools.partial(step_kernel, size),
        [
            shape((size.rows // KEYS * EMB, KEYS)),
            shape((size.first, HID)),
            shape((size.second, OUT)),
            shape((devices * lines, LANES)),
        ],
        [
            vm((devices, 1, message), jnp.int32),
            vm((devices, 1, message), jnp.int32),
            vm((size.rows // KEYS * EMB, KEYS), BF),
        ]
        + [exchange] * 4
        + [weights, weights, of_chips, of_chips, of_chips, of_chip, of_chip]
        + [
            vm((LANES, LANES), F32),
            vm((16, LANES, LANES), F32),
            vm((INPUT + ONES, LANES), F32),
            vm((16, INPUT), BF),
            vm((TASKS * (OUT + 1) + 6, LANES), F32),
            vm((TASKS, OUT, TOWER), BF),
            vm((TASKS, TOWER, OUT), BF),
            vm((LANES, LANES), F32),
            vm((DOUT, 16), F32),
            vm((DOUT, size.tokens), BF),
            vm((devices * lines, LANES), F32),
            vm((devices, lines, LANES), F32),
            vm((experts, HID, INPUT), BF),
            vm((experts, HID, OUT), BF),
            vm((experts, OUT, HID), BF),
            vm((INPUT, experts * HID + LANES), BF),
            vm((16, size.tokens), F32),
            vm((32, size.tokens), BF),
            vm((devices // 2 * EMB, KEYS), BF),
            vm((devices // 2 * EMB, KEYS), BF),
            vm((FIELDS, KEYS, CHUNK), BF),
            vm((FIELDS, KEYS, CHUNK), BF),
            vm((FIELDS, KEYS, CHUNK), BF),
            vm((INPUT + ONES, CHUNK), BF),
            vm((INPUT + ONES, CHUNK), BF),
            vm((experts, HID, CHUNK), F32),
            vm((experts, OUT, CHUNK), F32),
            vm((experts, HID + ONES, CHUNK), BF),
            vm((experts, OUT, CHUNK), F32),
            vm((TASKS, OUT + ONES, CHUNK), BF),
            vm((experts * HID + LANES, CHUNK), BF),
            vm((INPUT, CHUNK), F32),
            vm((INPUT, CHUNK), F32),
            vm((devices // 2 * EMB, KEYS), F32),
            vm((devices // 2 * EMB, KEYS), F32),
            vm((experts, INPUT + ONES, HID), F32),
            vm((experts, HID + ONES, OUT), F32),
            vm((16, INPUT + LANES), F32),
            vm((16, LANES), F32),
            vm((TASKS, OUT + ONES, TOWER), F32),
            vm((TASKS, 8, LANES), F32),
            vm((1, CHUNK), F32),
        ]
        + [dma, dma, dma, dma((chunks,)), dma, dma((chunks,))]
        + [dma] * 5
        + [dma((experts,)), dma, dma((experts,)), dma((experts,)), dma((experts,))]
        + [dma] * 5
        + [dma((experts,)), dma, dma((experts,))],
        0,
    )(
        requests[0],
        picks.T,
        dense_feats.T,
        labels.T,
        label_mask.T,
        table.T,
        first_w[0],
        second_w[0],
        jnp.pad(small, (0, flat_lines * LANES - count)).reshape(flat_lines, LANES),
    )
    tables = (table.T, table_m.T, table_v.T)
    firsts = (first_w[0], first_m[0], first_v[0])
    seconds = (second_w[0], second_m[0], second_v[0])
    new = call(
        functools.partial(update, size),
        [shape(a.shape) for a in tables + firsts + seconds] + [shape((1, 1))],
        [],
    )(table_grad, first_grad, second_grad, *tables, *firsts, *seconds, flat)
    flat = flat.reshape(-1)
    new_small = adamw(small, small_m, small_v, flat[:count], 0.15)
    return (
        (new[9].reshape(()),)
        + tuple(a.T for a in new[:3])
        + tuple(a[None] for a in new[3:9])
        + tuple(new_small)
    )


def solution(mesh):
    both = P(("batch", "expert"), None)
    shard = P("expert", "batch", None)
    ins = (both,) * 4 + (P(("batch", "expert"), None, None, None),) + (both,) * 3
    ins = ins + (shard,) * 6 + (P(),) * 3

    def step(*args):
        devices = mesh.shape["batch"] * mesh.shape["expert"]
        size = sizes_of(
            mesh, args[0].shape[0] // devices, args[4].shape[-1], args[5].shape[0] // devices
        )
        return jax.shard_map(
            functools.partial(local, size) if fits(size) else plain,
            mesh=mesh,
            in_specs=ins,
            out_specs=(P(),) + (both,) * 3 + (shard,) * 6 + (P(),) * 3,
            check_vma=False,
        )(*args)

    return step
```
